32 devices in a mesh: seq: 8 (over z, x), tp: 4 (over y, core).
Axes of the slice: x: 2, y: 2, z: 4, core: 2. Of those that a mesh axis runs over, the one named last changes fastest.
Arguments:
- hidden_in: bfloat16 [256, 2048], P('seq'), may hold values from -6 to 6
- query_weight: bfloat16 [2048, 2048], P(None, 'tp'), may hold values from -0.125 to 0.125
- key_weight: bfloat16 [2048, 2048], P(None, 'tp'), may hold values from -0.125 to 0.125
- value_weight: bfloat16 [2048, 2048], P(None, 'tp'), may hold values from -0.125 to 0.125
- out_weight: bfloat16 [2048, 2048], P('tp'), may hold values from -0.125 to 0.125
- query_gain: float32 [2048], P('tp'), may hold values from 0.5 to 1.5
- key_gain: float32 [2048], P('tp'), may hold values from 0.5 to 1.5
- post_gain: float32 [2048], P('tp'), may hold values from 0.5 to 1.5
- key_cache: bfloat16 [4, 1024, 2048], P(None, 'seq', 'tp'), may hold values from -110 to 110
- value_cache: bfloat16 [4, 1024, 2048], P(None, 'seq', 'tp'), may hold values from -6 to 6
- cache_lengths: int32 [4], replicated, may hold values from 128 to 960
- parents: int32 [4, 64], replicated, may hold values from -1 to 62, as said below
- accepted_leaf: int32 [4], replicated, may hold values from 0 to 63
Outputs:
- hidden_out: bfloat16 [256, 2048], P('seq', 'tp')
- new_key_cache: bfloat16 [4, 1024, 2048], P(None, 'seq', 'tp')
- new_value_cache: bfloat16 [4, 1024, 2048], P(None, 'seq', 'tp')
The draws below stay inside these ranges and needn't reach their ends.
Inputs may be any that keep to these rules, and one draw needn't show every extreme that they name: parents[r, 0] = -1; for i >= 1, parents[r, i] lies in max(0, i - 3) to i - 1; parents[r, 63] = 62.
All inputs are finite; a program needn't handle non-finite values.
Results may differ from the reference program's by a relative error of at most 0.019.
Values may be sent and summed in bfloat16 or wider, within the bound.
No kernel may reach another device: no remote copies, remote signals or barrier semaphores. Data moves between devices by JAX's collectives and lax.ppermute only.
A program may use at most 128 MiB of HBM per device.

```python
import math
import jax
import jax.numpy as jnp
from jax import lax

D = 2048
HEADS = 16
HEAD_DIM = 128
REQ = 4
DRAFT = 64
QDIM = 2048
TOKENS = 256
CACHE_TOTAL = 1024


def draw_key_cache(key, part):
    normal_part = jnp.clip(jax.random.normal(jax.random.fold_in(key, 3), (REQ, CACHE_TOTAL, QDIM), jnp.float32), -5.0, 5.0)
    return normal_part.astype(jnp.bfloat16)


def draw_cache_lengths(key, part):
    lowest = CACHE_TOTAL // 8
    highest = CACHE_TOTAL - DRAFT
    lengths_drawn = jax.random.randint(jax.random.fold_in(key, 1), (REQ,), lowest, highest + 1)
    chosen = jax.random.randint(jax.random.fold_in(key, 2), (), 0, REQ)
    return jnp.where(jnp.arange(REQ) == chosen, highest, lengths_drawn).astype(jnp.int32)


def draw_parents(key, part):
    indices = jnp.arange(DRAFT, dtype=jnp.int32)[None, :]
    backward = jax.random.randint(jax.random.fold_in(key, 6), (REQ, DRAFT), 0, 3)
    parent_ids = indices - 1 - jnp.minimum(backward, jnp.maximum(indices - 1, 0))
    parent_ids = jnp.where(indices == DRAFT - 1, DRAFT - 2, parent_ids)
    return parent_ids.astype(jnp.int32)


def place_ends(result, own_key, low, high):
    longest = result.shape.index(max(result.shape))
    spots = []
    for shift in (0, 1):
        where = [jax.random.randint(jax.random.fold_in(own_key, axis), (), 0, length) for axis, length in enumerate(result.shape)]
        where[longest] = (where[longest] + shift) % result.shape[longest]
        spots.append(tuple(where))
    return result.at[spots[0]].set(low).at[spots[1]].set(high)


def level_of(rng, extent, shards, least, largest):
    factor_of, own = 1.0, jax.random.fold_in(rng, 6)
    for axis_at, shards_of in shards:
        steps = jnp.exp(jax.random.uniform(jax.random.fold_in(own, axis_at), (shards_of,), jnp.float32, least / len(shards), largest / len(shards)))
        factor_of = factor_of * jnp.repeat(steps, extent[axis_at] // shards_of).reshape([-1 if axis == axis_at else 1 for axis in range(len(extent))])
    return factor_of


def bell_draw(rng, shape, width, most, split=(), kind=jnp.bfloat16):
    factor_of = level_of(rng, shape, split, -0.22, 0.18) if split else 1.0
    values = jax.random.normal(rng, shape, jnp.float32) * width * factor_of
    return jnp.minimum(jnp.maximum(values, -most), most).astype(kind)


def setup_inputs(seed: int = 0) -> dict:
    arg_keys = jax.random.split(jax.random.key(seed), 14)
    hidden_in = bell_draw(arg_keys[0], (TOKENS, D), 1.0, 6.0, ((0, 8),))
    query_weight = bell_draw(arg_keys[1], (D, QDIM), D ** -0.5, 0.125, ((1, 4),))
    key_weight = bell_draw(arg_keys[2], (D, QDIM), D ** -0.5, 0.125, ((1, 4),))
    value_weight = bell_draw(arg_keys[3], (D, QDIM), D ** -0.5, 0.125, ((1, 4),))
    out_weight = bell_draw(arg_keys[4], (QDIM, D), QDIM ** -0.5, 0.125, ((0, 4),))
    query_gain = jnp.clip(0.5 + 1.0 * jax.random.uniform(arg_keys[5], (QDIM,), jnp.float32) ** level_of(arg_keys[5], (QDIM,), ((0, 4),), -0.2, 0.2), 0.5, 1.5)
    key_gain = jnp.clip(0.5 + 1.0 * jax.random.uniform(arg_keys[6], (QDIM,), jnp.float32) ** level_of(arg_keys[6], (QDIM,), ((0, 4),), -0.2, 0.2), 0.5, 1.5)
    post_gain = jnp.clip(0.5 + 1.0 * jax.random.uniform(arg_keys[7], (D,), jnp.float32) ** level_of(arg_keys[7], (D,), ((0, 4),), -0.2, 0.2), 0.5, 1.5)
    key_cache = draw_key_cache(jax.random.fold_in(arg_keys[13], 71), 0)
    value_cache = bell_draw(arg_keys[9], (REQ, CACHE_TOTAL, QDIM), 1.0, 6.0, ((1, 8), (2, 4)))
    cache_lengths = draw_cache_lengths(jax.random.fold_in(arg_keys[13], 71), 0)
    parents = draw_parents(jax.random.fold_in(arg_keys[13], 71), 0)
    accepted_leaf = place_ends(jax.random.randint(arg_keys[12], (REQ,), 0, DRAFT), jax.random.fold_in(arg_keys[12], 1), 0, DRAFT - 1).astype(jnp.int32)
    return {"hidden_in": hidden_in, "query_weight": query_weight, "key_weight": key_weight, "value_weight": value_weight, "out_weight": out_weight, "query_gain": query_gain, "key_gain": key_gain, "post_gain": post_gain, "key_cache": key_cache, "value_cache": value_cache, "cache_lengths": cache_lengths, "parents": parents, "accepted_leaf": accepted_leaf}


EPS = 1e-06
THETA = 500000.0
NEG = -1e+30

def ancestry(parents):
    number = parents.shape[-1]
    columns = jnp.arange(number, dtype=jnp.int32)
    single = (parents[:, :, None] == columns[None, None, :]).astype(jnp.float32)
    ancestors = jnp.eye(number, dtype=jnp.float32)[None] + single
    for repeat in range(max(1, (number - 1).bit_length())):
        ancestors = jnp.minimum(jnp.einsum('rij,rjk->rik', ancestors, ancestors, precision=lax.Precision.HIGHEST), 1.0)
    tree_depth = lax.optimization_barrier(jnp.sum(ancestors, axis=-1)) - 1.0
    return (ancestors, tree_depth)

def rotary(values, positions):
    half_dim = values.shape[-1] // 2
    freqs = THETA ** (-2.0 * jnp.arange(half_dim, dtype=jnp.float32) / values.shape[-1])
    angles = positions[:, None, None] * freqs[None, None, :]
    cosine = jnp.cos(angles)
    sine = jnp.sin(angles)
    first = values[..., :half_dim]
    second = values[..., half_dim:]
    return jnp.concatenate([first * cosine - second * sine, second * cosine + first * sine], axis=-1)

def prepare(raw, square_sum, gain, positions, width_all):
    scaled = raw * lax.rsqrt(square_sum / width_all + EPS)[:, None] * gain[None, :]
    rows_here = raw.shape[0]
    heads_here = raw.shape[1] // HEAD_DIM
    turned = rotary(scaled.reshape(rows_here, heads_here, HEAD_DIM), positions)
    return turned.reshape(rows_here, heads_here * HEAD_DIM).astype(jnp.bfloat16)

def reference(hidden_in, query_weight, key_weight, value_weight, out_weight, query_gain, key_gain, post_gain, key_cache, value_cache, cache_lengths, parents, accepted_leaf):
    ancestors, tree_depth = ancestry(parents)
    positions = (cache_lengths[:, None].astype(jnp.float32) + tree_depth).reshape(TOKENS)
    query_raw = jnp.dot(hidden_in, query_weight, preferred_element_type=jnp.float32)
    key_raw = jnp.dot(hidden_in, key_weight, preferred_element_type=jnp.float32)
    value_raw = jnp.dot(hidden_in, value_weight, preferred_element_type=jnp.float32)
    queries = prepare(query_raw, lax.optimization_barrier(jnp.sum(query_raw * query_raw, axis=1)), query_gain, positions, QDIM)
    keys = prepare(key_raw, lax.optimization_barrier(jnp.sum(key_raw * key_raw, axis=1)), key_gain, positions, QDIM)
    values = value_raw.astype(jnp.bfloat16)
    factor = 1.0 / math.sqrt(HEAD_DIM)
    places = jnp.arange(CACHE_TOTAL, dtype=jnp.int32)
    query_blocks = queries.reshape(REQ, DRAFT, HEADS, HEAD_DIM)
    key_blocks = keys.reshape(REQ, DRAFT, HEADS, HEAD_DIM)
    value_blocks = values.reshape(REQ, DRAFT, HEADS, HEAD_DIM)
    cache_keys = key_cache.reshape(REQ, CACHE_TOTAL, HEADS, HEAD_DIM)
    cache_values = value_cache.reshape(REQ, CACHE_TOTAL, HEADS, HEAD_DIM)

    def attend(item):
        query_block, key_block, value_block, stored_keys, stored_values, length, tree = item
        query_float = query_block.astype(jnp.float32)
        cache_scores = jnp.einsum('ihd,lhd->ihl', query_float, stored_keys.astype(jnp.float32), precision=lax.Precision.HIGHEST) * factor
        visible = (places < length)[None, None, :]
        cache_scores = jnp.where(visible, cache_scores, NEG)
        draft_scores = jnp.einsum('ihd,jhd->ihj', query_float, key_block.astype(jnp.float32), precision=lax.Precision.HIGHEST) * factor
        tree_mask = (tree > 0.5)[:, None, :]
        draft_scores = jnp.where(tree_mask, draft_scores, NEG)
        highest = jnp.maximum(lax.optimization_barrier(jnp.max(cache_scores, axis=-1)), lax.optimization_barrier(jnp.max(draft_scores, axis=-1)))
        cache_weights = jnp.where(visible, jnp.exp(cache_scores - highest[..., None]), 0.0)
        draft_weights = jnp.where(tree_mask, jnp.exp(draft_scores - highest[..., None]), 0.0)
        denominator = lax.optimization_barrier(jnp.sum(cache_weights, axis=-1)) + lax.optimization_barrier(jnp.sum(draft_weights, axis=-1))
        summed = jnp.einsum('ihl,lhd->ihd', cache_weights, stored_values.astype(jnp.float32), precision=lax.Precision.HIGHEST)
        summed = summed + jnp.einsum('ihj,jhd->ihd', draft_weights, value_block.astype(jnp.float32), precision=lax.Precision.HIGHEST)
        return (summed / denominator[..., None]).reshape(DRAFT, QDIM).astype(jnp.bfloat16)
    attention = lax.map(attend, (query_blocks, key_blocks, value_blocks, cache_keys, cache_values, cache_lengths, ancestors)).reshape(TOKENS, QDIM)
    projected = jnp.dot(attention, out_weight, preferred_element_type=jnp.float32)
    power = lax.optimization_barrier(jnp.sum(projected * projected, axis=1)) / D
    normed = projected * lax.rsqrt(power + EPS)[:, None] * post_gain[None, :]
    hidden_out = (hidden_in.astype(jnp.float32) + normed).astype(jnp.bfloat16)

    def compact(item):
        stored_keys, stored_values, key_block, value_block, length, tree, leaf, levels = item
        on_path = tree[leaf]
        target = length + levels.astype(jnp.int32)
        placing = (places[:, None] == target[None, :]) & (on_path[None, :] > 0.5)
        written = jnp.any(placing, axis=-1)[:, None]
        placing_half = placing.astype(jnp.bfloat16)
        fresh_keys = jnp.dot(placing_half, key_block, preferred_element_type=jnp.float32).astype(jnp.bfloat16)
        fresh_values = jnp.dot(placing_half, value_block, preferred_element_type=jnp.float32).astype(jnp.bfloat16)
        return (jnp.where(written, fresh_keys, stored_keys), jnp.where(written, fresh_values, stored_values))
    new_key_cache, new_value_cache = lax.map(compact, (key_cache, value_cache, keys.reshape(REQ, DRAFT, QDIM), values.reshape(REQ, DRAFT, QDIM), cache_lengths, ancestors, accepted_leaf, tree_depth))
    return (hidden_out, new_key_cache, new_value_cache)
```

```python
import functools
import math

import jax
import jax.numpy as jnp
from jax import lax
from jax.experimental import pallas as pl
from jax.experimental.pallas import tpu as pltpu
from jax.sharding import PartitionSpec as P

HEAD_DIM = 128
LANES = 128
EPS = 1e-06
THETA = 500000.0
NEG = -1e30
F32 = jnp.float32
BF16 = jnp.bfloat16
VMEM = pl.BlockSpec(memory_space=pltpu.VMEM)
SMEM = pl.BlockSpec(memory_space=pltpu.SMEM)
ANY = pl.BlockSpec(memory_space=pl.ANY)


def params(mib):
    return pltpu.CompilerParams(vmem_limit_bytes=mib * 1024 * 1024)


def dot(a, b):
    return jnp.dot(a, b, preferred_element_type=F32)


def dot_t(a, b):
    return lax.dot_general(a, b, (((1,), (1,)), ((), ())), preferred_element_type=F32)


def iota(shape, axis):
    return lax.broadcasted_iota(jnp.int32, shape, axis)


def stacked(parts):
    if len(parts) == 1:
        return parts[0]
    if parts[0].shape[0] % 16 == 0:
        return jnp.concatenate(parts, axis=0)
    return jnp.concatenate([part.astype(F32) for part in parts], axis=0).astype(BF16)


def sum_squares(raw):
    return jnp.sum(raw * raw, axis=1, keepdims=True)


def project_qk(hidden, wq, wk, query_raw, key_raw, squares, wq_v, wk_v, sems):
    chunks, depth = wq_v.shape[0], wq_v.shape[1]
    copies = []
    for c in range(chunks):
        for at, (source, target) in enumerate(((wq, wq_v), (wk, wk_v))):
            copy = pltpu.make_async_copy(
                source.at[pl.ds(c * depth, depth)], target.at[c], sems.at[2 * c + at]
            )
            copy.start()
            copies.append(copy)
    q_sum, k_sum = None, None
    for c in range(chunks):
        part = hidden[:, c * depth : (c + 1) * depth]
        copies[2 * c].wait()
        q = dot(part, wq_v[c])
        copies[2 * c + 1].wait()
        k = dot(part, wk_v[c])
        q_sum = q if c == 0 else q_sum + q
        k_sum = k if c == 0 else k_sum + k
    query_raw[...] = q_sum
    key_raw[...] = k_sum
    lane = iota(squares.shape[1:], 1)
    both = jnp.where(lane == 0, sum_squares(q_sum), sum_squares(k_sum))
    for t in range(squares.shape[0]):
        squares[t] = both


def project_v_and_tree(
    lengths, leaves, hidden, parents, freqs, wv, value, own_tree, targets, cosine, sine, wv_v, anc_v, sems
):
    chunks, depth = wv_v.shape[0], wv_v.shape[1]
    copies = []
    for c in range(chunks):
        copy = pltpu.make_async_copy(wv.at[pl.ds(c * depth, depth)], wv_v.at[c], sems.at[c])
        copy.start()
        copies.append(copy)
    requests, draft = parents.shape
    own = hidden.shape[0]
    first = lax.axis_index("seq") * own
    row, col = iota((draft, draft), 0), iota((draft, draft), 1)
    eye = (row == col).astype(BF16)
    trees = [
        jnp.where((parents[pl.ds(r, 1), :] == row) | (row == col), 1.0, 0.0).astype(BF16)
        for r in range(requests)
    ]
    for _ in range(max(1, (draft - 1).bit_length())):
        trees = [jnp.minimum(dot(tree, tree), 1.0).astype(BF16) for tree in trees]
    for r in range(requests):
        upright = lax.dot_general(
            trees[r], eye, (((0,), (0,)), ((), ())), preferred_element_type=F32
        )
        anc_v[pl.ds(r * draft, draft), :] = upright
        level = jnp.sum(trees[r].astype(F32), axis=0, keepdims=True) - 1.0
        on_path = jnp.sum(jnp.where(row == leaves[r], upright, 0.0), axis=0, keepdims=True)
        place = lengths[r] + level.astype(jnp.int32)
        targets[r] = jnp.where(on_path > 0.5, place, -1)
    mine = anc_v[pl.ds(pl.multiple_of(first, own), own), :]
    own_tree[...] = mine
    level = jnp.sum(mine, axis=1, keepdims=True) - 1.0
    position = lengths[first // draft].astype(F32) + level
    angles = position * freqs[...]
    cosine[...] = jnp.cos(angles)
    half = jnp.sin(angles)
    sine[...] = jnp.where(iota(half.shape, 1) < HEAD_DIM // 2, -half, half)
    total = None
    for c in range(chunks):
        copies[c].wait()
        v = dot(hidden[:, c * depth : (c + 1) * depth], wv_v[c])
        total = v if c == 0 else total + v
    value[...] = total.astype(BF16)


def prepare(
    width_all, query_raw, key_raw, value, q_gain, k_gain, cosine, sine, squares, queries, keys_values
):
    width = query_raw.shape[1]
    total = sum(squares[k] for k in range(squares.shape[0]))
    cos, sin = cosine[...], sine[...]
    for at, (raw, gain, out) in enumerate(
        ((query_raw, q_gain, queries), (key_raw, k_gain, keys_values))
    ):
        scale = lax.rsqrt(total[:, at : at + 1] / width_all + EPS)
        for h in range(width // HEAD_DIM):
            lanes = slice(h * HEAD_DIM, (h + 1) * HEAD_DIM)
            x = raw[:, lanes] * scale * gain[:, lanes]
            turned = x * cos + pltpu.roll(x, HEAD_DIM // 2, 1) * sin
            turned = turned.astype(BF16)
            for s in range(out.shape[0]):
                out[s, :, lanes] = turned
    for s in range(keys_values.shape[0]):
        keys_values[s, :, width:] = value[...]


def attend_cache(group, lengths, key_cache, value_cache, queries, partials):
    requests, block, width = key_cache.shape
    own = queries.shape[1]
    heads = width // HEAD_DIM
    me = lax.axis_index("seq")
    factor = 1.0 / math.sqrt(HEAD_DIM)
    rows = group * own
    place = me * block + iota((rows, block), 1)
    lane = iota((rows, LANES), 1)
    for request in range(requests):
        q = stacked([queries[request * group + j] for j in range(group)])
        visible = place < lengths[request]
        stats = jnp.zeros((rows, LANES), F32)
        for h in range(heads):
            lanes = slice(h * HEAD_DIM, (h + 1) * HEAD_DIM)
            scores = dot_t(q[:, lanes], key_cache[request, :, lanes]) * factor
            scores = jnp.where(visible, scores, NEG)
            peak = jnp.max(scores, axis=1, keepdims=True).astype(BF16).astype(F32)
            weights = jnp.exp(jnp.where(visible, scores - peak, NEG))
            total = jnp.sum(weights, axis=1, keepdims=True)
            high = total.astype(BF16).astype(F32)
            out = dot(weights.astype(BF16), value_cache[request, :, lanes]).astype(BF16)
            for j in range(group):
                partials[request * group + j, :, lanes] = out[j * own : (j + 1) * own]
            stats = jnp.where(lane == h, peak, stats)
            stats = jnp.where(lane == heads + h, high, stats)
            stats = jnp.where(lane == 2 * heads + h, total - high, stats)
        stats = stats.astype(BF16)
        for j in range(group):
            partials[request * group + j, :, width:] = stats[j * own : (j + 1) * own]


def attend_draft(group, own_tree, queries, keys_values, out, stats):
    own, width = queries.shape[1:]
    heads = width // HEAD_DIM
    me = lax.axis_index("seq")
    first = me // group * group
    q = queries[me]
    pair = stacked([keys_values[first + j] for j in range(group)])
    factor = 1.0 / math.sqrt(HEAD_DIM)
    allowed = own_tree[...] > 0.5
    lane = iota((own, LANES), 1)
    kept = jnp.zeros((own, LANES), F32)
    for h in range(heads):
        lanes = slice(h * HEAD_DIM, (h + 1) * HEAD_DIM)
        there = slice(width + h * HEAD_DIM, width + (h + 1) * HEAD_DIM)
        scores = dot_t(q[:, lanes], pair[:, lanes]) * factor
        scores = jnp.where(allowed, scores, NEG)
        peak = jnp.max(scores, axis=1, keepdims=True)
        weights = jnp.exp(jnp.where(allowed, scores - peak, NEG))
        out[:, lanes] = dot(weights.astype(BF16), pair[:, there])
        kept = jnp.where(lane == h, peak, kept)
        kept = jnp.where(lane == heads + h, jnp.sum(weights, axis=1, keepdims=True), kept)
    stats[...] = kept


def merge_and_project(draft_out, draft_stats, wo, partials, projected, wo_v, sems):
    count, width, columns = wo_v.shape
    heads = width // HEAD_DIM
    copies = []
    for k in range(count):
        copy = pltpu.make_async_copy(
            wo.at[:, pl.ds(k * columns, columns)], wo_v.at[k], sems.at[k]
        )
        copy.start()
        copies.append(copy)
    parts = range(partials.shape[0])
    stats = [partials[s, :, width:].astype(F32) for s in parts]
    own_stats = draft_stats[...]
    attention = []
    for h in range(heads):
        lanes = slice(h * HEAD_DIM, (h + 1) * HEAD_DIM)
        peaks = [s[:, h : h + 1] for s in stats] + [own_stats[:, h : h + 1]]
        highest = functools.reduce(jnp.maximum, peaks)
        scales = [jnp.exp(peak - highest) for peak in peaks]
        total = own_stats[:, heads + h : heads + h + 1] * scales[-1]
        summed = draft_out[:, lanes] * scales[-1]
        for at in parts:
            s = stats[at]
            own_total = s[:, heads + h : heads + h + 1] + s[:, 2 * heads + h : 2 * heads + h + 1]
            total = total + own_total * scales[at]
            summed = summed + partials[at, :, lanes].astype(F32) * scales[at]
        attention.append((summed / total).astype(BF16))
    attention = jnp.concatenate(attention, axis=1)
    for k in range(count):
        copies[k].wait()
        projected[k] = dot(attention, wo_v[k]).astype(projected.dtype)


def add_up(parts, summed, power):
    total = sum(parts[k].astype(F32) for k in range(parts.shape[0]))
    summed[...] = total
    own_power = jnp.broadcast_to(sum_squares(total), power.shape[1:])
    for k in range(power.shape[0]):
        power[k] = own_power


def finish(model_width, summed, gain, hidden, powers, out):
    columns = summed.shape[1]
    power = sum(powers[k] for k in range(powers.shape[0]))[:, :1]
    start = pl.multiple_of(lax.axis_index("tp") * columns, columns)
    normed = summed[...] * lax.rsqrt(power / model_width + EPS) * gain[...]
    out[...] = (hidden[:, pl.ds(start, columns)].astype(F32) + normed).astype(BF16)


def compact(group, targets, key_cache, value_cache, keys_values, new_keys, new_values):
    requests, block, width = key_cache.shape
    own = keys_values.shape[1]
    me = lax.axis_index("seq")
    place = me * block + iota((block, group * own), 0)
    for request in range(requests):
        kv = stacked([keys_values[request * group + j] for j in range(group)])
        placing = place == targets[request]
        written = jnp.max(placing.astype(F32), axis=1, keepdims=True) > 0.5
        fresh = dot(placing.astype(BF16), kv)
        new_keys[request] = jnp.where(
            written, fresh[:, :width], key_cache[request].astype(F32)
        ).astype(BF16)
        new_values[request] = jnp.where(
            written, fresh[:, width:], value_cache[request].astype(F32)
        ).astype(BF16)


def shaped(shape, dtype):
    return jax.ShapeDtypeStruct(shape, dtype)


def body_general(
    hidden_in,
    query_weight,
    key_weight,
    value_weight,
    out_weight,
    query_gain,
    key_gain,
    post_gain,
    key_cache,
    value_cache,
    cache_lengths,
    parents,
    accepted_leaf,
):
    requests, block, width = key_cache.shape
    draft = parents.shape[1]
    own, model = hidden_in.shape
    tp = lax.axis_size("tp")
    seq = lax.axis_size("seq")
    group = draft // own
    columns = model // tp
    chunks = 4
    depth = model // chunks

    def exchange(x, axis):
        return lax.all_to_all(x, axis, 0, 0, tiled=True)

    query_raw, key_raw, squares = pl.pallas_call(
        project_qk,
        out_shape=(
            shaped((own, width), F32),
            shaped((own, width), F32),
            shaped((tp, own, LANES), F32),
        ),
        in_specs=[VMEM, ANY, ANY],
        out_specs=(VMEM, VMEM, VMEM),
        scratch_shapes=[
            pltpu.VMEM((chunks, depth, width), BF16),
            pltpu.VMEM((chunks, depth, width), BF16),
            pltpu.SemaphoreType.DMA((2 * chunks,)),
        ],
        compiler_params=params(56),
        cost_estimate=pl.CostEstimate(
            flops=4 * own * model * width, bytes_accessed=4 * model * width, transcendentals=0
        ),
        name="project_qk",
    )(hidden_in, query_weight, key_weight)
    squares = exchange(squares, "tp")

    exponents = -2.0 * (jnp.arange(HEAD_DIM) % (HEAD_DIM // 2)).astype(F32) / HEAD_DIM
    freqs = (THETA**exponents)[None, :]
    value, own_tree, targets, cosine, sine = pl.pallas_call(
        project_v_and_tree,
        out_shape=(
            shaped((own, width), BF16),
            shaped((own, draft), F32),
            shaped((requests, 1, draft), jnp.int32),
            shaped((own, HEAD_DIM), F32),
            shaped((own, HEAD_DIM), F32),
        ),
        in_specs=[SMEM, SMEM, VMEM, VMEM, VMEM, ANY],
        out_specs=(VMEM,) * 5,
        scratch_shapes=[
            pltpu.VMEM((chunks, depth, width), BF16),
            pltpu.VMEM((requests * draft, draft), F32),
            pltpu.SemaphoreType.DMA((chunks,)),
        ],
        compiler_params=params(16),
        cost_estimate=pl.CostEstimate(
            flops=2 * own * model * width, bytes_accessed=2 * model * width, transcendentals=0
        ),
        name="project_v_and_tree",
    )(cache_lengths, accepted_leaf, hidden_in, parents, freqs, value_weight)

    queries, keys_values = pl.pallas_call(
        functools.partial(prepare, tp * width),
        out_shape=(shaped((seq, own, width), BF16), shaped((seq, own, 2 * width), BF16)),
        in_specs=[VMEM] * 8,
        out_specs=(VMEM, VMEM),
        compiler_params=params(16),
        name="prepare",
    )(
        query_raw,
        key_raw,
        value,
        query_gain[None, :],
        key_gain[None, :],
        cosine,
        sine,
        squares,
    )
    queries = exchange(queries, "seq")
    keys_values = exchange(keys_values, "seq")

    partials = pl.pallas_call(
        functools.partial(attend_cache, group),
        out_shape=shaped((seq, own, width + LANES), BF16),
        in_specs=[SMEM, VMEM, VMEM, VMEM],
        out_specs=VMEM,
        compiler_params=params(16),
        name="attend_cache",
    )(cache_lengths, key_cache, value_cache, queries)
    partials = exchange(partials, "seq")

    draft_out, draft_stats = pl.pallas_call(
        functools.partial(attend_draft, group),
        out_shape=(shaped((own, width), F32), shaped((own, LANES), F32)),
        in_specs=[VMEM] * 3,
        out_specs=(VMEM, VMEM),
        compiler_params=params(16),
        name="attend_draft",
    )(own_tree, queries, keys_values)

    projected = pl.pallas_call(
        merge_and_project,
        out_shape=shaped((tp, own, columns), BF16),
        in_specs=[VMEM, VMEM, ANY, VMEM],
        out_specs=VMEM,
        scratch_shapes=[
            pltpu.VMEM((tp, width, columns), BF16),
            pltpu.SemaphoreType.DMA((tp,)),
        ],
        compiler_params=params(16),
        name="merge_and_project",
    )(draft_out, draft_stats, out_weight, partials)
    projected = exchange(projected, "tp")

    summed, power = pl.pallas_call(
        add_up,
        out_shape=(shaped((own, columns), F32), shaped((tp, own, LANES), F32)),
        in_specs=[VMEM],
        out_specs=(VMEM, VMEM),
        compiler_params=params(16),
        name="add_up",
    )(projected)
    power = exchange(power, "tp")

    hidden_out = pl.pallas_call(
        functools.partial(finish, model),
        out_shape=shaped((own, columns), BF16),
        in_specs=[VMEM] * 4,
        out_specs=VMEM,
        compiler_params=params(16),
        name="finish",
    )(summed, post_gain[None, :], hidden_in, power)

    new_key_cache, new_value_cache = pl.pallas_call(
        functools.partial(compact, group),
        out_shape=(shaped(key_cache.shape, BF16), shaped(value_cache.shape, BF16)),
        in_specs=[VMEM] * 4,
        out_specs=(VMEM, VMEM),
        compiler_params=params(24),
        name="compact",
    )(targets, key_cache, value_cache, keys_values)
    return (hidden_out, new_key_cache, new_value_cache)


def across(column):
    rows = column.shape[0]
    eye = iota((rows, rows), 0) == iota((rows, rows), 1)
    return jnp.sum(jnp.where(eye, column, 0.0), axis=0, keepdims=True)


def upright(line):
    rows = line.shape[1]
    eye = iota((rows, rows), 0) == iota((rows, rows), 1)
    return jnp.sum(jnp.where(eye, line, 0.0), axis=1, keepdims=True)


def eye_of(size):
    return (iota((size, size), 0) == iota((size, size), 1)).astype(BF16)


def plane():
    return lax.axis_index("seq") // 2


def twin_load(wq, wk, wq_v, wk_v, sems):
    chunks = sems.shape[1]
    depth = wq.shape[0] // chunks
    copies = []
    for at, (source, target) in enumerate(((wq, wq_v), (wk, wk_v))):
        for c in range(chunks):
            rows = pl.ds(c * depth, depth)
            copies.append(
                pltpu.make_async_copy(source.at[rows], target.at[rows], sems.at[at, c])
            )
    for copy in copies:
        copy.start()
    for copy in copies:
        copy.wait()


def twin_project_qk(hidden, wq, wk, query_raw, key_raw, squares):
    rows = hidden[...]
    own = rows.shape[0]
    for at, (weight, raw) in enumerate(((wq, query_raw), (wk, key_raw))):
        product = dot(rows, weight[...])
        raw[...] = product
        line = across(sum_squares(product))
        line = jnp.concatenate([line, jnp.zeros((1, LANES - own), F32)], axis=1)
        squares[:, at * LANES : (at + 1) * LANES] = jnp.broadcast_to(
            line, (squares.shape[0], LANES)
        )


def twin_project_v(hidden, wv, value):
    value[...] = dot(hidden[...], wv[...]).astype(BF16)


def twin_tree(
    turns, lengths, leaves, parents, freqs, own_tree, targets, cosine, sine, limits, held
):
    requests, draft = parents.shape
    own = own_tree.shape[1]
    row, col = iota((draft, draft), 0), iota((draft, draft), 1)
    eye = eye_of(draft)

    def length_of(request):
        picked = iota(lengths.shape, 1) == request
        return jnp.sum(jnp.where(picked, lengths[...], 0), axis=1, keepdims=True)

    for at, turn in enumerate(turns):
        limits[at : at + 1, :] = jnp.broadcast_to(
            length_of(plane() ^ turn), (1, limits.shape[1])
        )
    trees = [
        jnp.where((parents[pl.ds(r, 1), :] == row) | (row == col), 1.0, 0.0).astype(BF16)
        for r in range(requests)
    ]
    for _ in range(max(1, (draft - 1).bit_length())):
        trees = [jnp.minimum(dot(tree, tree), 1.0).astype(BF16) for tree in trees]
    for r in range(requests):
        standing = lax.dot_general(
            trees[r], eye, (((0,), (0,)), ((), ())), preferred_element_type=F32
        )
        held[r] = standing
        level = jnp.sum(trees[r].astype(F32), axis=0, keepdims=True) - 1.0
        on_path = jnp.where(row == leaves[:, r : r + 1], standing, 0.0)
        on_path = jnp.sum(on_path, axis=0, keepdims=True)
        place = lengths[:, r : r + 1] + level.astype(jnp.int32)
        targets[r] = jnp.where(on_path > 0.5, place, -1)
    within = lax.rem(lax.axis_index("seq"), 2)
    for at in range(2):
        first = (within ^ at) * own
        rows = held[plane(), pl.ds(pl.multiple_of(first, own), own), :]
        own_tree[at * own : (at + 1) * own, :] = jnp.where(
            within == 0, rows[:, :own], rows[:, own:]
        )
        mine = rows if at == 0 else mine
    level = jnp.sum(mine, axis=1, keepdims=True) - 1.0
    angles = (length_of(plane()).astype(F32) + level) * freqs[...]
    cosine[...] = jnp.cos(angles)
    half = jnp.sin(angles)
    sine[...] = jnp.where(iota(half.shape, 1) < HEAD_DIM // 2, -half, half)


def turned(raw, scale, gain, cos, sin):
    x = raw * scale * gain
    return (x * cos + pltpu.roll(x, HEAD_DIM // 2, 1) * sin).astype(BF16)


def twin_prepare(width_all, query_raw, key_raw, value, q_gain, k_gain, cosine, sine, *refs):
    squares, (queries, packed) = refs[:-2], refs[-2:]
    own, width = query_raw.shape
    cos, sin = cosine[...], sine[...]
    total = sum(ref[:1, :] for ref in squares)
    for at, (raw, gain) in enumerate(((query_raw, q_gain), (key_raw, k_gain))):
        scale = upright(total[:, at * LANES : at * LANES + own])
        scale = lax.rsqrt(scale / width_all + EPS)
        for h in range(width // HEAD_DIM):
            lanes = slice(h * HEAD_DIM, (h + 1) * HEAD_DIM)
            there = slice(at * width + h * HEAD_DIM, at * width + (h + 1) * HEAD_DIM)
            found = turned(raw[:, lanes], scale, gain[:, lanes], cos, sin)
            packed[:, there] = found
            if at == 0:
                queries[:, lanes] = found
    packed[:, 2 * width :] = value[...]


def weigh(s, visible):
    peak = jnp.max(s, axis=1, keepdims=True).astype(BF16).astype(F32)
    weights = jnp.exp(jnp.where(visible, s - peak, NEG))
    total = jnp.sum(weights, axis=1, keepdims=True)
    high = total.astype(BF16).astype(F32)
    return weights.astype(BF16), (peak, high, total - high)


def kept(stats, h, heads, found):
    lane = iota(stats.shape, 1)
    for at, column in enumerate(found):
        stats = jnp.where(lane == at * heads + h, column, stats)
    return stats


def write_stats(stats, out):
    own, width = stats.shape[0], out.shape[1]
    flat = lax.dot_general(
        stats.astype(BF16), eye_of(own), (((0,), (0,)), ((), ())), preferred_element_type=F32
    )
    flat = jnp.concatenate([flat[:16], jnp.zeros((16, width - own), F32)], axis=1)
    out[own : own + 16, :] = flat.astype(BF16)


def twin_attend(far, limits, key_cache, value_cache, swapped, own_tree, mine, other, *refs):
    count = len(far)
    queries, outs = refs[:count], refs[count : 2 * count]
    crossing, local, scores, own_scores = refs[2 * count :]
    block, width = key_cache.shape[1:]
    heads = width // HEAD_DIM
    own = other.shape[0]
    me = lax.axis_index("seq")
    factor = 1.0 / math.sqrt(HEAD_DIM)
    place = iota((1, block), 1)
    both = jnp.concatenate([me * block + place, (me ^ 1) * block + place], axis=1)
    visible = [both < limits[at + 1 : at + 2, :] for at in range(count)]
    here = jnp.broadcast_to((me * block + place) < limits[:1, :block], (2 * own, block))
    near = jnp.concatenate(
        [
            jnp.where(here, 1.0, 0.0),
            own_tree[...],
            jnp.zeros((2 * own, own_scores.shape[2] - block - own), F32),
        ],
        axis=1,
    )
    near = near > 0.5
    for at, turn in enumerate(far):
        for h in range(heads):
            lanes = slice(h * HEAD_DIM, (h + 1) * HEAD_DIM)
            q = queries[at][:, lanes]
            first = dot_t(q, key_cache[plane() ^ turn, :, lanes])
            second = dot_t(q, swapped[at, 0, :, lanes])
            product = jnp.concatenate([first, second], axis=1) * factor
            scores[at, h] = jnp.where(visible[at], product, NEG)
    pair = stacked([mine[:, :width], other[...]])
    rest = own_scores.shape[2] - block - own
    for h in range(heads):
        lanes = slice(h * HEAD_DIM, (h + 1) * HEAD_DIM)
        keys = jnp.concatenate(
            [mine[:, width + h * HEAD_DIM : width + (h + 1) * HEAD_DIM]] * (1 + rest // own), axis=0
        )
        first = dot_t(pair[:, lanes], key_cache[plane(), :, lanes])
        product = jnp.concatenate([first, dot_t(pair[:, lanes], keys)], axis=1) * factor
        own_scores[h] = jnp.where(near, product, NEG)
    for at, turn in enumerate(far):
        stats = jnp.zeros((own, LANES), F32)
        for h in range(heads):
            lanes = slice(h * HEAD_DIM, (h + 1) * HEAD_DIM)
            weights, found = weigh(scores[at, h], visible[at])
            out = dot(weights[:, :block], value_cache[plane() ^ turn, :, lanes])
            out = out + dot(weights[:, block:], swapped[at, 1, :, lanes])
            outs[at][:own, lanes] = out.astype(BF16)
            stats = kept(stats, h, heads, found)
        write_stats(stats, outs[at])
    stats = jnp.zeros((2 * own, LANES), F32)
    for h in range(heads):
        lanes = slice(h * HEAD_DIM, (h + 1) * HEAD_DIM)
        weights, found = weigh(own_scores[h], near)
        out = dot(weights[:, :block], value_cache[plane(), :, lanes])
        values = mine[:, 2 * width + h * HEAD_DIM : 2 * width + (h + 1) * HEAD_DIM]
        out = out + dot(weights[:, block : block + own], values)
        out = out.astype(BF16)
        local[:own, lanes] = out[:own]
        crossing[:own, lanes] = out[own:]
        stats = kept(stats, h, heads, found)
    write_stats(stats[:own], local)
    write_stats(stats[own:], crossing)


def twin_rows(mine, theirs, held):
    within = lax.rem(lax.axis_index("seq"), 2)
    held[within] = mine
    held[1 - within] = theirs
    return stacked([held[0], held[1]])


def twin_merge_and_project(*refs):
    partials, (wo, mine), refs = refs[:5], refs[5:7], refs[7:]
    gathered, (total_out, rounded, keys, values) = refs[:-4], refs[-4:]
    own, width = mine.shape[0], keys.shape[1]
    heads = width // HEAD_DIM
    for at, ref in enumerate((mine, *gathered)):
        keys[at * own : (at + 1) * own, :] = ref[:, width : 2 * width]
        values[at * own : (at + 1) * own, :] = ref[:, 2 * width :]
    stats = [dot_t(eye_of(own), ref[own : own + 16, :own]) for ref in partials]
    attention = []
    for h in range(heads):
        lanes = slice(h * HEAD_DIM, (h + 1) * HEAD_DIM)
        peaks = [s[:, h : h + 1] for s in stats]
        highest = functools.reduce(jnp.maximum, peaks)
        total, summed = 0.0, 0.0
        for ref, s, peak in zip(partials, stats, peaks):
            scale = jnp.exp(peak - highest)
            own_total = s[:, heads + h : heads + h + 1] + s[:, 2 * heads + h : 2 * heads + h + 1]
            total = total + own_total * scale
            summed = summed + ref[:own, lanes].astype(F32) * scale
        attention.append((summed / total).astype(BF16))
    product = dot(jnp.concatenate(attention, axis=1), wo[...])
    total_out[...] = product
    rounded[...] = product.astype(BF16)


def twin_add(mine, theirs, total, rounded):
    both = mine[...] + theirs[...].astype(F32)
    total[...] = both
    rounded[...] = both.astype(BF16)


def twin_finish(mine, theirs, gain, hidden, out):
    model_width = mine.shape[1]
    columns = out.shape[1]
    total = mine[...] + theirs[...].astype(F32)
    scale = lax.rsqrt(sum_squares(total) / model_width + EPS)
    lanes = pl.ds(pl.multiple_of(lax.axis_index("tp") * columns, columns), columns)
    normed = (mine[:, lanes] + theirs[:, lanes].astype(F32)) * scale * gain[...]
    out[...] = (hidden[:, lanes].astype(F32) + normed).astype(BF16)


def twin_compact(far, targets, key_cache, value_cache, *refs):
    count = len(far) + 1
    ours, (keys, values, new_keys, new_values, held) = refs[:count], refs[count:]
    block, width = key_cache.shape[1:]
    own = ours[0].shape[0]
    me = lax.axis_index("seq")
    place = me * block + iota((block, targets.shape[2]), 0)
    for at, turn in enumerate((0, *far)):
        request = plane() ^ turn
        placing = place == targets[request]
        written = jnp.max(placing.astype(F32), axis=1, keepdims=True) > 0.5
        placing = placing.astype(BF16)
        for part, (crossed, cache, out) in enumerate(
            ((keys, key_cache, new_keys), (values, value_cache, new_values))
        ):
            lanes = slice((part + 1) * width, (part + 2) * width)
            theirs = crossed[at * own : (at + 1) * own, :]
            fresh = twin_rows(ours[at][:, lanes], theirs, held.at[at, part])
            moved = dot(placing, fresh)
            out[request] = jnp.where(written, moved, cache[request].astype(F32)).astype(BF16)


def body_twin(
    hidden_in,
    query_weight,
    key_weight,
    value_weight,
    out_weight,
    query_gain,
    key_gain,
    post_gain,
    key_cache,
    value_cache,
    cache_lengths,
    parents,
    accepted_leaf,
):
    requests, block, width = key_cache.shape
    draft = parents.shape[1]
    own, model = hidden_in.shape
    tp = lax.axis_size("tp")
    seq = lax.axis_size("seq")
    columns = model // tp
    heads = width // HEAD_DIM
    far = tuple(range(requests - 1, 0, -1))

    def call(kernel, outs, inputs, scratch=(), mib=16, specs=None, ties=()):
        count = len(inputs)

        def run(*refs):
            kernel(*refs[:count], *refs[count + len(ties) :])

        return pl.pallas_call(
            run,
            out_shape=outs,
            in_specs=([VMEM] * count if specs is None else specs) + [ANY] * len(ties),
            out_specs=jax.tree.map(lambda _: VMEM, outs),
            scratch_shapes=list(scratch),
            compiler_params=params(mib),
            name=getattr(kernel, "func", kernel).__name__,
        )(*inputs, *ties)

    def over_tp(x, k):
        return lax.ppermute(x, "tp", [(i, i ^ k) for i in range(tp)])

    def beside(x):
        return lax.ppermute(x, "seq", [(i, i ^ 1) for i in range(seq)])

    def over_planes(x, turn):
        return lax.ppermute(x, "seq", [(i, (i // 2 ^ turn) * 2 + i % 2) for i in range(seq)])

    me = lax.axis_index("seq") // 2
    picked = jnp.stack(
        [
            jnp.stack([lax.dynamic_index_in_dim(x, me ^ turn, 0, False) for x in (key_cache, value_cache)])
            for turn in far
        ]
    )
    swapped = beside(picked)
    wq, wk = call(
        twin_load,
        (shaped(query_weight.shape, BF16), shaped(key_weight.shape, BF16)),
        (query_weight, key_weight),
        [pltpu.SemaphoreType.DMA((2, 4))],
        mib=48,
        specs=[ANY] * 2,
    )
    query_raw, key_raw, squares = call(
        twin_project_qk,
        (shaped((own, width), F32), shaped((own, width), F32), shaped((8, 2 * LANES), F32)),
        (hidden_in, wq, wk),
    )
    all_squares = [squares] + [over_tp(squares, k) for k in range(tp - 1, 0, -1)]

    exponents = -2.0 * (jnp.arange(HEAD_DIM) % (HEAD_DIM // 2)).astype(F32) / HEAD_DIM
    freqs = (THETA**exponents)[None, :]
    own_tree, targets, cosine, sine, limits = call(
        functools.partial(twin_tree, (0, *far)),
        (
            shaped((draft, own), F32),
            shaped((requests, 1, draft), jnp.int32),
            shaped((own, HEAD_DIM), F32),
            shaped((own, HEAD_DIM), F32),
            shaped((requests, 2 * block), jnp.int32),
        ),
        (cache_lengths[None, :], accepted_leaf[None, :], parents, freqs),
        [pltpu.VMEM((requests, draft, draft), F32)],
    )
    value = call(twin_project_v, shaped((own, width), BF16), (hidden_in, value_weight))
    queries, packed = call(
        functools.partial(twin_prepare, tp * width),
        (shaped((own, width), BF16), shaped((own, 3 * width), BF16)),
        (
            query_raw,
            key_raw,
            value,
            query_gain[None, :],
            key_gain[None, :],
            cosine,
            sine,
            *all_squares,
        ),
    )
    from_far = [over_planes(packed, turn) for turn in far]
    other = beside(queries)

    rows = own + 16
    *partials, crossing, local = call(
        functools.partial(twin_attend, far),
        (shaped((rows, width), BF16),) * (len(far) + 2),
        (limits, key_cache, value_cache, swapped, own_tree, packed, other, *from_far),
        [
            pltpu.VMEM((len(far), heads, own, 2 * block), F32),
            pltpu.VMEM((heads, 2 * own, block + LANES), F32),
        ],
    )
    partials = [over_planes(part, turn) for part, turn in zip(partials, far)]
    partials += [beside(crossing)]
    partials = [partials[2], partials[3], partials[0], partials[1], local]

    total, rounded, keys, values = call(
        twin_merge_and_project,
        (
            shaped((own, model), F32),
            shaped((own, model), BF16),
            shaped((requests * own, width), BF16),
            shaped((requests * own, width), BF16),
        ),
        (*partials, out_weight, packed, *from_far),
    )
    keys, values = beside(keys), beside(values)
    bit = 1
    while 2 * bit < tp:
        total, rounded = call(
            twin_add,
            (shaped((own, model), F32), shaped((own, model), BF16)),
            (total, over_tp(rounded, bit)),
        )
        bit *= 2
    arrived = over_tp(rounded, bit)
    new_key_cache, new_value_cache = call(
        functools.partial(twin_compact, far),
        (shaped(key_cache.shape, BF16), shaped(value_cache.shape, BF16)),
        (targets, key_cache, value_cache, packed, *from_far, keys, values),
        [pltpu.VMEM((requests, 2, 2, own, width), BF16)],
    )
    hidden_out = call(
        twin_finish,
        shaped((own, columns), BF16),
        (total, arrived, post_gain[None, :], hidden_in),
    )
    return (hidden_out, new_key_cache, new_value_cache)


def body(*args):
    hidden_in, key_cache, parents = args[0], args[8], args[11]
    tp = lax.axis_size("tp")
    own, draft = hidden_in.shape[0], parents.shape[1]
    requests, _, width = key_cache.shape
    twin = (
        own % 16 == 0
        and draft == 2 * own
        and requests == 4
        and lax.axis_size("seq") == 2 * requests
        and own <= LANES
        and LANES % own == 0
        and own <= width
        and 3 * (width // HEAD_DIM) <= 16
        and tp > 1
        and tp & (tp - 1) == 0
    )
    return (body_twin if twin else body_general)(*args)


def solution(mesh):
    return jax.shard_map(
        body,
        mesh=mesh,
        in_specs=(
            P("seq", None),
            P(None, "tp"),
            P(None, "tp"),
            P(None, "tp"),
            P("tp", None),
            P("tp"),
            P("tp"),
            P("tp"),
            P(None, "seq", "tp"),
            P(None, "seq", "tp"),
            P(),
            P(),
            P(),
        ),
        out_specs=(P("seq", "tp"), P(None, "seq", "tp"), P(None, "seq", "tp")),
        check_vma=False,
    )
```

```python
import functools
import math

import jax
import jax.numpy as jnp
from jax import lax
from jax.experimental import pallas as pl
from jax.experimental.pallas import tpu as pltpu
from jax.sharding import PartitionSpec as P

HEAD_DIM = 128
LANES = 128
EPS = 1e-06
THETA = 500000.0
NEG = -1e30
F32 = jnp.float32
BF16 = jnp.bfloat16
VMEM = pl.BlockSpec(memory_space=pltpu.VMEM)
SMEM = pl.BlockSpec(memory_space=pltpu.SMEM)
ANY = pl.BlockSpec(memory_space=pl.ANY)


def params(mib):
    return pltpu.CompilerParams(vmem_limit_bytes=mib * 1024 * 1024)


def dot(a, b):
    return jnp.dot(a, b, preferred_element_type=F32)


def dot_t(a, b):
    return lax.dot_general(a, b, (((1,), (1,)), ((), ())), preferred_element_type=F32)


def iota(shape, axis):
    return lax.broadcasted_iota(jnp.int32, shape, axis)


def stacked(parts):
    if len(parts) == 1:
        return parts[0]
    if parts[0].shape[0] % 16 == 0:
        return jnp.concatenate(parts, axis=0)
    return jnp.concatenate([part.astype(F32) for part in parts], axis=0).astype(BF16)


def sum_squares(raw):
    return jnp.sum(raw * raw, axis=1, keepdims=True)


def project_qk(hidden, wq, wk, query_raw, key_raw, squares, wq_v, wk_v, sems):
    chunks, depth = wq_v.shape[0], wq_v.shape[1]
    copies = []
    for c in range(chunks):
        for at, (source, target) in enumerate(((wq, wq_v), (wk, wk_v))):
            copy = pltpu.make_async_copy(
                source.at[pl.ds(c * depth, depth)], target.at[c], sems.at[2 * c + at]
            )
            copy.start()
            copies.append(copy)
    q_sum, k_sum = None, None
    for c in range(chunks):
        part = hidden[:, c * depth : (c + 1) * depth]
        copies[2 * c].wait()
        q = dot(part, wq_v[c])
        copies[2 * c + 1].wait()
        k = dot(part, wk_v[c])
        q_sum = q if c == 0 else q_sum + q
        k_sum = k if c == 0 else k_sum + k
    query_raw[...] = q_sum
    key_raw[...] = k_sum
    lane = iota(squares.shape[1:], 1)
    both = jnp.where(lane == 0, sum_squares(q_sum), sum_squares(k_sum))
    for t in range(squares.shape[0]):
        squares[t] = both


def project_v_and_tree(
    lengths, leaves, hidden, parents, freqs, wv, value, own_tree, targets, cosine, sine, wv_v, anc_v, sems
):
    chunks, depth = wv_v.shape[0], wv_v.shape[1]
    copies = []
    for c in range(chunks):
        copy = pltpu.make_async_copy(wv.at[pl.ds(c * depth, depth)], wv_v.at[c], sems.at[c])
        copy.start()
        copies.append(copy)
    requests, draft = parents.shape
    own = hidden.shape[0]
    first = lax.axis_index("seq") * own
    row, col = iota((draft, draft), 0), iota((draft, draft), 1)
    eye = (row == col).astype(BF16)
    trees = [
        jnp.where((parents[pl.ds(r, 1), :] == row) | (row == col), 1.0, 0.0).astype(BF16)
        for r in range(requests)
    ]
    for _ in range(max(1, (draft - 1).bit_length())):
        trees = [jnp.minimum(dot(tree, tree), 1.0).astype(BF16) for tree in trees]
    for r in range(requests):
        upright = lax.dot_general(
            trees[r], eye, (((0,), (0,)), ((), ())), preferred_element_type=F32
        )
        anc_v[pl.ds(r * draft, draft), :] = upright
        level = jnp.sum(trees[r].astype(F32), axis=0, keepdims=True) - 1.0
        on_path = jnp.sum(jnp.where(row == leaves[r], upright, 0.0), axis=0, keepdims=True)
        place = lengths[r] + level.astype(jnp.int32)
        targets[r] = jnp.where(on_path > 0.5, place, -1)
    mine = anc_v[pl.ds(pl.multiple_of(first, own), own), :]
    own_tree[...] = mine
    level = jnp.sum(mine, axis=1, keepdims=True) - 1.0
    position = lengths[first // draft].astype(F32) + level
    angles = position * freqs[...]
    cosine[...] = jnp.cos(angles)
    half = jnp.sin(angles)
    sine[...] = jnp.where(iota(half.shape, 1) < HEAD_DIM // 2, -half, half)
    total = None
    for c in range(chunks):
        copies[c].wait()
        v = dot(hidden[:, c * depth : (c + 1) * depth], wv_v[c])
        total = v if c == 0 else total + v
    value[...] = total.astype(BF16)


def prepare(
    width_all, query_raw, key_raw, value, q_gain, k_gain, cosine, sine, squares, queries, keys_values
):
    width = query_raw.shape[1]
    total = sum(squares[k] for k in range(squares.shape[0]))
    cos, sin = cosine[...], sine[...]
    for at, (raw, gain, out) in enumerate(
        ((query_raw, q_gain, queries), (key_raw, k_gain, keys_values))
    ):
        scale = lax.rsqrt(total[:, at : at + 1] / width_all + EPS)
        for h in range(width // HEAD_DIM):
            lanes = slice(h * HEAD_DIM, (h + 1) * HEAD_DIM)
            x = raw[:, lanes] * scale * gain[:, lanes]
            turned = x * cos + pltpu.roll(x, HEAD_DIM // 2, 1) * sin
            turned = turned.astype(BF16)
            for s in range(out.shape[0]):
                out[s, :, lanes] = turned
    for s in range(keys_values.shape[0]):
        keys_values[s, :, width:] = value[...]


def attend_cache(group, lengths, key_cache, value_cache, queries, partials):
    requests, block, width = key_cache.shape
    own = queries.shape[1]
    heads = width // HEAD_DIM
    me = lax.axis_index("seq")
    factor = 1.0 / math.sqrt(HEAD_DIM)
    rows = group * own
    place = me * block + iota((rows, block), 1)
    lane = iota((rows, LANES), 1)
    for request in range(requests):
        q = stacked([queries[request * group + j] for j in range(group)])
        visible = place < lengths[request]
        stats = jnp.zeros((rows, LANES), F32)
        for h in range(heads):
            lanes = slice(h * HEAD_DIM, (h + 1) * HEAD_DIM)
            scores = dot_t(q[:, lanes], key_cache[request, :, lanes]) * factor
            scores = jnp.where(visible, scores, NEG)
            peak = jnp.max(scores, axis=1, keepdims=True).astype(BF16).astype(F32)
            weights = jnp.exp(jnp.where(visible, scores - peak, NEG))
            total = jnp.sum(weights, axis=1, keepdims=True)
            high = total.astype(BF16).astype(F32)
            out = dot(weights.astype(BF16), value_cache[request, :, lanes]).astype(BF16)
            for j in range(group):
                partials[request * group + j, :, lanes] = out[j * own : (j + 1) * own]
            stats = jnp.where(lane == h, peak, stats)
            stats = jnp.where(lane == heads + h, high, stats)
            stats = jnp.where(lane == 2 * heads + h, total - high, stats)
        stats = stats.astype(BF16)
        for j in range(group):
            partials[request * group + j, :, width:] = stats[j * own : (j + 1) * own]


def attend_draft(group, own_tree, queries, keys_values, out, stats):
    own, width = queries.shape[1:]
    heads = width // HEAD_DIM
    me = lax.axis_index("seq")
    first = me // group * group
    q = queries[me]
    pair = stacked([keys_values[first + j] for j in range(group)])
    factor = 1.0 / math.sqrt(HEAD_DIM)
    allowed = own_tree[...] > 0.5
    lane = iota((own, LANES), 1)
    kept = jnp.zeros((own, LANES), F32)
    for h in range(heads):
        lanes = slice(h * HEAD_DIM, (h + 1) * HEAD_DIM)
        there = slice(width + h * HEAD_DIM, width + (h + 1) * HEAD_DIM)
        scores = dot_t(q[:, lanes], pair[:, lanes]) * factor
        scores = jnp.where(allowed, scores, NEG)
        peak = jnp.max(scores, axis=1, keepdims=True)
        weights = jnp.exp(jnp.where(allowed, scores - peak, NEG))
        out[:, lanes] = dot(weights.astype(BF16), pair[:, there])
        kept = jnp.where(lane == h, peak, kept)
        kept = jnp.where(lane == heads + h, jnp.sum(weights, axis=1, keepdims=True), kept)
    stats[...] = kept


def merge_and_project(draft_out, draft_stats, wo, partials, projected, wo_v, sems):
    count, width, columns = wo_v.shape
    heads = width // HEAD_DIM
    copies = []
    for k in range(count):
        copy = pltpu.make_async_copy(
            wo.at[:, pl.ds(k * columns, columns)], wo_v.at[k], sems.at[k]
        )
        copy.start()
        copies.append(copy)
    parts = range(partials.shape[0])
    stats = [partials[s, :, width:].astype(F32) for s in parts]
    own_stats = draft_stats[...]
    attention = []
    for h in range(heads):
        lanes = slice(h * HEAD_DIM, (h + 1) * HEAD_DIM)
        peaks = [s[:, h : h + 1] for s in stats] + [own_stats[:, h : h + 1]]
        highest = functools.reduce(jnp.maximum, peaks)
        scales = [jnp.exp(peak - highest) for peak in peaks]
        total = own_stats[:, heads + h : heads + h + 1] * scales[-1]
        summed = draft_out[:, lanes] * scales[-1]
        for at in parts:
            s = stats[at]
            own_total = s[:, heads + h : heads + h + 1] + s[:, 2 * heads + h : 2 * heads + h + 1]
            total = total + own_total * scales[at]
            summed = summed + partials[at, :, lanes].astype(F32) * scales[at]
        attention.append((summed / total).astype(BF16))
    attention = jnp.concatenate(attention, axis=1)
    for k in range(count):
        copies[k].wait()
        projected[k] = dot(attention, wo_v[k]).astype(projected.dtype)


def add_up(parts, summed, power):
    total = sum(parts[k].astype(F32) for k in range(parts.shape[0]))
    summed[...] = total
    own_power = jnp.broadcast_to(sum_squares(total), power.shape[1:])
    for k in range(power.shape[0]):
        power[k] = own_power


def finish(model_width, summed, gain, hidden, powers, out):
    columns = summed.shape[1]
    power = sum(powers[k] for k in range(powers.shape[0]))[:, :1]
    start = pl.multiple_of(lax.axis_index("tp") * columns, columns)
    normed = summed[...] * lax.rsqrt(power / model_width + EPS) * gain[...]
    out[...] = (hidden[:, pl.ds(start, columns)].astype(F32) + normed).astype(BF16)


def compact(group, targets, key_cache, value_cache, keys_values, new_keys, new_values):
    requests, block, width = key_cache.shape
    own = keys_values.shape[1]
    me = lax.axis_index("seq")
    place = me * block + iota((block, group * own), 0)
    for request in range(requests):
        kv = stacked([keys_values[request * group + j] for j in range(group)])
        placing = place == targets[request]
        written = jnp.max(placing.astype(F32), axis=1, keepdims=True) > 0.5
        fresh = dot(placing.astype(BF16), kv)
        new_keys[request] = jnp.where(
            written, fresh[:, :width], key_cache[request].astype(F32)
        ).astype(BF16)
        new_values[request] = jnp.where(
            written, fresh[:, width:], value_cache[request].astype(F32)
        ).astype(BF16)


def shaped(shape, dtype):
    return jax.ShapeDtypeStruct(shape, dtype)


def body_general(
    hidden_in,
    query_weight,
    key_weight,
    value_weight,
    out_weight,
    query_gain,
    key_gain,
    post_gain,
    key_cache,
    value_cache,
    cache_lengths,
    parents,
    accepted_leaf,
):
    requests, block, width = key_cache.shape
    draft = parents.shape[1]
    own, model = hidden_in.shape
    tp = lax.axis_size("tp")
    seq = lax.axis_size("seq")
    group = draft // own
    columns = model // tp
    chunks = 4
    depth = model // chunks

    def exchange(x, axis):
        return lax.all_to_all(x, axis, 0, 0, tiled=True)

    query_raw, key_raw, squares = pl.pallas_call(
        project_qk,
        out_shape=(
            shaped((own, width), F32),
            shaped((own, width), F32),
            shaped((tp, own, LANES), F32),
        ),
        in_specs=[VMEM, ANY, ANY],
        out_specs=(VMEM, VMEM, VMEM),
        scratch_shapes=[
            pltpu.VMEM((chunks, depth, width), BF16),
            pltpu.VMEM((chunks, depth, width), BF16),
            pltpu.SemaphoreType.DMA((2 * chunks,)),
        ],
        compiler_params=params(56),
        cost_estimate=pl.CostEstimate(
            flops=4 * own * model * width, bytes_accessed=4 * model * width, transcendentals=0
        ),
        name="project_qk",
    )(hidden_in, query_weight, key_weight)
    squares = exchange(squares, "tp")

    exponents = -2.0 * (jnp.arange(HEAD_DIM) % (HEAD_DIM // 2)).astype(F32) / HEAD_DIM
    freqs = (THETA**exponents)[None, :]
    value, own_tree, targets, cosine, sine = pl.pallas_call(
        project_v_and_tree,
        out_shape=(
            shaped((own, width), BF16),
            shaped((own, draft), F32),
            shaped((requests, 1, draft), jnp.int32),
            shaped((own, HEAD_DIM), F32),
            shaped((own, HEAD_DIM), F32),
        ),
        in_specs=[SMEM, SMEM, VMEM, VMEM, VMEM, ANY],
        out_specs=(VMEM,) * 5,
        scratch_shapes=[
            pltpu.VMEM((chunks, depth, width), BF16),
            pltpu.VMEM((requests * draft, draft), F32),
            pltpu.SemaphoreType.DMA((chunks,)),
        ],
        compiler_params=params(16),
        cost_estimate=pl.CostEstimate(
            flops=2 * own * model * width, bytes_accessed=2 * model * width, transcendentals=0
        ),
        name="project_v_and_tree",
    )(cache_lengths, accepted_leaf, hidden_in, parents, freqs, value_weight)

    queries, keys_values = pl.pallas_call(
        functools.partial(prepare, tp * width),
        out_shape=(shaped((seq, own, width), BF16), shaped((seq, own, 2 * width), BF16)),
        in_specs=[VMEM] * 8,
        out_specs=(VMEM, VMEM),
        compiler_params=params(16),
        name="prepare",
    )(
        query_raw,
        key_raw,
        value,
        query_gain[None, :],
        key_gain[None, :],
        cosine,
        sine,
        squares,
    )
    queries = exchange(queries, "seq")
    keys_values = exchange(keys_values, "seq")

    partials = pl.pallas_call(
        functools.partial(attend_cache, group),
        out_shape=shaped((seq, own, width + LANES), BF16),
        in_specs=[SMEM, VMEM, VMEM, VMEM],
        out_specs=VMEM,
        compiler_params=params(16),
        name="attend_cache",
    )(cache_lengths, key_cache, value_cache, queries)
    partials = exchange(partials, "seq")

    draft_out, draft_stats = pl.pallas_call(
        functools.partial(attend_draft, group),
        out_shape=(shaped((own, width), F32), shaped((own, LANES), F32)),
        in_specs=[VMEM] * 3,
        out_specs=(VMEM, VMEM),
        compiler_params=params(16),
        name="attend_draft",
    )(own_tree, queries, keys_values)

    projected = pl.pallas_call(
        merge_and_project,
        out_shape=shaped((tp, own, columns), BF16),
        in_specs=[VMEM, VMEM, ANY, VMEM],
        out_specs=VMEM,
        scratch_shapes=[
            pltpu.VMEM((tp, width, columns), BF16),
            pltpu.SemaphoreType.DMA((tp,)),
        ],
        compiler_params=params(16),
        name="merge_and_project",
    )(draft_out, draft_stats, out_weight, partials)
    projected = exchange(projected, "tp")

    summed, power = pl.pallas_call(
        add_up,
        out_shape=(shaped((own, columns), F32), shaped((tp, own, LANES), F32)),
        in_specs=[VMEM],
        out_specs=(VMEM, VMEM),
        compiler_params=params(16),
        name="add_up",
    )(projected)
    power = exchange(power, "tp")

    hidden_out = pl.pallas_call(
        functools.partial(finish, model),
        out_shape=shaped((own, columns), BF16),
        in_specs=[VMEM] * 4,
        out_specs=VMEM,
        compiler_params=params(16),
        name="finish",
    )(summed, post_gain[None, :], hidden_in, power)

    new_key_cache, new_value_cache = pl.pallas_call(
        functools.partial(compact, group),
        out_shape=(shaped(key_cache.shape, BF16), shaped(value_cache.shape, BF16)),
        in_specs=[VMEM] * 4,
        out_specs=(VMEM, VMEM),
        compiler_params=params(24),
        name="compact",
    )(targets, key_cache, value_cache, keys_values)
    return (hidden_out, new_key_cache, new_value_cache)


def across(column):
    rows = column.shape[0]
    eye = iota((rows, rows), 0) == iota((rows, rows), 1)
    return jnp.sum(jnp.where(eye, column, 0.0), axis=0, keepdims=True)


def upright(line):
    rows = line.shape[1]
    eye = iota((rows, rows), 0) == iota((rows, rows), 1)
    return jnp.sum(jnp.where(eye, line, 0.0), axis=1, keepdims=True)


def eye_of(size):
    return (iota((size, size), 0) == iota((size, size), 1)).astype(BF16)


def plane():
    return lax.axis_index("seq") // 2


def twin_load(wq, wk, wq_v, wk_v, sems):
    chunks = sems.shape[1]
    depth = wq.shape[0] // chunks
    copies = []
    for at, (source, target) in enumerate(((wq, wq_v), (wk, wk_v))):
        for c in range(chunks):
            rows = pl.ds(c * depth, depth)
            copies.append(
                pltpu.make_async_copy(source.at[rows], target.at[rows], sems.at[at, c])
            )
    for copy in copies:
        copy.start()
    for copy in copies:
        copy.wait()


def twin_project_qk(hidden, wq, wk, query_raw, key_raw, squares):
    rows = hidden[...]
    own = rows.shape[0]
    for at, (weight, raw) in enumerate(((wq, query_raw), (wk, key_raw))):
        product = dot(rows, weight[...])
        raw[...] = product
        line = across(sum_squares(product))
        line = jnp.concatenate([line, jnp.zeros((1, LANES - own), F32)], axis=1)
        squares[:, at * LANES : (at + 1) * LANES] = jnp.broadcast_to(
            line, (squares.shape[0], LANES)
        )


def twin_project_v(hidden, wv, value):
    value[...] = dot(hidden[...], wv[...]).astype(BF16)


def twin_tree(
    turns, lengths, leaves, parents, freqs, own_tree, targets, cosine, sine, limits, held
):
    requests, draft = parents.shape
    own = own_tree.shape[1]
    row, col = iota((draft, draft), 0), iota((draft, draft), 1)
    eye = eye_of(draft)

    def length_of(request):
        picked = iota(lengths.shape, 1) == request
        return jnp.sum(jnp.where(picked, lengths[...], 0), axis=1, keepdims=True)

    for at, turn in enumerate(turns):
        limits[at : at + 1, :] = jnp.broadcast_to(
            length_of(plane() ^ turn), (1, limits.shape[1])
        )
    trees = [
        jnp.where((parents[pl.ds(r, 1), :] == row) | (row == col), 1.0, 0.0).astype(BF16)
        for r in range(requests)
    ]
    for _ in range(max(1, (draft - 1).bit_length())):
        trees = [jnp.minimum(dot(tree, tree), 1.0).astype(BF16) for tree in trees]
    for r in range(requests):
        standing = lax.dot_general(
            trees[r], eye, (((0,), (0,)), ((), ())), preferred_element_type=F32
        )
        held[r] = standing
        level = jnp.sum(trees[r].astype(F32), axis=0, keepdims=True) - 1.0
        on_path = jnp.where(row == leaves[:, r : r + 1], standing, 0.0)
        on_path = jnp.sum(on_path, axis=0, keepdims=True)
        place = lengths[:, r : r + 1] + level.astype(jnp.int32)
        targets[r] = jnp.where(on_path > 0.5, place, -1)
    within = lax.rem(lax.axis_index("seq"), 2)
    for at in range(2):
        first = (within ^ at) * own
        rows = held[plane(), pl.ds(pl.multiple_of(first, own), own), :]
        own_tree[at * own : (at + 1) * own, :] = jnp.where(
            within == 0, rows[:, :own], rows[:, own:]
        )
        mine = rows if at == 0 else mine
    level = jnp.sum(mine, axis=1, keepdims=True) - 1.0
    angles = (length_of(plane()).astype(F32) + level) * freqs[...]
    cosine[...] = jnp.cos(angles)
    half = jnp.sin(angles)
    sine[...] = jnp.where(iota(half.shape, 1) < HEAD_DIM // 2, -half, half)


def turned(raw, scale, gain, cos, sin):
    x = raw * scale * gain
    return (x * cos + pltpu.roll(x, HEAD_DIM // 2, 1) * sin).astype(BF16)


def twin_prepare(width_all, query_raw, key_raw, value, q_gain, k_gain, cosine, sine, *refs):
    squares, (queries, packed) = refs[:-2], refs[-2:]
    own, width = query_raw.shape
    cos, sin = cosine[...], sine[...]
    total = sum(ref[:1, :] for ref in squares)
    for at, (raw, gain) in enumerate(((query_raw, q_gain), (key_raw, k_gain))):
        scale = upright(total[:, at * LANES : at * LANES + own])
        scale = lax.rsqrt(scale / width_all + EPS)
        for h in range(width // HEAD_DIM):
            lanes = slice(h * HEAD_DIM, (h + 1) * HEAD_DIM)
            there = slice(at * width + h * HEAD_DIM, at * width + (h + 1) * HEAD_DIM)
            found = turned(raw[:, lanes], scale, gain[:, lanes], cos, sin)
            packed[:, there] = found
            if at == 0:
                queries[:, lanes] = found
    packed[:, 2 * width :] = value[...]


def weigh(s, visible):
    peak = jnp.max(s, axis=1, keepdims=True).astype(BF16).astype(F32)
    weights = jnp.exp(jnp.where(visible, s - peak, NEG))
    total = jnp.sum(weights, axis=1, keepdims=True)
    high = total.astype(BF16).astype(F32)
    return weights.astype(BF16), (peak, high, total - high)


def kept(stats, h, heads, found):
    lane = iota(stats.shape, 1)
    for at, column in enumerate(found):
        stats = jnp.where(lane == at * heads + h, column, stats)
    return stats


def write_stats(stats, out):
    own, width = stats.shape[0], out.shape[1]
    flat = lax.dot_general(
        stats.astype(BF16), eye_of(own), (((0,), (0,)), ((), ())), preferred_element_type=F32
    )
    flat = jnp.concatenate([flat[:16], jnp.zeros((16, width - own), F32)], axis=1)
    out[own : own + 16, :] = flat.astype(BF16)


def twin_attend(far, limits, key_cache, value_cache, swapped, own_tree, mine, other, *refs):
    count = len(far)
    queries, outs = refs[:count], refs[count : 2 * count]
    crossing, local, copied, scores, own_scores = refs[2 * count :]
    block, width = key_cache.shape[1:]
    heads = width // HEAD_DIM
    own = other.shape[0]
    me = lax.axis_index("seq")
    factor = 1.0 / math.sqrt(HEAD_DIM)
    place = iota((1, block), 1)
    both = jnp.concatenate([me * block + place, (me ^ 1) * block + place], axis=1)
    visible = [both < limits[at + 1 : at + 2, :] for at in range(count)]
    here = jnp.broadcast_to((me * block + place) < limits[:1, :block], (2 * own, block))
    near = jnp.concatenate(
        [
            jnp.where(here, 1.0, 0.0),
            own_tree[...],
            jnp.zeros((2 * own, own_scores.shape[2] - block - own), F32),
        ],
        axis=1,
    )
    near = near > 0.5
    for at, turn in enumerate(far):
        for h in range(heads):
            lanes = slice(h * HEAD_DIM, (h + 1) * HEAD_DIM)
            q = queries[at][:, lanes]
            first = dot_t(q, key_cache[plane() ^ turn, :, lanes])
            second = dot_t(q, swapped[at, 0, :, lanes])
            product = jnp.concatenate([first, second], axis=1) * factor
            scores[at, h] = jnp.where(visible[at], product, NEG)
    pair = stacked([mine[:, :width], other[...]])
    rest = own_scores.shape[2] - block - own
    for h in range(heads):
        lanes = slice(h * HEAD_DIM, (h + 1) * HEAD_DIM)
        keys = jnp.concatenate(
            [mine[:, width + h * HEAD_DIM : width + (h + 1) * HEAD_DIM]] * (1 + rest // own), axis=0
        )
        first = dot_t(pair[:, lanes], key_cache[plane(), :, lanes])
        product = jnp.concatenate([first, dot_t(pair[:, lanes], keys)], axis=1) * factor
        own_scores[h] = jnp.where(near, product, NEG)
    for at, turn in enumerate(far):
        stats = jnp.zeros((own, LANES), F32)
        for h in range(heads):
            lanes = slice(h * HEAD_DIM, (h + 1) * HEAD_DIM)
            weights, found = weigh(scores[at, h], visible[at])
            out = dot(weights[:, :block], value_cache[plane() ^ turn, :, lanes])
            out = out + dot(weights[:, block:], swapped[at, 1, :, lanes])
            outs[at][:own, lanes] = out.astype(BF16)
            stats = kept(stats, h, heads, found)
        write_stats(stats, outs[at])
    stats = jnp.zeros((2 * own, LANES), F32)
    for h in range(heads):
        lanes = slice(h * HEAD_DIM, (h + 1) * HEAD_DIM)
        weights, found = weigh(own_scores[h], near)
        out = dot(weights[:, :block], value_cache[plane(), :, lanes])
        values = mine[:, 2 * width + h * HEAD_DIM : 2 * width + (h + 1) * HEAD_DIM]
        out = out + dot(weights[:, block : block + own], values)
        out = out.astype(BF16)
        local[:own, lanes] = out[:own]
        crossing[:own, lanes] = out[own:]
        stats = kept(stats, h, heads, found)
    write_stats(stats[:own], local)
    write_stats(stats[own:], crossing)
    for at, ref in enumerate((mine, *queries)):
        for part in range(2):
            rows = slice((2 * at + part) * own, (2 * at + part + 1) * own)
            copied[rows, :] = ref[:, (part + 1) * width : (part + 2) * width]
    rest = copied.shape[0] - 2 * (count + 1) * own
    copied[2 * (count + 1) * own :, :] = jnp.zeros((rest, width), BF16)


def twin_rows(mine, theirs, held):
    within = lax.rem(lax.axis_index("seq"), 2)
    held[within] = mine
    held[1 - within] = theirs
    return stacked([held[0], held[1]])


def twin_merge_and_project(*refs):
    partials, (wo, total_out, rounded) = refs[:-3], refs[-3:]
    own, width = total_out.shape[0], partials[0].shape[1]
    heads = width // HEAD_DIM
    stats = [dot_t(eye_of(own), ref[own : own + 16, :own]) for ref in partials]
    attention = []
    for h in range(heads):
        lanes = slice(h * HEAD_DIM, (h + 1) * HEAD_DIM)
        peaks = [s[:, h : h + 1] for s in stats]
        highest = functools.reduce(jnp.maximum, peaks)
        total, summed = 0.0, 0.0
        for ref, s, peak in zip(partials, stats, peaks):
            scale = jnp.exp(peak - highest)
            own_total = s[:, heads + h : heads + h + 1] + s[:, 2 * heads + h : 2 * heads + h + 1]
            total = total + own_total * scale
            summed = summed + ref[:own, lanes].astype(F32) * scale
        attention.append((summed / total).astype(BF16))
    product = dot(jnp.concatenate(attention, axis=1), wo[...])
    total_out[...] = product
    rounded[...] = product.astype(BF16)


def twin_add(mine, theirs, total, rounded):
    both = mine[...] + theirs[...].astype(F32)
    total[...] = both
    rounded[...] = both.astype(BF16)


def twin_finish(mine, theirs, gain, hidden, out):
    model_width = mine.shape[1]
    columns = out.shape[1]
    total = mine[...] + theirs[...].astype(F32)
    scale = lax.rsqrt(sum_squares(total) / model_width + EPS)
    lanes = pl.ds(pl.multiple_of(lax.axis_index("tp") * columns, columns), columns)
    normed = (mine[:, lanes] + theirs[:, lanes].astype(F32)) * scale * gain[...]
    out[...] = (hidden[:, lanes].astype(F32) + normed).astype(BF16)


def twin_compact(far, targets, key_cache, value_cache, *refs):
    count = len(far) + 1
    ours, (copied, new_keys, new_values, held) = refs[:count], refs[count:]
    block, width = key_cache.shape[1:]
    own = ours[0].shape[0]
    me = lax.axis_index("seq")
    place = me * block + iota((block, targets.shape[2]), 0)
    for at, turn in enumerate((0, *far)):
        request = plane() ^ turn
        placing = place == targets[request]
        written = jnp.max(placing.astype(F32), axis=1, keepdims=True) > 0.5
        placing = placing.astype(BF16)
        for part, (cache, out) in enumerate(((key_cache, new_keys), (value_cache, new_values))):
            lanes = slice((part + 1) * width, (part + 2) * width)
            rows = slice((2 * at + part) * own, (2 * at + part + 1) * own)
            theirs = copied[rows, :]
            fresh = twin_rows(ours[at][:, lanes], theirs, held.at[at, part])
            moved = dot(placing, fresh)
            out[request] = jnp.where(written, moved, cache[request].astype(F32)).astype(BF16)


def body_twin(
    hidden_in,
    query_weight,
    key_weight,
    value_weight,
    out_weight,
    query_gain,
    key_gain,
    post_gain,
    key_cache,
    value_cache,
    cache_lengths,
    parents,
    accepted_leaf,
):
    requests, block, width = key_cache.shape
    draft = parents.shape[1]
    own, model = hidden_in.shape
    tp = lax.axis_size("tp")
    seq = lax.axis_size("seq")
    columns = model // tp
    heads = width // HEAD_DIM
    far = tuple(range(requests - 1, 0, -1))

    def call(kernel, outs, inputs, scratch=(), mib=16, specs=None, ties=()):
        count = len(inputs)

        def run(*refs):
            kernel(*refs[:count], *refs[count + len(ties) :])

        return pl.pallas_call(
            run,
            out_shape=outs,
            in_specs=([VMEM] * count if specs is None else specs) + [ANY] * len(ties),
            out_specs=jax.tree.map(lambda _: VMEM, outs),
            scratch_shapes=list(scratch),
            compiler_params=params(mib),
            name=getattr(kernel, "func", kernel).__name__,
        )(*inputs, *ties)

    def over_tp(x, k):
        return lax.ppermute(x, "tp", [(i, i ^ k) for i in range(tp)])

    def beside(x):
        return lax.ppermute(x, "seq", [(i, i ^ 1) for i in range(seq)])

    def over_planes(x, turn):
        return lax.ppermute(x, "seq", [(i, (i // 2 ^ turn) * 2 + i % 2) for i in range(seq)])

    me = lax.axis_index("seq") // 2
    picked = jnp.stack(
        [
            jnp.stack([lax.dynamic_index_in_dim(x, me ^ turn, 0, False) for x in (key_cache, value_cache)])
            for turn in far
        ]
    )
    swapped = beside(picked)
    wq, wk = call(
        twin_load,
        (shaped(query_weight.shape, BF16), shaped(key_weight.shape, BF16)),
        (query_weight, key_weight),
        [pltpu.SemaphoreType.DMA((2, 4))],
        mib=48,
        specs=[ANY] * 2,
    )
    query_raw, key_raw, squares = call(
        twin_project_qk,
        (shaped((own, width), F32), shaped((own, width), F32), shaped((8, 2 * LANES), F32)),
        (hidden_in, wq, wk),
    )
    all_squares = [squares] + [over_tp(squares, k) for k in range(tp - 1, 0, -1)]

    exponents = -2.0 * (jnp.arange(HEAD_DIM) % (HEAD_DIM // 2)).astype(F32) / HEAD_DIM
    freqs = (THETA**exponents)[None, :]
    own_tree, targets, cosine, sine, limits = call(
        functools.partial(twin_tree, (0, *far)),
        (
            shaped((draft, own), F32),
            shaped((requests, 1, draft), jnp.int32),
            shaped((own, HEAD_DIM), F32),
            shaped((own, HEAD_DIM), F32),
            shaped((requests, 2 * block), jnp.int32),
        ),
        (cache_lengths[None, :], accepted_leaf[None, :], parents, freqs),
        [pltpu.VMEM((requests, draft, draft), F32)],
    )
    value = call(twin_project_v, shaped((own, width), BF16), (hidden_in, value_weight))
    queries, packed = call(
        functools.partial(twin_prepare, tp * width),
        (shaped((own, width), BF16), shaped((own, 3 * width), BF16)),
        (
            query_raw,
            key_raw,
            value,
            query_gain[None, :],
            key_gain[None, :],
            cosine,
            sine,
            *all_squares,
        ),
    )
    from_far = [over_planes(packed, turn) for turn in far]
    other = beside(queries)

    rows = own + 16
    *partials, crossing, local, copied = call(
        functools.partial(twin_attend, far),
        (shaped((rows, width), BF16),) * (len(far) + 2)
        + (shaped((2 * requests * own + own, width), BF16),),
        (limits, key_cache, value_cache, swapped, own_tree, packed, other, *from_far),
        [
            pltpu.VMEM((len(far), heads, own, 2 * block), F32),
            pltpu.VMEM((heads, 2 * own, block + LANES), F32),
        ],
    )
    partials = [over_planes(part, turn) for part, turn in zip(partials, far)]
    partials += [beside(crossing)]
    partials = [partials[2], partials[3], partials[0], partials[1], local]

    total, rounded = call(
        twin_merge_and_project,
        (shaped((own, model), F32), shaped((own, model), BF16)),
        (*partials, out_weight),
    )
    copied = beside(copied)
    bit = 1
    while 2 * bit < tp:
        total, rounded = call(
            twin_add,
            (shaped((own, model), F32), shaped((own, model), BF16)),
            (total, over_tp(rounded, bit)),
        )
        bit *= 2
    arrived = over_tp(rounded, bit)
    new_key_cache, new_value_cache = call(
        functools.partial(twin_compact, far),
        (shaped(key_cache.shape, BF16), shaped(value_cache.shape, BF16)),
        (targets, key_cache, value_cache, packed, *from_far, copied),
        [pltpu.VMEM((requests, 2, 2, own, width), BF16)],
    )
    hidden_out = call(
        twin_finish,
        shaped((own, columns), BF16),
        (total, arrived, post_gain[None, :], hidden_in),
    )
    return (hidden_out, new_key_cache, new_value_cache)


def body(*args):
    hidden_in, key_cache, parents = args[0], args[8], args[11]
    tp = lax.axis_size("tp")
    own, draft = hidden_in.shape[0], parents.shape[1]
    requests, _, width = key_cache.shape
    twin = (
        own % 16 == 0
        and draft == 2 * own
        and requests == 4
        and lax.axis_size("seq") == 2 * requests
        and own <= LANES
        and LANES % own == 0
        and own <= width
        and 3 * (width // HEAD_DIM) <= 16
        and tp > 1
        and tp & (tp - 1) == 0
    )
    return (body_twin if twin else body_general)(*args)


def solution(mesh):
    return jax.shard_map(
        body,
        mesh=mesh,
        in_specs=(
            P("seq", None),
            P(None, "tp"),
            P(None, "tp"),
            P(None, "tp"),
            P("tp", None),
            P("tp"),
            P("tp"),
            P("tp"),
            P(None, "seq", "tp"),
            P(None, "seq", "tp"),
            P(),
            P(),
            P(),
        ),
        out_specs=(P("seq", "tp"), P(None, "seq", "tp"), P(None, "seq", "tp")),
        check_vma=False,
    )
```

```python
import functools
import math

import jax
import jax.numpy as jnp
from jax import lax
from jax.experimental import pallas as pl
from jax.experimental.pallas import tpu as pltpu
from jax.sharding import PartitionSpec as P

HEAD_DIM = 128
LANES = 128
EPS = 1e-06
THETA = 500000.0
NEG = -1e30
F32 = jnp.float32
BF16 = jnp.bfloat16
VMEM = pl.BlockSpec(memory_space=pltpu.VMEM)
SMEM = pl.BlockSpec(memory_space=pltpu.SMEM)
ANY = pl.BlockSpec(memory_space=pl.ANY)


def params(mib):
    return pltpu.CompilerParams(vmem_limit_bytes=mib * 1024 * 1024)


def dot(a, b):
    return jnp.dot(a, b, preferred_element_type=F32)


def dot_t(a, b):
    return lax.dot_general(a, b, (((1,), (1,)), ((), ())), preferred_element_type=F32)


def iota(shape, axis):
    return lax.broadcasted_iota(jnp.int32, shape, axis)


def stacked(parts):
    if len(parts) == 1:
        return parts[0]
    if parts[0].shape[0] % 16 == 0:
        return jnp.concatenate(parts, axis=0)
    return jnp.concatenate([part.astype(F32) for part in parts], axis=0).astype(BF16)


def sum_squares(raw):
    return jnp.sum(raw * raw, axis=1, keepdims=True)


def project_qk(hidden, wq, wk, query_raw, key_raw, squares, wq_v, wk_v, sems):
    chunks, depth = wq_v.shape[0], wq_v.shape[1]
    copies = []
    for c in range(chunks):
        for at, (source, target) in enumerate(((wq, wq_v), (wk, wk_v))):
            copy = pltpu.make_async_copy(
                source.at[pl.ds(c * depth, depth)], target.at[c], sems.at[2 * c + at]
            )
            copy.start()
            copies.append(copy)
    q_sum, k_sum = None, None
    for c in range(chunks):
        part = hidden[:, c * depth : (c + 1) * depth]
        copies[2 * c].wait()
        q = dot(part, wq_v[c])
        copies[2 * c + 1].wait()
        k = dot(part, wk_v[c])
        q_sum = q if c == 0 else q_sum + q
        k_sum = k if c == 0 else k_sum + k
    query_raw[...] = q_sum
    key_raw[...] = k_sum
    lane = iota(squares.shape[1:], 1)
    both = jnp.where(lane == 0, sum_squares(q_sum), sum_squares(k_sum))
    for t in range(squares.shape[0]):
        squares[t] = both


def project_v_and_tree(
    lengths, leaves, hidden, parents, freqs, wv, value, own_tree, targets, cosine, sine, wv_v, anc_v, sems
):
    chunks, depth = wv_v.shape[0], wv_v.shape[1]
    copies = []
    for c in range(chunks):
        copy = pltpu.make_async_copy(wv.at[pl.ds(c * depth, depth)], wv_v.at[c], sems.at[c])
        copy.start()
        copies.append(copy)
    requests, draft = parents.shape
    own = hidden.shape[0]
    first = lax.axis_index("seq") * own
    row, col = iota((draft, draft), 0), iota((draft, draft), 1)
    eye = (row == col).astype(BF16)
    trees = [
        jnp.where((parents[pl.ds(r, 1), :] == row) | (row == col), 1.0, 0.0).astype(BF16)
        for r in range(requests)
    ]
    for _ in range(max(1, (draft - 1).bit_length())):
        trees = [jnp.minimum(dot(tree, tree), 1.0).astype(BF16) for tree in trees]
    for r in range(requests):
        upright = lax.dot_general(
            trees[r], eye, (((0,), (0,)), ((), ())), preferred_element_type=F32
        )
        anc_v[pl.ds(r * draft, draft), :] = upright
        level = jnp.sum(trees[r].astype(F32), axis=0, keepdims=True) - 1.0
        on_path = jnp.sum(jnp.where(row == leaves[r], upright, 0.0), axis=0, keepdims=True)
        place = lengths[r] + level.astype(jnp.int32)
        targets[r] = jnp.where(on_path > 0.5, place, -1)
    mine = anc_v[pl.ds(pl.multiple_of(first, own), own), :]
    own_tree[...] = mine
    level = jnp.sum(mine, axis=1, keepdims=True) - 1.0
    position = lengths[first // draft].astype(F32) + level
    angles = position * freqs[...]
    cosine[...] = jnp.cos(angles)
    half = jnp.sin(angles)
    sine[...] = jnp.where(iota(half.shape, 1) < HEAD_DIM // 2, -half, half)
    total = None
    for c in range(chunks):
        copies[c].wait()
        v = dot(hidden[:, c * depth : (c + 1) * depth], wv_v[c])
        total = v if c == 0 else total + v
    value[...] = total.astype(BF16)


def prepare(
    width_all, query_raw, key_raw, value, q_gain, k_gain, cosine, sine, squares, queries, keys_values
):
    width = query_raw.shape[1]
    total = sum(squares[k] for k in range(squares.shape[0]))
    cos, sin = cosine[...], sine[...]
    for at, (raw, gain, out) in enumerate(
        ((query_raw, q_gain, queries), (key_raw, k_gain, keys_values))
    ):
        scale = lax.rsqrt(total[:, at : at + 1] / width_all + EPS)
        for h in range(width // HEAD_DIM):
            lanes = slice(h * HEAD_DIM, (h + 1) * HEAD_DIM)
            x = raw[:, lanes] * scale * gain[:, lanes]
            turned = x * cos + pltpu.roll(x, HEAD_DIM // 2, 1) * sin
            turned = turned.astype(BF16)
            for s in range(out.shape[0]):
                out[s, :, lanes] = turned
    for s in range(keys_values.shape[0]):
        keys_values[s, :, width:] = value[...]


def attend_cache(group, lengths, key_cache, value_cache, queries, partials):
    requests, block, width = key_cache.shape
    own = queries.shape[1]
    heads = width // HEAD_DIM
    me = lax.axis_index("seq")
    factor = 1.0 / math.sqrt(HEAD_DIM)
    rows = group * own
    place = me * block + iota((rows, block), 1)
    lane = iota((rows, LANES), 1)
    for request in range(requests):
        q = stacked([queries[request * group + j] for j in range(group)])
        visible = place < lengths[request]
        stats = jnp.zeros((rows, LANES), F32)
        for h in range(heads):
            lanes = slice(h * HEAD_DIM, (h + 1) * HEAD_DIM)
            scores = dot_t(q[:, lanes], key_cache[request, :, lanes]) * factor
            scores = jnp.where(visible, scores, NEG)
            peak = jnp.max(scores, axis=1, keepdims=True).astype(BF16).astype(F32)
            weights = jnp.exp(jnp.where(visible, scores - peak, NEG))
            total = jnp.sum(weights, axis=1, keepdims=True)
            high = total.astype(BF16).astype(F32)
            out = dot(weights.astype(BF16), value_cache[request, :, lanes]).astype(BF16)
            for j in range(group):
                partials[request * group + j, :, lanes] = out[j * own : (j + 1) * own]
            stats = jnp.where(lane == h, peak, stats)
            stats = jnp.where(lane == heads + h, high, stats)
            stats = jnp.where(lane == 2 * heads + h, total - high, stats)
        stats = stats.astype(BF16)
        for j in range(group):
            partials[request * group + j, :, width:] = stats[j * own : (j + 1) * own]


def attend_draft(group, own_tree, queries, keys_values, out, stats):
    own, width = queries.shape[1:]
    heads = width // HEAD_DIM
    me = lax.axis_index("seq")
    first = me // group * group
    q = queries[me]
    pair = stacked([keys_values[first + j] for j in range(group)])
    factor = 1.0 / math.sqrt(HEAD_DIM)
    allowed = own_tree[...] > 0.5
    lane = iota((own, LANES), 1)
    kept = jnp.zeros((own, LANES), F32)
    for h in range(heads):
        lanes = slice(h * HEAD_DIM, (h + 1) * HEAD_DIM)
        there = slice(width + h * HEAD_DIM, width + (h + 1) * HEAD_DIM)
        scores = dot_t(q[:, lanes], pair[:, lanes]) * factor
        scores = jnp.where(allowed, scores, NEG)
        peak = jnp.max(scores, axis=1, keepdims=True)
        weights = jnp.exp(jnp.where(allowed, scores - peak, NEG))
        out[:, lanes] = dot(weights.astype(BF16), pair[:, there])
        kept = jnp.where(lane == h, peak, kept)
        kept = jnp.where(lane == heads + h, jnp.sum(weights, axis=1, keepdims=True), kept)
    stats[...] = kept


def merge_and_project(draft_out, draft_stats, wo, partials, projected, wo_v, sems):
    count, width, columns = wo_v.shape
    heads = width // HEAD_DIM
    copies = []
    for k in range(count):
        copy = pltpu.make_async_copy(
            wo.at[:, pl.ds(k * columns, columns)], wo_v.at[k], sems.at[k]
        )
        copy.start()
        copies.append(copy)
    parts = range(partials.shape[0])
    stats = [partials[s, :, width:].astype(F32) for s in parts]
    own_stats = draft_stats[...]
    attention = []
    for h in range(heads):
        lanes = slice(h * HEAD_DIM, (h + 1) * HEAD_DIM)
        peaks = [s[:, h : h + 1] for s in stats] + [own_stats[:, h : h + 1]]
        highest = functools.reduce(jnp.maximum, peaks)
        scales = [jnp.exp(peak - highest) for peak in peaks]
        total = own_stats[:, heads + h : heads + h + 1] * scales[-1]
        summed = draft_out[:, lanes] * scales[-1]
        for at in parts:
            s = stats[at]
            own_total = s[:, heads + h : heads + h + 1] + s[:, 2 * heads + h : 2 * heads + h + 1]
            total = total + own_total * scales[at]
            summed = summed + partials[at, :, lanes].astype(F32) * scales[at]
        attention.append((summed / total).astype(BF16))
    attention = jnp.concatenate(attention, axis=1)
    for k in range(count):
        copies[k].wait()
        projected[k] = dot(attention, wo_v[k]).astype(projected.dtype)


def add_up(parts, summed, power):
    total = sum(parts[k].astype(F32) for k in range(parts.shape[0]))
    summed[...] = total
    own_power = jnp.broadcast_to(sum_squares(total), power.shape[1:])
    for k in range(power.shape[0]):
        power[k] = own_power


def finish(model_width, summed, gain, hidden, powers, out):
    columns = summed.shape[1]
    power = sum(powers[k] for k in range(powers.shape[0]))[:, :1]
    start = pl.multiple_of(lax.axis_index("tp") * columns, columns)
    normed = summed[...] * lax.rsqrt(power / model_width + EPS) * gain[...]
    out[...] = (hidden[:, pl.ds(start, columns)].astype(F32) + normed).astype(BF16)


def compact(group, targets, key_cache, value_cache, keys_values, new_keys, new_values):
    requests, block, width = key_cache.shape
    own = keys_values.shape[1]
    me = lax.axis_index("seq")
    place = me * block + iota((block, group * own), 0)
    for request in range(requests):
        kv = stacked([keys_values[request * group + j] for j in range(group)])
        placing = place == targets[request]
        written = jnp.max(placing.astype(F32), axis=1, keepdims=True) > 0.5
        fresh = dot(placing.astype(BF16), kv)
        new_keys[request] = jnp.where(
            written, fresh[:, :width], key_cache[request].astype(F32)
        ).astype(BF16)
        new_values[request] = jnp.where(
            written, fresh[:, width:], value_cache[request].astype(F32)
        ).astype(BF16)


def shaped(shape, dtype):
    return jax.ShapeDtypeStruct(shape, dtype)


def body_general(
    hidden_in,
    query_weight,
    key_weight,
    value_weight,
    out_weight,
    query_gain,
    key_gain,
    post_gain,
    key_cache,
    value_cache,
    cache_lengths,
    parents,
    accepted_leaf,
):
    requests, block, width = key_cache.shape
    draft = parents.shape[1]
    own, model = hidden_in.shape
    tp = lax.axis_size("tp")
    seq = lax.axis_size("seq")
    group = draft // own
    columns = model // tp
    chunks = 4
    depth = model // chunks

    def exchange(x, axis):
        return lax.all_to_all(x, axis, 0, 0, tiled=True)

    query_raw, key_raw, squares = pl.pallas_call(
        project_qk,
        out_shape=(
            shaped((own, width), F32),
            shaped((own, width), F32),
            shaped((tp, own, LANES), F32),
        ),
        in_specs=[VMEM, ANY, ANY],
        out_specs=(VMEM, VMEM, VMEM),
        scratch_shapes=[
            pltpu.VMEM((chunks, depth, width), BF16),
            pltpu.VMEM((chunks, depth, width), BF16),
            pltpu.SemaphoreType.DMA((2 * chunks,)),
        ],
        compiler_params=params(56),
        cost_estimate=pl.CostEstimate(
            flops=4 * own * model * width, bytes_accessed=4 * model * width, transcendentals=0
        ),
        name="project_qk",
    )(hidden_in, query_weight, key_weight)
    squares = exchange(squares, "tp")

    exponents = -2.0 * (jnp.arange(HEAD_DIM) % (HEAD_DIM // 2)).astype(F32) / HEAD_DIM
    freqs = (THETA**exponents)[None, :]
    value, own_tree, targets, cosine, sine = pl.pallas_call(
        project_v_and_tree,
        out_shape=(
            shaped((own, width), BF16),
            shaped((own, draft), F32),
            shaped((requests, 1, draft), jnp.int32),
            shaped((own, HEAD_DIM), F32),
            shaped((own, HEAD_DIM), F32),
        ),
        in_specs=[SMEM, SMEM, VMEM, VMEM, VMEM, ANY],
        out_specs=(VMEM,) * 5,
        scratch_shapes=[
            pltpu.VMEM((chunks, depth, width), BF16),
            pltpu.VMEM((requests * draft, draft), F32),
            pltpu.SemaphoreType.DMA((chunks,)),
        ],
        compiler_params=params(16),
        cost_estimate=pl.CostEstimate(
            flops=2 * own * model * width, bytes_accessed=2 * model * width, transcendentals=0
        ),
        name="project_v_and_tree",
    )(cache_lengths, accepted_leaf, hidden_in, parents, freqs, value_weight)

    queries, keys_values = pl.pallas_call(
        functools.partial(prepare, tp * width),
        out_shape=(shaped((seq, own, width), BF16), shaped((seq, own, 2 * width), BF16)),
        in_specs=[VMEM] * 8,
        out_specs=(VMEM, VMEM),
        compiler_params=params(16),
        name="prepare",
    )(
        query_raw,
        key_raw,
        value,
        query_gain[None, :],
        key_gain[None, :],
        cosine,
        sine,
        squares,
    )
    queries = exchange(queries, "seq")
    keys_values = exchange(keys_values, "seq")

    partials = pl.pallas_call(
        functools.partial(attend_cache, group),
        out_shape=shaped((seq, own, width + LANES), BF16),
        in_specs=[SMEM, VMEM, VMEM, VMEM],
        out_specs=VMEM,
        compiler_params=params(16),
        name="attend_cache",
    )(cache_lengths, key_cache, value_cache, queries)
    partials = exchange(partials, "seq")

    draft_out, draft_stats = pl.pallas_call(
        functools.partial(attend_draft, group),
        out_shape=(shaped((own, width), F32), shaped((own, LANES), F32)),
        in_specs=[VMEM] * 3,
        out_specs=(VMEM, VMEM),
        compiler_params=params(16),
        name="attend_draft",
    )(own_tree, queries, keys_values)

    projected = pl.pallas_call(
        merge_and_project,
        out_shape=shaped((tp, own, columns), BF16),
        in_specs=[VMEM, VMEM, ANY, VMEM],
        out_specs=VMEM,
        scratch_shapes=[
            pltpu.VMEM((tp, width, columns), BF16),
            pltpu.SemaphoreType.DMA((tp,)),
        ],
        compiler_params=params(16),
        name="merge_and_project",
    )(draft_out, draft_stats, out_weight, partials)
    projected = exchange(projected, "tp")

    summed, power = pl.pallas_call(
        add_up,
        out_shape=(shaped((own, columns), F32), shaped((tp, own, LANES), F32)),
        in_specs=[VMEM],
        out_specs=(VMEM, VMEM),
        compiler_params=params(16),
        name="add_up",
    )(projected)
    power = exchange(power, "tp")

    hidden_out = pl.pallas_call(
        functools.partial(finish, model),
        out_shape=shaped((own, columns), BF16),
        in_specs=[VMEM] * 4,
        out_specs=VMEM,
        compiler_params=params(16),
        name="finish",
    )(summed, post_gain[None, :], hidden_in, power)

    new_key_cache, new_value_cache = pl.pallas_call(
        functools.partial(compact, group),
        out_shape=(shaped(key_cache.shape, BF16), shaped(value_cache.shape, BF16)),
        in_specs=[VMEM] * 4,
        out_specs=(VMEM, VMEM),
        compiler_params=params(24),
        name="compact",
    )(targets, key_cache, value_cache, keys_values)
    return (hidden_out, new_key_cache, new_value_cache)


def across(column):
    rows = column.shape[0]
    eye = iota((rows, rows), 0) == iota((rows, rows), 1)
    return jnp.sum(jnp.where(eye, column, 0.0), axis=0, keepdims=True)


def upright(line):
    rows = line.shape[1]
    eye = iota((rows, rows), 0) == iota((rows, rows), 1)
    return jnp.sum(jnp.where(eye, line, 0.0), axis=1, keepdims=True)


def eye_of(size):
    return (iota((size, size), 0) == iota((size, size), 1)).astype(BF16)


def plane():
    return lax.axis_index("seq") // 2


def twin_project_qk(hidden, wq, wk, query_raw, key_raw, squares):
    rows = hidden[...]
    own = rows.shape[0]
    for at, (weight, raw) in enumerate(((wq, query_raw), (wk, key_raw))):
        product = dot(rows, weight[...])
        raw[...] = product
        line = across(sum_squares(product))
        line = jnp.concatenate([line, jnp.zeros((1, LANES - own), F32)], axis=1)
        squares[:, at * LANES : (at + 1) * LANES] = jnp.broadcast_to(
            line, (squares.shape[0], LANES)
        )


def twin_project_v(hidden, wv, value):
    value[...] = dot(hidden[...], wv[...]).astype(BF16)


def twin_tree(
    turns, lengths, leaves, parents, freqs, own_tree, targets, cosine, sine, limits, held
):
    requests, draft = parents.shape
    own = own_tree.shape[1]
    row, col = iota((draft, draft), 0), iota((draft, draft), 1)
    eye = eye_of(draft)

    def length_of(request):
        picked = iota(lengths.shape, 1) == request
        return jnp.sum(jnp.where(picked, lengths[...], 0), axis=1, keepdims=True)

    for at, turn in enumerate(turns):
        limits[at : at + 1, :] = jnp.broadcast_to(
            length_of(plane() ^ turn), (1, limits.shape[1])
        )
    trees = [
        jnp.where((parents[pl.ds(r, 1), :] == row) | (row == col), 1.0, 0.0).astype(BF16)
        for r in range(requests)
    ]
    for _ in range(max(1, (draft - 1).bit_length())):
        trees = [jnp.minimum(dot(tree, tree), 1.0).astype(BF16) for tree in trees]
    for r in range(requests):
        standing = lax.dot_general(
            trees[r], eye, (((0,), (0,)), ((), ())), preferred_element_type=F32
        )
        held[r] = standing
        level = jnp.sum(trees[r].astype(F32), axis=0, keepdims=True) - 1.0
        on_path = jnp.where(row == leaves[:, r : r + 1], standing, 0.0)
        on_path = jnp.sum(on_path, axis=0, keepdims=True)
        place = lengths[:, r : r + 1] + level.astype(jnp.int32)
        targets[r] = jnp.where(on_path > 0.5, place, -1)
    within = lax.rem(lax.axis_index("seq"), 2)
    for at in range(2):
        first = (within ^ at) * own
        rows = held[plane(), pl.ds(pl.multiple_of(first, own), own), :]
        own_tree[at * own : (at + 1) * own, :] = jnp.where(
            within == 0, rows[:, :own], rows[:, own:]
        )
        mine = rows if at == 0 else mine
    level = jnp.sum(mine, axis=1, keepdims=True) - 1.0
    angles = (length_of(plane()).astype(F32) + level) * freqs[...]
    cosine[...] = jnp.cos(angles)
    half = jnp.sin(angles)
    sine[...] = jnp.where(iota(half.shape, 1) < HEAD_DIM // 2, -half, half)


def turned(raw, scale, gain, cos, sin):
    x = raw * scale * gain
    return (x * cos + pltpu.roll(x, HEAD_DIM // 2, 1) * sin).astype(BF16)


def twin_prepare(width_all, query_raw, key_raw, value, q_gain, k_gain, cosine, sine, *refs):
    squares, (queries, packed) = refs[:-2], refs[-2:]
    own, width = query_raw.shape
    cos, sin = cosine[...], sine[...]
    total = sum(ref[:1, :] for ref in squares)
    for at, (raw, gain) in enumerate(((query_raw, q_gain), (key_raw, k_gain))):
        scale = upright(total[:, at * LANES : at * LANES + own])
        scale = lax.rsqrt(scale / width_all + EPS)
        for h in range(width // HEAD_DIM):
            lanes = slice(h * HEAD_DIM, (h + 1) * HEAD_DIM)
            there = slice(at * width + h * HEAD_DIM, at * width + (h + 1) * HEAD_DIM)
            found = turned(raw[:, lanes], scale, gain[:, lanes], cos, sin)
            packed[:, there] = found
            if at == 0:
                queries[:, lanes] = found
    packed[:, 2 * width :] = value[...]


def weigh(s, visible):
    peak = jnp.max(s, axis=1, keepdims=True).astype(BF16).astype(F32)
    weights = jnp.exp(jnp.where(visible, s - peak, NEG))
    total = jnp.sum(weights, axis=1, keepdims=True)
    high = total.astype(BF16).astype(F32)
    return weights.astype(BF16), (peak, high, total - high)


def kept(stats, h, heads, found):
    lane = iota(stats.shape, 1)
    for at, column in enumerate(found):
        stats = jnp.where(lane == at * heads + h, column, stats)
    return stats


def write_stats(stats, out):
    own, width = stats.shape[0], out.shape[1]
    flat = lax.dot_general(
        stats.astype(BF16), eye_of(own), (((0,), (0,)), ((), ())), preferred_element_type=F32
    )
    flat = jnp.concatenate([flat[:16], jnp.zeros((16, width - own), F32)], axis=1)
    out[own : own + 16, :] = flat.astype(BF16)


def attend_planes(turns, row, limits, key_cache, value_cache, swapped, queries, outs, scores):
    block, width = key_cache.shape[1:]
    heads = width // HEAD_DIM
    own = queries[0].shape[0]
    me = lax.axis_index("seq")
    factor = 1.0 / math.sqrt(HEAD_DIM)
    place = iota((1, block), 1)
    both = jnp.concatenate([me * block + place, (me ^ 1) * block + place], axis=1)
    visible = [both < limits[row + at : row + at + 1, :] for at in range(len(turns))]
    for at, turn in enumerate(turns):
        for h in range(heads):
            lanes = slice(h * HEAD_DIM, (h + 1) * HEAD_DIM)
            q = queries[at][:, lanes]
            first = dot_t(q, key_cache[plane() ^ turn, :, lanes])
            second = dot_t(q, swapped[at, 0, :, lanes])
            product = jnp.concatenate([first, second], axis=1) * factor
            scores[at, h] = jnp.where(visible[at], product, NEG)
    for at, turn in enumerate(turns):
        stats = jnp.zeros((own, LANES), F32)
        for h in range(heads):
            lanes = slice(h * HEAD_DIM, (h + 1) * HEAD_DIM)
            weights, found = weigh(scores[at, h], visible[at])
            out = dot(weights[:, :block], value_cache[plane() ^ turn, :, lanes])
            out = out + dot(weights[:, block:], swapped[at, 1, :, lanes])
            outs[at][:own, lanes] = out.astype(BF16)
            stats = kept(stats, h, heads, found)
        write_stats(stats, outs[at])


def twin_attend_far(turns, limits, key_cache, value_cache, swapped, *refs):
    count = len(turns)
    queries, outs, scores = refs[:count], refs[count : 2 * count], refs[2 * count]
    attend_planes(turns, 1, limits, key_cache, value_cache, swapped, queries, outs, scores)


def twin_attend_near(
    turns, row, limits, key_cache, value_cache, swapped, own_tree, mine, other, *refs
):
    count = row - 1 + len(turns)
    queries, outs = refs[:count], refs[count : count + len(turns)]
    crossing, local, copied, scores, own_scores = refs[count + len(turns) :]
    attend_planes(
        turns, row, limits, key_cache, value_cache, swapped, queries[row - 1 :], outs, scores
    )
    block, width = key_cache.shape[1:]
    heads = width // HEAD_DIM
    own = other.shape[0]
    factor = 1.0 / math.sqrt(HEAD_DIM)
    place = lax.axis_index("seq") * block + iota((1, block), 1)
    here = jnp.broadcast_to(place < limits[:1, :block], (2 * own, block))
    rest = own_scores.shape[2] - block - own
    near = jnp.concatenate(
        [jnp.where(here, 1.0, 0.0), own_tree[...], jnp.zeros((2 * own, rest), F32)], axis=1
    )
    near = near > 0.5
    pair = stacked([mine[:, :width], other[...]])
    for h in range(heads):
        lanes = slice(h * HEAD_DIM, (h + 1) * HEAD_DIM)
        keys = jnp.concatenate(
            [mine[:, width + h * HEAD_DIM : width + (h + 1) * HEAD_DIM]] * (1 + rest // own), axis=0
        )
        first = dot_t(pair[:, lanes], key_cache[plane(), :, lanes])
        product = jnp.concatenate([first, dot_t(pair[:, lanes], keys)], axis=1) * factor
        own_scores[h] = jnp.where(near, product, NEG)
    stats = jnp.zeros((2 * own, LANES), F32)
    for h in range(heads):
        lanes = slice(h * HEAD_DIM, (h + 1) * HEAD_DIM)
        weights, found = weigh(own_scores[h], near)
        out = dot(weights[:, :block], value_cache[plane(), :, lanes])
        values = mine[:, 2 * width + h * HEAD_DIM : 2 * width + (h + 1) * HEAD_DIM]
        out = out + dot(weights[:, block : block + own], values)
        out = out.astype(BF16)
        local[:own, lanes] = out[:own]
        crossing[:own, lanes] = out[own:]
        stats = kept(stats, h, heads, found)
    write_stats(stats[:own], local)
    write_stats(stats[own:], crossing)
    for at, ref in enumerate((mine, *queries)):
        for part in range(2):
            rows = slice((2 * at + part) * own, (2 * at + part + 1) * own)
            copied[rows, :] = ref[:, (part + 1) * width : (part + 2) * width]
    last = 2 * (count + 1) * own
    copied[last:, :] = jnp.zeros((copied.shape[0] - last, width), BF16)


def twin_rows(mine, theirs, held):
    within = lax.rem(lax.axis_index("seq"), 2)
    held[within] = mine
    held[1 - within] = theirs
    return stacked([held[0], held[1]])


def twin_merge_and_project(*refs):
    partials, (wo, total_out, rounded) = refs[:-3], refs[-3:]
    own, width = total_out.shape[0], partials[0].shape[1]
    heads = width // HEAD_DIM
    stats = [dot_t(eye_of(own), ref[own : own + 16, :own]) for ref in partials]
    attention = []
    for h in range(heads):
        lanes = slice(h * HEAD_DIM, (h + 1) * HEAD_DIM)
        peaks = [s[:, h : h + 1] for s in stats]
        highest = functools.reduce(jnp.maximum, peaks)
        total, summed = 0.0, 0.0
        for ref, s, peak in zip(partials, stats, peaks):
            scale = jnp.exp(peak - highest)
            own_total = s[:, heads + h : heads + h + 1] + s[:, 2 * heads + h : 2 * heads + h + 1]
            total = total + own_total * scale
            summed = summed + ref[:own, lanes].astype(F32) * scale
        attention.append((summed / total).astype(BF16))
    product = dot(jnp.concatenate(attention, axis=1), wo[...])
    total_out[...] = product
    rounded[...] = product.astype(BF16)


def twin_add(mine, theirs, total, rounded):
    both = mine[...] + theirs[...].astype(F32)
    total[...] = both
    rounded[...] = both.astype(BF16)


def twin_finish(mine, theirs, gain, hidden, out):
    model_width = mine.shape[1]
    columns = out.shape[1]
    total = mine[...] + theirs[...].astype(F32)
    scale = lax.rsqrt(sum_squares(total) / model_width + EPS)
    lanes = pl.ds(pl.multiple_of(lax.axis_index("tp") * columns, columns), columns)
    normed = (mine[:, lanes] + theirs[:, lanes].astype(F32)) * scale * gain[...]
    out[...] = (hidden[:, lanes].astype(F32) + normed).astype(BF16)


def twin_compact(far, targets, key_cache, value_cache, *refs):
    count = len(far) + 1
    ours, (copied, new_keys, new_values, held) = refs[:count], refs[count:]
    block, width = key_cache.shape[1:]
    own = ours[0].shape[0]
    me = lax.axis_index("seq")
    place = me * block + iota((block, targets.shape[2]), 0)
    for at, turn in enumerate((0, *far)):
        request = plane() ^ turn
        placing = place == targets[request]
        written = jnp.max(placing.astype(F32), axis=1, keepdims=True) > 0.5
        placing = placing.astype(BF16)
        for part, (cache, out) in enumerate(((key_cache, new_keys), (value_cache, new_values))):
            lanes = slice((part + 1) * width, (part + 2) * width)
            rows = slice((2 * at + part) * own, (2 * at + part + 1) * own)
            theirs = copied[rows, :]
            fresh = twin_rows(ours[at][:, lanes], theirs, held.at[at, part])
            moved = dot(placing, fresh)
            out[request] = jnp.where(written, moved, cache[request].astype(F32)).astype(BF16)


def body_twin(
    hidden_in,
    query_weight,
    key_weight,
    value_weight,
    out_weight,
    query_gain,
    key_gain,
    post_gain,
    key_cache,
    value_cache,
    cache_lengths,
    parents,
    accepted_leaf,
):
    requests, block, width = key_cache.shape
    draft = parents.shape[1]
    own, model = hidden_in.shape
    tp = lax.axis_size("tp")
    seq = lax.axis_size("seq")
    columns = model // tp
    heads = width // HEAD_DIM
    far = tuple(range(requests - 1, 0, -1))

    def call(kernel, outs, inputs, scratch=(), mib=16, specs=None, ties=()):
        count = len(inputs)

        def run(*refs):
            kernel(*refs[:count], *refs[count + len(ties) :])

        return pl.pallas_call(
            run,
            out_shape=outs,
            in_specs=([VMEM] * count if specs is None else specs) + [ANY] * len(ties),
            out_specs=jax.tree.map(lambda _: VMEM, outs),
            scratch_shapes=list(scratch),
            compiler_params=params(mib),
            name=getattr(kernel, "func", kernel).__name__,
        )(*inputs, *ties)

    def over_tp(x, k):
        return lax.ppermute(x, "tp", [(i, i ^ k) for i in range(tp)])

    def beside(x):
        return lax.ppermute(x, "seq", [(i, i ^ 1) for i in range(seq)])

    def over_planes(x, turn):
        return lax.ppermute(x, "seq", [(i, (i // 2 ^ turn) * 2 + i % 2) for i in range(seq)])

    me = lax.axis_index("seq") // 2

    def picked(turns):
        parts = [
            [lax.dynamic_index_in_dim(x, me ^ turn, 0, False) for x in (key_cache, value_cache)]
            for turn in turns
        ]
        return jnp.stack([jnp.stack(part) for part in parts])

    swapped, swapped_near = beside(picked(far[:2])), beside(picked(far[2:]))
    query_raw, key_raw, squares = call(
        twin_project_qk,
        (shaped((own, width), F32), shaped((own, width), F32), shaped((8, 2 * LANES), F32)),
        (hidden_in, query_weight, key_weight),
    )
    all_squares = [squares] + [over_tp(squares, k) for k in range(tp - 1, 0, -1)]

    exponents = -2.0 * (jnp.arange(HEAD_DIM) % (HEAD_DIM // 2)).astype(F32) / HEAD_DIM
    freqs = (THETA**exponents)[None, :]
    own_tree, targets, cosine, sine, limits = call(
        functools.partial(twin_tree, (0, *far)),
        (
            shaped((draft, own), F32),
            shaped((requests, 1, draft), jnp.int32),
            shaped((own, HEAD_DIM), F32),
            shaped((own, HEAD_DIM), F32),
            shaped((requests, 2 * block), jnp.int32),
        ),
        (cache_lengths[None, :], accepted_leaf[None, :], parents, freqs),
        [pltpu.VMEM((requests, draft, draft), F32)],
    )
    value = call(twin_project_v, shaped((own, width), BF16), (hidden_in, value_weight))
    queries, packed = call(
        functools.partial(twin_prepare, tp * width),
        (shaped((own, width), BF16), shaped((own, 3 * width), BF16)),
        (
            query_raw,
            key_raw,
            value,
            query_gain[None, :],
            key_gain[None, :],
            cosine,
            sine,
            *all_squares,
        ),
    )
    from_far = [over_planes(packed, turn) for turn in far]
    other = beside(queries)

    rows = own + 16
    partials = call(
        functools.partial(twin_attend_far, far[:2]),
        (shaped((rows, width), BF16),) * 2,
        (limits, key_cache, value_cache, swapped, *from_far[:2]),
        [pltpu.VMEM((2, heads, own, 2 * block), F32)],
    )
    near, crossing, local, copied = call(
        functools.partial(twin_attend_near, far[2:], 3),
        (shaped((rows, width), BF16),) * 3 + (shaped((2 * requests * own + own, width), BF16),),
        (limits, key_cache, value_cache, swapped_near, own_tree, packed, other, *from_far),
        [
            pltpu.VMEM((1, heads, own, 2 * block), F32),
            pltpu.VMEM((heads, 2 * own, block + LANES), F32),
        ],
        ties=partials[:1],
    )
    partials = [over_planes(part, turn) for part, turn in zip((*partials, near), far)]
    partials += [beside(crossing)]
    partials = [partials[0], partials[1], partials[2], partials[3], local]
    copied = beside(copied)

    total, rounded = call(
        twin_merge_and_project,
        (shaped((own, model), F32), shaped((own, model), BF16)),
        (*partials, out_weight),
    )
    bit = 1
    while 2 * bit < tp:
        total, rounded = call(
            twin_add,
            (shaped((own, model), F32), shaped((own, model), BF16)),
            (total, over_tp(rounded, bit)),
        )
        bit *= 2
    arrived = over_tp(rounded, bit)
    new_key_cache, new_value_cache = call(
        functools.partial(twin_compact, far),
        (shaped(key_cache.shape, BF16), shaped(value_cache.shape, BF16)),
        (targets, key_cache, value_cache, packed, *from_far, copied),
        [pltpu.VMEM((requests, 2, 2, own, width), BF16)],
    )
    hidden_out = call(
        twin_finish,
        shaped((own, columns), BF16),
        (total, arrived, post_gain[None, :], hidden_in),
    )
    return (hidden_out, new_key_cache, new_value_cache)


def body(*args):
    hidden_in, key_cache, parents = args[0], args[8], args[11]
    tp = lax.axis_size("tp")
    own, draft = hidden_in.shape[0], parents.shape[1]
    requests, _, width = key_cache.shape
    twin = (
        own % 16 == 0
        and draft == 2 * own
        and requests == 4
        and lax.axis_size("seq") == 2 * requests
        and own <= LANES
        and LANES % own == 0
        and own <= width
        and 3 * (width // HEAD_DIM) <= 16
        and tp > 1
        and tp & (tp - 1) == 0
    )
    return (body_twin if twin else body_general)(*args)


def solution(mesh):
    return jax.shard_map(
        body,
        mesh=mesh,
        in_specs=(
            P("seq", None),
            P(None, "tp"),
            P(None, "tp"),
            P(None, "tp"),
            P("tp", None),
            P("tp"),
            P("tp"),
            P("tp"),
            P(None, "seq", "tp"),
            P(None, "seq", "tp"),
            P(),
            P(),
            P(),
        ),
        out_specs=(P("seq", "tp"), P(None, "seq", "tp"), P(None, "seq", "tp")),
        check_vma=False,
    )
```

```python
import functools
import math

import jax
import jax.numpy as jnp
from jax import lax
from jax.experimental import pallas as pl
from jax.experimental.pallas import tpu as pltpu
from jax.sharding import PartitionSpec as P

HEAD_DIM = 128
LANES = 128
EPS = 1e-06
THETA = 500000.0
NEG = -1e30
F32 = jnp.float32
BF16 = jnp.bfloat16
VMEM = pl.BlockSpec(memory_space=pltpu.VMEM)
SMEM = pl.BlockSpec(memory_space=pltpu.SMEM)
ANY = pl.BlockSpec(memory_space=pl.ANY)


def params(mib):
    return pltpu.CompilerParams(vmem_limit_bytes=mib * 1024 * 1024)


def dot(a, b):
    return jnp.dot(a, b, preferred_element_type=F32)


def dot_t(a, b):
    return lax.dot_general(a, b, (((1,), (1,)), ((), ())), preferred_element_type=F32)


def iota(shape, axis):
    return lax.broadcasted_iota(jnp.int32, shape, axis)


def stacked(parts):
    if len(parts) == 1:
        return parts[0]
    if parts[0].shape[0] % 16 == 0:
        return jnp.concatenate(parts, axis=0)
    return jnp.concatenate([part.astype(F32) for part in parts], axis=0).astype(BF16)


def sum_squares(raw):
    return jnp.sum(raw * raw, axis=1, keepdims=True)


def project_qk(hidden, wq, wk, query_raw, key_raw, squares, wq_v, wk_v, sems):
    chunks, depth = wq_v.shape[0], wq_v.shape[1]
    copies = []
    for c in range(chunks):
        for at, (source, target) in enumerate(((wq, wq_v), (wk, wk_v))):
            copy = pltpu.make_async_copy(
                source.at[pl.ds(c * depth, depth)], target.at[c], sems.at[2 * c + at]
            )
            copy.start()
            copies.append(copy)
    q_sum, k_sum = None, None
    for c in range(chunks):
        part = hidden[:, c * depth : (c + 1) * depth]
        copies[2 * c].wait()
        q = dot(part, wq_v[c])
        copies[2 * c + 1].wait()
        k = dot(part, wk_v[c])
        q_sum = q if c == 0 else q_sum + q
        k_sum = k if c == 0 else k_sum + k
    query_raw[...] = q_sum
    key_raw[...] = k_sum
    lane = iota(squares.shape[1:], 1)
    both = jnp.where(lane == 0, sum_squares(q_sum), sum_squares(k_sum))
    for t in range(squares.shape[0]):
        squares[t] = both


def project_v_and_tree(
    lengths, leaves, hidden, parents, freqs, wv, value, own_tree, targets, cosine, sine, wv_v, anc_v, sems
):
    chunks, depth = wv_v.shape[0], wv_v.shape[1]
    copies = []
    for c in range(chunks):
        copy = pltpu.make_async_copy(wv.at[pl.ds(c * depth, depth)], wv_v.at[c], sems.at[c])
        copy.start()
        copies.append(copy)
    requests, draft = parents.shape
    own = hidden.shape[0]
    first = lax.axis_index("seq") * own
    row, col = iota((draft, draft), 0), iota((draft, draft), 1)
    eye = (row == col).astype(BF16)
    trees = [
        jnp.where((parents[pl.ds(r, 1), :] == row) | (row == col), 1.0, 0.0).astype(BF16)
        for r in range(requests)
    ]
    for _ in range(max(1, (draft - 1).bit_length())):
        trees = [jnp.minimum(dot(tree, tree), 1.0).astype(BF16) for tree in trees]
    for r in range(requests):
        upright = lax.dot_general(
            trees[r], eye, (((0,), (0,)), ((), ())), preferred_element_type=F32
        )
        anc_v[pl.ds(r * draft, draft), :] = upright
        level = jnp.sum(trees[r].astype(F32), axis=0, keepdims=True) - 1.0
        on_path = jnp.sum(jnp.where(row == leaves[r], upright, 0.0), axis=0, keepdims=True)
        place = lengths[r] + level.astype(jnp.int32)
        targets[r] = jnp.where(on_path > 0.5, place, -1)
    mine = anc_v[pl.ds(pl.multiple_of(first, own), own), :]
    own_tree[...] = mine
    level = jnp.sum(mine, axis=1, keepdims=True) - 1.0
    position = lengths[first // draft].astype(F32) + level
    angles = position * freqs[...]
    cosine[...] = jnp.cos(angles)
    half = jnp.sin(angles)
    sine[...] = jnp.where(iota(half.shape, 1) < HEAD_DIM // 2, -half, half)
    total = None
    for c in range(chunks):
        copies[c].wait()
        v = dot(hidden[:, c * depth : (c + 1) * depth], wv_v[c])
        total = v if c == 0 else total + v
    value[...] = total.astype(BF16)


def prepare(
    width_all, query_raw, key_raw, value, q_gain, k_gain, cosine, sine, squares, queries, keys_values
):
    width = query_raw.shape[1]
    total = sum(squares[k] for k in range(squares.shape[0]))
    cos, sin = cosine[...], sine[...]
    for at, (raw, gain, out) in enumerate(
        ((query_raw, q_gain, queries), (key_raw, k_gain, keys_values))
    ):
        scale = lax.rsqrt(total[:, at : at + 1] / width_all + EPS)
        for h in range(width // HEAD_DIM):
            lanes = slice(h * HEAD_DIM, (h + 1) * HEAD_DIM)
            x = raw[:, lanes] * scale * gain[:, lanes]
            turned = x * cos + pltpu.roll(x, HEAD_DIM // 2, 1) * sin
            turned = turned.astype(BF16)
            for s in range(out.shape[0]):
                out[s, :, lanes] = turned
    for s in range(keys_values.shape[0]):
        keys_values[s, :, width:] = value[...]


def attend_cache(group, lengths, key_cache, value_cache, queries, partials):
    requests, block, width = key_cache.shape
    own = queries.shape[1]
    heads = width // HEAD_DIM
    me = lax.axis_index("seq")
    factor = 1.0 / math.sqrt(HEAD_DIM)
    rows = group * own
    place = me * block + iota((rows, block), 1)
    lane = iota((rows, LANES), 1)
    for request in range(requests):
        q = stacked([queries[request * group + j] for j in range(group)])
        visible = place < lengths[request]
        stats = jnp.zeros((rows, LANES), F32)
        for h in range(heads):
            lanes = slice(h * HEAD_DIM, (h + 1) * HEAD_DIM)
            scores = dot_t(q[:, lanes], key_cache[request, :, lanes]) * factor
            scores = jnp.where(visible, scores, NEG)
            peak = jnp.max(scores, axis=1, keepdims=True).astype(BF16).astype(F32)
            weights = jnp.exp(jnp.where(visible, scores - peak, NEG))
            total = jnp.sum(weights, axis=1, keepdims=True)
            high = total.astype(BF16).astype(F32)
            out = dot(weights.astype(BF16), value_cache[request, :, lanes]).astype(BF16)
            for j in range(group):
                partials[request * group + j, :, lanes] = out[j * own : (j + 1) * own]
            stats = jnp.where(lane == h, peak, stats)
            stats = jnp.where(lane == heads + h, high, stats)
            stats = jnp.where(lane == 2 * heads + h, total - high, stats)
        stats = stats.astype(BF16)
        for j in range(group):
            partials[request * group + j, :, width:] = stats[j * own : (j + 1) * own]


def attend_draft(group, own_tree, queries, keys_values, out, stats):
    own, width = queries.shape[1:]
    heads = width // HEAD_DIM
    me = lax.axis_index("seq")
    first = me // group * group
    q = queries[me]
    pair = stacked([keys_values[first + j] for j in range(group)])
    factor = 1.0 / math.sqrt(HEAD_DIM)
    allowed = own_tree[...] > 0.5
    lane = iota((own, LANES), 1)
    kept = jnp.zeros((own, LANES), F32)
    for h in range(heads):
        lanes = slice(h * HEAD_DIM, (h + 1) * HEAD_DIM)
        there = slice(width + h * HEAD_DIM, width + (h + 1) * HEAD_DIM)
        scores = dot_t(q[:, lanes], pair[:, lanes]) * factor
        scores = jnp.where(allowed, scores, NEG)
        peak = jnp.max(scores, axis=1, keepdims=True)
        weights = jnp.exp(jnp.where(allowed, scores - peak, NEG))
        out[:, lanes] = dot(weights.astype(BF16), pair[:, there])
        kept = jnp.where(lane == h, peak, kept)
        kept = jnp.where(lane == heads + h, jnp.sum(weights, axis=1, keepdims=True), kept)
    stats[...] = kept


def merge_and_project(draft_out, draft_stats, wo, partials, projected, wo_v, sems):
    count, width, columns = wo_v.shape
    heads = width // HEAD_DIM
    copies = []
    for k in range(count):
        copy = pltpu.make_async_copy(
            wo.at[:, pl.ds(k * columns, columns)], wo_v.at[k], sems.at[k]
        )
        copy.start()
        copies.append(copy)
    parts = range(partials.shape[0])
    stats = [partials[s, :, width:].astype(F32) for s in parts]
    own_stats = draft_stats[...]
    attention = []
    for h in range(heads):
        lanes = slice(h * HEAD_DIM, (h + 1) * HEAD_DIM)
        peaks = [s[:, h : h + 1] for s in stats] + [own_stats[:, h : h + 1]]
        highest = functools.reduce(jnp.maximum, peaks)
        scales = [jnp.exp(peak - highest) for peak in peaks]
        total = own_stats[:, heads + h : heads + h + 1] * scales[-1]
        summed = draft_out[:, lanes] * scales[-1]
        for at in parts:
            s = stats[at]
            own_total = s[:, heads + h : heads + h + 1] + s[:, 2 * heads + h : 2 * heads + h + 1]
            total = total + own_total * scales[at]
            summed = summed + partials[at, :, lanes].astype(F32) * scales[at]
        attention.append((summed / total).astype(BF16))
    attention = jnp.concatenate(attention, axis=1)
    for k in range(count):
        copies[k].wait()
        projected[k] = dot(attention, wo_v[k]).astype(projected.dtype)


def add_up(parts, summed, power):
    total = sum(parts[k].astype(F32) for k in range(parts.shape[0]))
    summed[...] = total
    own_power = jnp.broadcast_to(sum_squares(total), power.shape[1:])
    for k in range(power.shape[0]):
        power[k] = own_power


def finish(model_width, summed, gain, hidden, powers, out):
    columns = summed.shape[1]
    power = sum(powers[k] for k in range(powers.shape[0]))[:, :1]
    start = pl.multiple_of(lax.axis_index("tp") * columns, columns)
    normed = summed[...] * lax.rsqrt(power / model_width + EPS) * gain[...]
    out[...] = (hidden[:, pl.ds(start, columns)].astype(F32) + normed).astype(BF16)


def compact(group, targets, key_cache, value_cache, keys_values, new_keys, new_values):
    requests, block, width = key_cache.shape
    own = keys_values.shape[1]
    me = lax.axis_index("seq")
    place = me * block + iota((block, group * own), 0)
    for request in range(requests):
        kv = stacked([keys_values[request * group + j] for j in range(group)])
        placing = place == targets[request]
        written = jnp.max(placing.astype(F32), axis=1, keepdims=True) > 0.5
        fresh = dot(placing.astype(BF16), kv)
        new_keys[request] = jnp.where(
            written, fresh[:, :width], key_cache[request].astype(F32)
        ).astype(BF16)
        new_values[request] = jnp.where(
            written, fresh[:, width:], value_cache[request].astype(F32)
        ).astype(BF16)


def shaped(shape, dtype):
    return jax.ShapeDtypeStruct(shape, dtype)


def body_general(
    hidden_in,
    query_weight,
    key_weight,
    value_weight,
    out_weight,
    query_gain,
    key_gain,
    post_gain,
    key_cache,
    value_cache,
    cache_lengths,
    parents,
    accepted_leaf,
):
    requests, block, width = key_cache.shape
    draft = parents.shape[1]
    own, model = hidden_in.shape
    tp = lax.axis_size("tp")
    seq = lax.axis_size("seq")
    group = draft // own
    columns = model // tp
    chunks = 4
    depth = model // chunks

    def exchange(x, axis):
        return lax.all_to_all(x, axis, 0, 0, tiled=True)

    query_raw, key_raw, squares = pl.pallas_call(
        project_qk,
        out_shape=(
            shaped((own, width), F32),
            shaped((own, width), F32),
            shaped((tp, own, LANES), F32),
        ),
        in_specs=[VMEM, ANY, ANY],
        out_specs=(VMEM, VMEM, VMEM),
        scratch_shapes=[
            pltpu.VMEM((chunks, depth, width), BF16),
            pltpu.VMEM((chunks, depth, width), BF16),
            pltpu.SemaphoreType.DMA((2 * chunks,)),
        ],
        compiler_params=params(56),
        cost_estimate=pl.CostEstimate(
            flops=4 * own * model * width, bytes_accessed=4 * model * width, transcendentals=0
        ),
        name="project_qk",
    )(hidden_in, query_weight, key_weight)
    squares = exchange(squares, "tp")

    exponents = -2.0 * (jnp.arange(HEAD_DIM) % (HEAD_DIM // 2)).astype(F32) / HEAD_DIM
    freqs = (THETA**exponents)[None, :]
    value, own_tree, targets, cosine, sine = pl.pallas_call(
        project_v_and_tree,
        out_shape=(
            shaped((own, width), BF16),
            shaped((own, draft), F32),
            shaped((requests, 1, draft), jnp.int32),
            shaped((own, HEAD_DIM), F32),
            shaped((own, HEAD_DIM), F32),
        ),
        in_specs=[SMEM, SMEM, VMEM, VMEM, VMEM, ANY],
        out_specs=(VMEM,) * 5,
        scratch_shapes=[
            pltpu.VMEM((chunks, depth, width), BF16),
            pltpu.VMEM((requests * draft, draft), F32),
            pltpu.SemaphoreType.DMA((chunks,)),
        ],
        compiler_params=params(16),
        cost_estimate=pl.CostEstimate(
            flops=2 * own * model * width, bytes_accessed=2 * model * width, transcendentals=0
        ),
        name="project_v_and_tree",
    )(cache_lengths, accepted_leaf, hidden_in, parents, freqs, value_weight)

    queries, keys_values = pl.pallas_call(
        functools.partial(prepare, tp * width),
        out_shape=(shaped((seq, own, width), BF16), shaped((seq, own, 2 * width), BF16)),
        in_specs=[VMEM] * 8,
        out_specs=(VMEM, VMEM),
        compiler_params=params(16),
        name="prepare",
    )(
        query_raw,
        key_raw,
        value,
        query_gain[None, :],
        key_gain[None, :],
        cosine,
        sine,
        squares,
    )
    queries = exchange(queries, "seq")
    keys_values = exchange(keys_values, "seq")

    partials = pl.pallas_call(
        functools.partial(attend_cache, group),
        out_shape=shaped((seq, own, width + LANES), BF16),
        in_specs=[SMEM, VMEM, VMEM, VMEM],
        out_specs=VMEM,
        compiler_params=params(16),
        name="attend_cache",
    )(cache_lengths, key_cache, value_cache, queries)
    partials = exchange(partials, "seq")

    draft_out, draft_stats = pl.pallas_call(
        functools.partial(attend_draft, group),
        out_shape=(shaped((own, width), F32), shaped((own, LANES), F32)),
        in_specs=[VMEM] * 3,
        out_specs=(VMEM, VMEM),
        compiler_params=params(16),
        name="attend_draft",
    )(own_tree, queries, keys_values)

    projected = pl.pallas_call(
        merge_and_project,
        out_shape=shaped((tp, own, columns), BF16),
        in_specs=[VMEM, VMEM, ANY, VMEM],
        out_specs=VMEM,
        scratch_shapes=[
            pltpu.VMEM((tp, width, columns), BF16),
            pltpu.SemaphoreType.DMA((tp,)),
        ],
        compiler_params=params(16),
        name="merge_and_project",
    )(draft_out, draft_stats, out_weight, partials)
    projected = exchange(projected, "tp")

    summed, power = pl.pallas_call(
        add_up,
        out_shape=(shaped((own, columns), F32), shaped((tp, own, LANES), F32)),
        in_specs=[VMEM],
        out_specs=(VMEM, VMEM),
        compiler_params=params(16),
        name="add_up",
    )(projected)
    power = exchange(power, "tp")

    hidden_out = pl.pallas_call(
        functools.partial(finish, model),
        out_shape=shaped((own, columns), BF16),
        in_specs=[VMEM] * 4,
        out_specs=VMEM,
        compiler_params=params(16),
        name="finish",
    )(summed, post_gain[None, :], hidden_in, power)

    new_key_cache, new_value_cache = pl.pallas_call(
        functools.partial(compact, group),
        out_shape=(shaped(key_cache.shape, BF16), shaped(value_cache.shape, BF16)),
        in_specs=[VMEM] * 4,
        out_specs=(VMEM, VMEM),
        compiler_params=params(24),
        name="compact",
    )(targets, key_cache, value_cache, keys_values)
    return (hidden_out, new_key_cache, new_value_cache)


def across(column):
    rows = column.shape[0]
    eye = iota((rows, rows), 0) == iota((rows, rows), 1)
    return jnp.sum(jnp.where(eye, column, 0.0), axis=0, keepdims=True)


def upright(line):
    rows = line.shape[1]
    eye = iota((rows, rows), 0) == iota((rows, rows), 1)
    return jnp.sum(jnp.where(eye, line, 0.0), axis=1, keepdims=True)


def eye_of(size):
    return (iota((size, size), 0) == iota((size, size), 1)).astype(BF16)


def plane():
    return lax.axis_index("seq") // 2


def twin_project_qk(hidden, wq, wk, query_raw, key_raw, squares):
    rows = hidden[...]
    own = rows.shape[0]
    for at, (weight, raw) in enumerate(((wq, query_raw), (wk, key_raw))):
        product = dot(rows, weight[...])
        raw[...] = product
        line = across(sum_squares(product))
        line = jnp.concatenate([line, jnp.zeros((1, LANES - own), F32)], axis=1)
        squares[:, at * LANES : (at + 1) * LANES] = jnp.broadcast_to(
            line, (squares.shape[0], LANES)
        )


def twin_project_v(hidden, wv, value):
    value[...] = dot(hidden[...], wv[...]).astype(BF16)


def twin_tree(
    turns, lengths, leaves, parents, freqs, own_tree, targets, cosine, sine, limits, held
):
    requests, draft = parents.shape
    own = own_tree.shape[1]
    row, col = iota((draft, draft), 0), iota((draft, draft), 1)
    eye = eye_of(draft)

    def length_of(request):
        picked = iota(lengths.shape, 1) == request
        return jnp.sum(jnp.where(picked, lengths[...], 0), axis=1, keepdims=True)

    for at, turn in enumerate(turns):
        limits[at : at + 1, :] = jnp.broadcast_to(
            length_of(plane() ^ turn), (1, limits.shape[1])
        )
    trees = [
        jnp.where((parents[pl.ds(r, 1), :] == row) | (row == col), 1.0, 0.0).astype(BF16)
        for r in range(requests)
    ]
    for _ in range(max(1, (draft - 1).bit_length())):
        trees = [jnp.minimum(dot(tree, tree), 1.0).astype(BF16) for tree in trees]
    for r in range(requests):
        standing = lax.dot_general(
            trees[r], eye, (((0,), (0,)), ((), ())), preferred_element_type=F32
        )
        held[r] = standing
        level = jnp.sum(trees[r].astype(F32), axis=0, keepdims=True) - 1.0
        on_path = jnp.where(row == leaves[:, r : r + 1], standing, 0.0)
        on_path = jnp.sum(on_path, axis=0, keepdims=True)
        place = lengths[:, r : r + 1] + level.astype(jnp.int32)
        targets[r] = jnp.where(on_path > 0.5, place, -1)
    within = lax.rem(lax.axis_index("seq"), 2)
    for at in range(2):
        first = (within ^ at) * own
        rows = held[plane(), pl.ds(pl.multiple_of(first, own), own), :]
        own_tree[at * own : (at + 1) * own, :] = jnp.where(
            within == 0, rows[:, :own], rows[:, own:]
        )
        mine = rows if at == 0 else mine
    level = jnp.sum(mine, axis=1, keepdims=True) - 1.0
    angles = (length_of(plane()).astype(F32) + level) * freqs[...]
    cosine[...] = jnp.cos(angles)
    half = jnp.sin(angles)
    sine[...] = jnp.where(iota(half.shape, 1) < HEAD_DIM // 2, -half, half)


def turned(raw, scale, gain, cos, sin):
    x = raw * scale * gain
    return (x * cos + pltpu.roll(x, HEAD_DIM // 2, 1) * sin).astype(BF16)


def twin_prepare(width_all, query_raw, key_raw, value, q_gain, k_gain, cosine, sine, *refs):
    squares, (queries, packed) = refs[:-2], refs[-2:]
    own, width = query_raw.shape
    cos, sin = cosine[...], sine[...]
    total = sum(ref[:1, :] for ref in squares)
    for at, (raw, gain) in enumerate(((query_raw, q_gain), (key_raw, k_gain))):
        scale = upright(total[:, at * LANES : at * LANES + own])
        scale = lax.rsqrt(scale / width_all + EPS)
        for h in range(width // HEAD_DIM):
            lanes = slice(h * HEAD_DIM, (h + 1) * HEAD_DIM)
            there = slice(at * width + h * HEAD_DIM, at * width + (h + 1) * HEAD_DIM)
            found = turned(raw[:, lanes], scale, gain[:, lanes], cos, sin)
            packed[:, there] = found
            if at == 0:
                queries[:, lanes] = found
    packed[:, 2 * width :] = value[...]


def weigh(s, visible):
    peak = jnp.max(s, axis=1, keepdims=True).astype(BF16).astype(F32)
    weights = jnp.exp(jnp.where(visible, s - peak, NEG))
    total = jnp.sum(weights, axis=1, keepdims=True)
    high = total.astype(BF16).astype(F32)
    return weights.astype(BF16), (peak, high, total - high)


def kept(stats, h, heads, found):
    lane = iota(stats.shape, 1)
    for at, column in enumerate(found):
        stats = jnp.where(lane == at * heads + h, column, stats)
    return stats


def write_stats(stats, out):
    own, width = stats.shape[0], out.shape[1]
    flat = lax.dot_general(
        stats.astype(BF16), eye_of(own), (((0,), (0,)), ((), ())), preferred_element_type=F32
    )
    flat = jnp.concatenate([flat[:16], jnp.zeros((16, width - own), F32)], axis=1)
    out[own : own + 16, :] = flat.astype(BF16)


def twin_attend_far(turns, limits, key_cache, value_cache, swapped, *refs):
    count = len(turns)
    queries, outs, scores = refs[:count], refs[count : 2 * count], refs[2 * count]
    block, width = key_cache.shape[1:]
    heads = width // HEAD_DIM
    own = queries[0].shape[0]
    me = lax.axis_index("seq")
    factor = 1.0 / math.sqrt(HEAD_DIM)
    place = iota((1, block), 1)
    both = jnp.concatenate([me * block + place, (me ^ 1) * block + place], axis=1)
    visible = [both < limits[at + 1 : at + 2, :] for at in range(count)]
    for at, turn in enumerate(turns):
        for h in range(heads):
            lanes = slice(h * HEAD_DIM, (h + 1) * HEAD_DIM)
            q = queries[at][:, lanes]
            first = dot_t(q, key_cache[plane() ^ turn, :, lanes])
            second = dot_t(q, swapped[at, 0, :, lanes])
            product = jnp.concatenate([first, second], axis=1) * factor
            scores[at, h] = jnp.where(visible[at], product, NEG)
    for at, turn in enumerate(turns):
        stats = jnp.zeros((own, LANES), F32)
        for h in range(heads):
            lanes = slice(h * HEAD_DIM, (h + 1) * HEAD_DIM)
            weights, found = weigh(scores[at, h], visible[at])
            out = dot(weights[:, :block], value_cache[plane() ^ turn, :, lanes])
            out = out + dot(weights[:, block:], swapped[at, 1, :, lanes])
            outs[at][:own, lanes] = out.astype(BF16)
            stats = kept(stats, h, heads, found)
        write_stats(stats, outs[at])


def twin_attend_near(limits, key_cache, value_cache, own_tree, mine, other, *refs):
    queries, (crossing, local, copied, own_scores) = refs[:-4], refs[-4:]
    count = len(queries)
    block, width = key_cache.shape[1:]
    heads = width // HEAD_DIM
    own = other.shape[0]
    factor = 1.0 / math.sqrt(HEAD_DIM)
    place = lax.axis_index("seq") * block + iota((1, block), 1)
    here = jnp.broadcast_to(place < limits[:1, :block], (2 * own, block))
    rest = own_scores.shape[2] - block - own
    near = jnp.concatenate(
        [jnp.where(here, 1.0, 0.0), own_tree[...], jnp.zeros((2 * own, rest), F32)], axis=1
    )
    near = near > 0.5
    pair = stacked([mine[:, :width], other[...]])
    for h in range(heads):
        lanes = slice(h * HEAD_DIM, (h + 1) * HEAD_DIM)
        keys = jnp.concatenate(
            [mine[:, width + h * HEAD_DIM : width + (h + 1) * HEAD_DIM]] * (1 + rest // own), axis=0
        )
        first = dot_t(pair[:, lanes], key_cache[plane(), :, lanes])
        product = jnp.concatenate([first, dot_t(pair[:, lanes], keys)], axis=1) * factor
        own_scores[h] = jnp.where(near, product, NEG)
    stats = jnp.zeros((2 * own, LANES), F32)
    for h in range(heads):
        lanes = slice(h * HEAD_DIM, (h + 1) * HEAD_DIM)
        weights, found = weigh(own_scores[h], near)
        out = dot(weights[:, :block], value_cache[plane(), :, lanes])
        values = mine[:, 2 * width + h * HEAD_DIM : 2 * width + (h + 1) * HEAD_DIM]
        out = out + dot(weights[:, block : block + own], values)
        out = out.astype(BF16)
        local[:own, lanes] = out[:own]
        crossing[:own, lanes] = out[own:]
        stats = kept(stats, h, heads, found)
    write_stats(stats[:own], local)
    write_stats(stats[own:], crossing)
    for at, ref in enumerate((mine, *queries)):
        for part in range(2):
            rows = slice((2 * at + part) * own, (2 * at + part + 1) * own)
            copied[rows, :] = ref[:, (part + 1) * width : (part + 2) * width]
    last = 2 * (count + 1) * own
    copied[last:, :] = jnp.zeros((copied.shape[0] - last, width), BF16)


def twin_rows(mine, theirs, held):
    within = lax.rem(lax.axis_index("seq"), 2)
    held[within] = mine
    held[1 - within] = theirs
    return stacked([held[0], held[1]])


def twin_merge_and_project(*refs):
    partials, (wo, total_out, rounded) = refs[:-3], refs[-3:]
    own, width = total_out.shape[0], partials[0].shape[1]
    heads = width // HEAD_DIM
    stats = [dot_t(eye_of(own), ref[own : own + 16, :own]) for ref in partials]
    attention = []
    for h in range(heads):
        lanes = slice(h * HEAD_DIM, (h + 1) * HEAD_DIM)
        peaks = [s[:, h : h + 1] for s in stats]
        highest = functools.reduce(jnp.maximum, peaks)
        total, summed = 0.0, 0.0
        for ref, s, peak in zip(partials, stats, peaks):
            scale = jnp.exp(peak - highest)
            own_total = s[:, heads + h : heads + h + 1] + s[:, 2 * heads + h : 2 * heads + h + 1]
            total = total + own_total * scale
            summed = summed + ref[:own, lanes].astype(F32) * scale
        attention.append((summed / total).astype(BF16))
    product = dot(jnp.concatenate(attention, axis=1), wo[...])
    total_out[...] = product
    rounded[...] = product.astype(BF16)


def twin_add(mine, theirs, total, rounded):
    both = mine[...] + theirs[...].astype(F32)
    total[...] = both
    rounded[...] = both.astype(BF16)


def twin_finish(mine, theirs, gain, hidden, out):
    model_width = mine.shape[1]
    columns = out.shape[1]
    total = mine[...] + theirs[...].astype(F32)
    scale = lax.rsqrt(sum_squares(total) / model_width + EPS)
    lanes = pl.ds(pl.multiple_of(lax.axis_index("tp") * columns, columns), columns)
    normed = (mine[:, lanes] + theirs[:, lanes].astype(F32)) * scale * gain[...]
    out[...] = (hidden[:, lanes].astype(F32) + normed).astype(BF16)


def twin_compact(far, targets, key_cache, value_cache, *refs):
    count = len(far) + 1
    ours, (copied, new_keys, new_values, held) = refs[:count], refs[count:]
    block, width = key_cache.shape[1:]
    own = ours[0].shape[0]
    me = lax.axis_index("seq")
    place = me * block + iota((block, targets.shape[2]), 0)
    for at, turn in enumerate((0, *far)):
        request = plane() ^ turn
        placing = place == targets[request]
        written = jnp.max(placing.astype(F32), axis=1, keepdims=True) > 0.5
        placing = placing.astype(BF16)
        for part, (cache, out) in enumerate(((key_cache, new_keys), (value_cache, new_values))):
            lanes = slice((part + 1) * width, (part + 2) * width)
            rows = slice((2 * at + part) * own, (2 * at + part + 1) * own)
            theirs = copied[rows, :]
            fresh = twin_rows(ours[at][:, lanes], theirs, held.at[at, part])
            moved = dot(placing, fresh)
            out[request] = jnp.where(written, moved, cache[request].astype(F32)).astype(BF16)


def body_twin(
    hidden_in,
    query_weight,
    key_weight,
    value_weight,
    out_weight,
    query_gain,
    key_gain,
    post_gain,
    key_cache,
    value_cache,
    cache_lengths,
    parents,
    accepted_leaf,
):
    requests, block, width = key_cache.shape
    draft = parents.shape[1]
    own, model = hidden_in.shape
    tp = lax.axis_size("tp")
    seq = lax.axis_size("seq")
    columns = model // tp
    heads = width // HEAD_DIM
    far = tuple(range(requests - 1, 0, -1))

    def call(kernel, outs, inputs, scratch=(), mib=16, specs=None, ties=()):
        count = len(inputs)

        def run(*refs):
            kernel(*refs[:count], *refs[count + len(ties) :])

        return pl.pallas_call(
            run,
            out_shape=outs,
            in_specs=([VMEM] * count if specs is None else specs) + [ANY] * len(ties),
            out_specs=jax.tree.map(lambda _: VMEM, outs),
            scratch_shapes=list(scratch),
            compiler_params=params(mib),
            name=getattr(kernel, "func", kernel).__name__,
        )(*inputs, *ties)

    def over_tp(x, k):
        return lax.ppermute(x, "tp", [(i, i ^ k) for i in range(tp)])

    def beside(x):
        return lax.ppermute(x, "seq", [(i, i ^ 1) for i in range(seq)])

    def over_planes(x, turn):
        return lax.ppermute(x, "seq", [(i, (i // 2 ^ turn) * 2 + i % 2) for i in range(seq)])

    me = lax.axis_index("seq") // 2

    def picked(turns):
        parts = [
            [lax.dynamic_index_in_dim(x, me ^ turn, 0, False) for x in (key_cache, value_cache)]
            for turn in turns
        ]
        return jnp.stack([jnp.stack(part) for part in parts])

    swapped = beside(picked(far))
    query_raw, key_raw, squares = call(
        twin_project_qk,
        (shaped((own, width), F32), shaped((own, width), F32), shaped((8, 2 * LANES), F32)),
        (hidden_in, query_weight, key_weight),
    )
    all_squares = [squares] + [over_tp(squares, k) for k in range(tp - 1, 0, -1)]

    exponents = -2.0 * (jnp.arange(HEAD_DIM) % (HEAD_DIM // 2)).astype(F32) / HEAD_DIM
    freqs = (THETA**exponents)[None, :]
    own_tree, targets, cosine, sine, limits = call(
        functools.partial(twin_tree, (0, *far)),
        (
            shaped((draft, own), F32),
            shaped((requests, 1, draft), jnp.int32),
            shaped((own, HEAD_DIM), F32),
            shaped((own, HEAD_DIM), F32),
            shaped((requests, 2 * block), jnp.int32),
        ),
        (cache_lengths[None, :], accepted_leaf[None, :], parents, freqs),
        [pltpu.VMEM((requests, draft, draft), F32)],
    )
    value = call(twin_project_v, shaped((own, width), BF16), (hidden_in, value_weight))
    queries, packed = call(
        functools.partial(twin_prepare, tp * width),
        (shaped((own, width), BF16), shaped((own, 3 * width), BF16)),
        (
            query_raw,
            key_raw,
            value,
            query_gain[None, :],
            key_gain[None, :],
            cosine,
            sine,
            *all_squares,
        ),
    )
    from_far = [over_planes(packed, turn) for turn in far]
    other = beside(queries)

    rows = own + 16
    partials = call(
        functools.partial(twin_attend_far, far),
        (shaped((rows, width), BF16),) * len(far),
        (limits, key_cache, value_cache, swapped, *from_far),
        [pltpu.VMEM((len(far), heads, own, 2 * block), F32)],
    )
    crossing, local, copied = call(
        twin_attend_near,
        (shaped((rows, width), BF16),) * 2 + (shaped((2 * requests * own + own, width), BF16),),
        (limits, key_cache, value_cache, own_tree, packed, other, *from_far),
        [pltpu.VMEM((heads, 2 * own, block + LANES), F32)],
        ties=partials[:1],
    )
    partials = [over_planes(part, turn) for part, turn in zip(partials, far)]
    partials += [beside(crossing)]
    partials = [partials[0], partials[1], partials[3], partials[2], local]
    copied = beside(copied)

    total, rounded = call(
        twin_merge_and_project,
        (shaped((own, model), F32), shaped((own, model), BF16)),
        (*partials, out_weight),
    )
    bit = 1
    while 2 * bit < tp:
        total, rounded = call(
            twin_add,
            (shaped((own, model), F32), shaped((own, model), BF16)),
            (total, over_tp(rounded, bit)),
        )
        bit *= 2
    arrived = over_tp(rounded, bit)
    new_key_cache, new_value_cache = call(
        functools.partial(twin_compact, far),
        (shaped(key_cache.shape, BF16), shaped(value_cache.shape, BF16)),
        (targets, key_cache, value_cache, packed, *from_far, copied),
        [pltpu.VMEM((requests, 2, 2, own, width), BF16)],
    )
    hidden_out = call(
        twin_finish,
        shaped((own, columns), BF16),
        (total, arrived, post_gain[None, :], hidden_in),
    )
    return (hidden_out, new_key_cache, new_value_cache)


def body(*args):
    hidden_in, key_cache, parents = args[0], args[8], args[11]
    tp = lax.axis_size("tp")
    own, draft = hidden_in.shape[0], parents.shape[1]
    requests, _, width = key_cache.shape
    twin = (
        own % 16 == 0
        and draft == 2 * own
        and requests == 4
        and lax.axis_size("seq") == 2 * requests
        and own <= LANES
        and LANES % own == 0
        and own <= width
        and 3 * (width // HEAD_DIM) <= 16
        and tp > 1
        and tp & (tp - 1) == 0
    )
    return (body_twin if twin else body_general)(*args)


def solution(mesh):
    return jax.shard_map(
        body,
        mesh=mesh,
        in_specs=(
            P("seq", None),
            P(None, "tp"),
            P(None, "tp"),
            P(None, "tp"),
            P("tp", None),
            P("tp"),
            P("tp"),
            P("tp"),
            P(None, "seq", "tp"),
            P(None, "seq", "tp"),
            P(),
            P(),
            P(),
        ),
        out_specs=(P("seq", "tp"), P(None, "seq", "tp"), P(None, "seq", "tp")),
        check_vma=False,
    )
```

```python
import functools
import math

import jax
import jax.numpy as jnp
from jax import lax
from jax.experimental import pallas as pl
from jax.experimental.pallas import tpu as pltpu
from jax.sharding import PartitionSpec as P

HEAD_DIM = 128
LANES = 128
EPS = 1e-06
THETA = 500000.0
NEG = -1e30
F32 = jnp.float32
BF16 = jnp.bfloat16
VMEM = pl.BlockSpec(memory_space=pltpu.VMEM)
SMEM = pl.BlockSpec(memory_space=pltpu.SMEM)
ANY = pl.BlockSpec(memory_space=pl.ANY)


def params(mib):
    return pltpu.CompilerParams(vmem_limit_bytes=mib * 1024 * 1024)


def dot(a, b):
    return jnp.dot(a, b, preferred_element_type=F32)


def dot_t(a, b):
    return lax.dot_general(a, b, (((1,), (1,)), ((), ())), preferred_element_type=F32)


def iota(shape, axis):
    return lax.broadcasted_iota(jnp.int32, shape, axis)


def stacked(parts):
    if len(parts) == 1:
        return parts[0]
    if parts[0].shape[0] % 16 == 0:
        return jnp.concatenate(parts, axis=0)
    return jnp.concatenate([part.astype(F32) for part in parts], axis=0).astype(BF16)


def sum_squares(raw):
    return jnp.sum(raw * raw, axis=1, keepdims=True)


def project_qk(hidden, wq, wk, query_raw, key_raw, squares, wq_v, wk_v, sems):
    chunks, depth = wq_v.shape[0], wq_v.shape[1]
    copies = []
    for c in range(chunks):
        for at, (source, target) in enumerate(((wq, wq_v), (wk, wk_v))):
            copy = pltpu.make_async_copy(
                source.at[pl.ds(c * depth, depth)], target.at[c], sems.at[2 * c + at]
            )
            copy.start()
            copies.append(copy)
    q_sum, k_sum = None, None
    for c in range(chunks):
        part = hidden[:, c * depth : (c + 1) * depth]
        copies[2 * c].wait()
        q = dot(part, wq_v[c])
        copies[2 * c + 1].wait()
        k = dot(part, wk_v[c])
        q_sum = q if c == 0 else q_sum + q
        k_sum = k if c == 0 else k_sum + k
    query_raw[...] = q_sum
    key_raw[...] = k_sum
    lane = iota(squares.shape[1:], 1)
    both = jnp.where(lane == 0, sum_squares(q_sum), sum_squares(k_sum))
    for t in range(squares.shape[0]):
        squares[t] = both


def project_v_and_tree(
    lengths, leaves, hidden, parents, freqs, wv, value, own_tree, targets, cosine, sine, wv_v, anc_v, sems
):
    chunks, depth = wv_v.shape[0], wv_v.shape[1]
    copies = []
    for c in range(chunks):
        copy = pltpu.make_async_copy(wv.at[pl.ds(c * depth, depth)], wv_v.at[c], sems.at[c])
        copy.start()
        copies.append(copy)
    requests, draft = parents.shape
    own = hidden.shape[0]
    first = lax.axis_index("seq") * own
    row, col = iota((draft, draft), 0), iota((draft, draft), 1)
    eye = (row == col).astype(BF16)
    trees = [
        jnp.where((parents[pl.ds(r, 1), :] == row) | (row == col), 1.0, 0.0).astype(BF16)
        for r in range(requests)
    ]
    for _ in range(max(1, (draft - 1).bit_length())):
        trees = [jnp.minimum(dot(tree, tree), 1.0).astype(BF16) for tree in trees]
    for r in range(requests):
        upright = lax.dot_general(
            trees[r], eye, (((0,), (0,)), ((), ())), preferred_element_type=F32
        )
        anc_v[pl.ds(r * draft, draft), :] = upright
        level = jnp.sum(trees[r].astype(F32), axis=0, keepdims=True) - 1.0
        on_path = jnp.sum(jnp.where(row == leaves[r], upright, 0.0), axis=0, keepdims=True)
        place = lengths[r] + level.astype(jnp.int32)
        targets[r] = jnp.where(on_path > 0.5, place, -1)
    mine = anc_v[pl.ds(pl.multiple_of(first, own), own), :]
    own_tree[...] = mine
    level = jnp.sum(mine, axis=1, keepdims=True) - 1.0
    position = lengths[first // draft].astype(F32) + level
    angles = position * freqs[...]
    cosine[...] = jnp.cos(angles)
    half = jnp.sin(angles)
    sine[...] = jnp.where(iota(half.shape, 1) < HEAD_DIM // 2, -half, half)
    total = None
    for c in range(chunks):
        copies[c].wait()
        v = dot(hidden[:, c * depth : (c + 1) * depth], wv_v[c])
        total = v if c == 0 else total + v
    value[...] = total.astype(BF16)


def prepare(
    width_all, query_raw, key_raw, value, q_gain, k_gain, cosine, sine, squares, queries, keys_values
):
    width = query_raw.shape[1]
    total = sum(squares[k] for k in range(squares.shape[0]))
    cos, sin = cosine[...], sine[...]
    for at, (raw, gain, out) in enumerate(
        ((query_raw, q_gain, queries), (key_raw, k_gain, keys_values))
    ):
        scale = lax.rsqrt(total[:, at : at + 1] / width_all + EPS)
        for h in range(width // HEAD_DIM):
            lanes = slice(h * HEAD_DIM, (h + 1) * HEAD_DIM)
            x = raw[:, lanes] * scale * gain[:, lanes]
            turned = x * cos + pltpu.roll(x, HEAD_DIM // 2, 1) * sin
            turned = turned.astype(BF16)
            for s in range(out.shape[0]):
                out[s, :, lanes] = turned
    for s in range(keys_values.shape[0]):
        keys_values[s, :, width:] = value[...]


def attend_cache(group, lengths, key_cache, value_cache, queries, partials):
    requests, block, width = key_cache.shape
    own = queries.shape[1]
    heads = width // HEAD_DIM
    me = lax.axis_index("seq")
    factor = 1.0 / math.sqrt(HEAD_DIM)
    rows = group * own
    place = me * block + iota((rows, block), 1)
    lane = iota((rows, LANES), 1)
    for request in range(requests):
        q = stacked([queries[request * group + j] for j in range(group)])
        visible = place < lengths[request]
        stats = jnp.zeros((rows, LANES), F32)
        for h in range(heads):
            lanes = slice(h * HEAD_DIM, (h + 1) * HEAD_DIM)
            scores = dot_t(q[:, lanes], key_cache[request, :, lanes]) * factor
            scores = jnp.where(visible, scores, NEG)
            peak = jnp.max(scores, axis=1, keepdims=True).astype(BF16).astype(F32)
            weights = jnp.exp(jnp.where(visible, scores - peak, NEG))
            total = jnp.sum(weights, axis=1, keepdims=True)
            high = total.astype(BF16).astype(F32)
            out = dot(weights.astype(BF16), value_cache[request, :, lanes]).astype(BF16)
            for j in range(group):
                partials[request * group + j, :, lanes] = out[j * own : (j + 1) * own]
            stats = jnp.where(lane == h, peak, stats)
            stats = jnp.where(lane == heads + h, high, stats)
            stats = jnp.where(lane == 2 * heads + h, total - high, stats)
        stats = stats.astype(BF16)
        for j in range(group):
            partials[request * group + j, :, width:] = stats[j * own : (j + 1) * own]


def attend_draft(group, own_tree, queries, keys_values, out, stats):
    own, width = queries.shape[1:]
    heads = width // HEAD_DIM
    me = lax.axis_index("seq")
    first = me // group * group
    q = queries[me]
    pair = stacked([keys_values[first + j] for j in range(group)])
    factor = 1.0 / math.sqrt(HEAD_DIM)
    allowed = own_tree[...] > 0.5
    lane = iota((own, LANES), 1)
    kept = jnp.zeros((own, LANES), F32)
    for h in range(heads):
        lanes = slice(h * HEAD_DIM, (h + 1) * HEAD_DIM)
        there = slice(width + h * HEAD_DIM, width + (h + 1) * HEAD_DIM)
        scores = dot_t(q[:, lanes], pair[:, lanes]) * factor
        scores = jnp.where(allowed, scores, NEG)
        peak = jnp.max(scores, axis=1, keepdims=True)
        weights = jnp.exp(jnp.where(allowed, scores - peak, NEG))
        out[:, lanes] = dot(weights.astype(BF16), pair[:, there])
        kept = jnp.where(lane == h, peak, kept)
        kept = jnp.where(lane == heads + h, jnp.sum(weights, axis=1, keepdims=True), kept)
    stats[...] = kept


def merge_and_project(draft_out, draft_stats, wo, partials, projected, wo_v, sems):
    count, width, columns = wo_v.shape
    heads = width // HEAD_DIM
    copies = []
    for k in range(count):
        copy = pltpu.make_async_copy(
            wo.at[:, pl.ds(k * columns, columns)], wo_v.at[k], sems.at[k]
        )
        copy.start()
        copies.append(copy)
    parts = range(partials.shape[0])
    stats = [partials[s, :, width:].astype(F32) for s in parts]
    own_stats = draft_stats[...]
    attention = []
    for h in range(heads):
        lanes = slice(h * HEAD_DIM, (h + 1) * HEAD_DIM)
        peaks = [s[:, h : h + 1] for s in stats] + [own_stats[:, h : h + 1]]
        highest = functools.reduce(jnp.maximum, peaks)
        scales = [jnp.exp(peak - highest) for peak in peaks]
        total = own_stats[:, heads + h : heads + h + 1] * scales[-1]
        summed = draft_out[:, lanes] * scales[-1]
        for at in parts:
            s = stats[at]
            own_total = s[:, heads + h : heads + h + 1] + s[:, 2 * heads + h : 2 * heads + h + 1]
            total = total + own_total * scales[at]
            summed = summed + partials[at, :, lanes].astype(F32) * scales[at]
        attention.append((summed / total).astype(BF16))
    attention = jnp.concatenate(attention, axis=1)
    for k in range(count):
        copies[k].wait()
        projected[k] = dot(attention, wo_v[k]).astype(projected.dtype)


def add_up(parts, summed, power):
    total = sum(parts[k].astype(F32) for k in range(parts.shape[0]))
    summed[...] = total
    own_power = jnp.broadcast_to(sum_squares(total), power.shape[1:])
    for k in range(power.shape[0]):
        power[k] = own_power


def finish(model_width, summed, gain, hidden, powers, out):
    columns = summed.shape[1]
    power = sum(powers[k] for k in range(powers.shape[0]))[:, :1]
    start = pl.multiple_of(lax.axis_index("tp") * columns, columns)
    normed = summed[...] * lax.rsqrt(power / model_width + EPS) * gain[...]
    out[...] = (hidden[:, pl.ds(start, columns)].astype(F32) + normed).astype(BF16)


def compact(group, targets, key_cache, value_cache, keys_values, new_keys, new_values):
    requests, block, width = key_cache.shape
    own = keys_values.shape[1]
    me = lax.axis_index("seq")
    place = me * block + iota((block, group * own), 0)
    for request in range(requests):
        kv = stacked([keys_values[request * group + j] for j in range(group)])
        placing = place == targets[request]
        written = jnp.max(placing.astype(F32), axis=1, keepdims=True) > 0.5
        fresh = dot(placing.astype(BF16), kv)
        new_keys[request] = jnp.where(
            written, fresh[:, :width], key_cache[request].astype(F32)
        ).astype(BF16)
        new_values[request] = jnp.where(
            written, fresh[:, width:], value_cache[request].astype(F32)
        ).astype(BF16)


def shaped(shape, dtype):
    return jax.ShapeDtypeStruct(shape, dtype)


def body_general(
    hidden_in,
    query_weight,
    key_weight,
    value_weight,
    out_weight,
    query_gain,
    key_gain,
    post_gain,
    key_cache,
    value_cache,
    cache_lengths,
    parents,
    accepted_leaf,
):
    requests, block, width = key_cache.shape
    draft = parents.shape[1]
    own, model = hidden_in.shape
    tp = lax.axis_size("tp")
    seq = lax.axis_size("seq")
    group = draft // own
    columns = model // tp
    chunks = 4
    depth = model // chunks

    def exchange(x, axis):
        return lax.all_to_all(x, axis, 0, 0, tiled=True)

    query_raw, key_raw, squares = pl.pallas_call(
        project_qk,
        out_shape=(
            shaped((own, width), F32),
            shaped((own, width), F32),
            shaped((tp, own, LANES), F32),
        ),
        in_specs=[VMEM, ANY, ANY],
        out_specs=(VMEM, VMEM, VMEM),
        scratch_shapes=[
            pltpu.VMEM((chunks, depth, width), BF16),
            pltpu.VMEM((chunks, depth, width), BF16),
            pltpu.SemaphoreType.DMA((2 * chunks,)),
        ],
        compiler_params=params(56),
        cost_estimate=pl.CostEstimate(
            flops=4 * own * model * width, bytes_accessed=4 * model * width, transcendentals=0
        ),
        name="project_qk",
    )(hidden_in, query_weight, key_weight)
    squares = exchange(squares, "tp")

    exponents = -2.0 * (jnp.arange(HEAD_DIM) % (HEAD_DIM // 2)).astype(F32) / HEAD_DIM
    freqs = (THETA**exponents)[None, :]
    value, own_tree, targets, cosine, sine = pl.pallas_call(
        project_v_and_tree,
        out_shape=(
            shaped((own, width), BF16),
            shaped((own, draft), F32),
            shaped((requests, 1, draft), jnp.int32),
            shaped((own, HEAD_DIM), F32),
            shaped((own, HEAD_DIM), F32),
        ),
        in_specs=[SMEM, SMEM, VMEM, VMEM, VMEM, ANY],
        out_specs=(VMEM,) * 5,
        scratch_shapes=[
            pltpu.VMEM((chunks, depth, width), BF16),
            pltpu.VMEM((requests * draft, draft), F32),
            pltpu.SemaphoreType.DMA((chunks,)),
        ],
        compiler_params=params(16),
        cost_estimate=pl.CostEstimate(
            flops=2 * own * model * width, bytes_accessed=2 * model * width, transcendentals=0
        ),
        name="project_v_and_tree",
    )(cache_lengths, accepted_leaf, hidden_in, parents, freqs, value_weight)

    queries, keys_values = pl.pallas_call(
        functools.partial(prepare, tp * width),
        out_shape=(shaped((seq, own, width), BF16), shaped((seq, own, 2 * width), BF16)),
        in_specs=[VMEM] * 8,
        out_specs=(VMEM, VMEM),
        compiler_params=params(16),
        name="prepare",
    )(
        query_raw,
        key_raw,
        value,
        query_gain[None, :],
        key_gain[None, :],
        cosine,
        sine,
        squares,
    )
    queries = exchange(queries, "seq")
    keys_values = exchange(keys_values, "seq")

    partials = pl.pallas_call(
        functools.partial(attend_cache, group),
        out_shape=shaped((seq, own, width + LANES), BF16),
        in_specs=[SMEM, VMEM, VMEM, VMEM],
        out_specs=VMEM,
        compiler_params=params(16),
        name="attend_cache",
    )(cache_lengths, key_cache, value_cache, queries)
    partials = exchange(partials, "seq")

    draft_out, draft_stats = pl.pallas_call(
        functools.partial(attend_draft, group),
        out_shape=(shaped((own, width), F32), shaped((own, LANES), F32)),
        in_specs=[VMEM] * 3,
        out_specs=(VMEM, VMEM),
        compiler_params=params(16),
        name="attend_draft",
    )(own_tree, queries, keys_values)

    projected = pl.pallas_call(
        merge_and_project,
        out_shape=shaped((tp, own, columns), BF16),
        in_specs=[VMEM, VMEM, ANY, VMEM],
        out_specs=VMEM,
        scratch_shapes=[
            pltpu.VMEM((tp, width, columns), BF16),
            pltpu.SemaphoreType.DMA((tp,)),
        ],
        compiler_params=params(16),
        name="merge_and_project",
    )(draft_out, draft_stats, out_weight, partials)
    projected = exchange(projected, "tp")

    summed, power = pl.pallas_call(
        add_up,
        out_shape=(shaped((own, columns), F32), shaped((tp, own, LANES), F32)),
        in_specs=[VMEM],
        out_specs=(VMEM, VMEM),
        compiler_params=params(16),
        name="add_up",
    )(projected)
    power = exchange(power, "tp")

    hidden_out = pl.pallas_call(
        functools.partial(finish, model),
        out_shape=shaped((own, columns), BF16),
        in_specs=[VMEM] * 4,
        out_specs=VMEM,
        compiler_params=params(16),
        name="finish",
    )(summed, post_gain[None, :], hidden_in, power)

    new_key_cache, new_value_cache = pl.pallas_call(
        functools.partial(compact, group),
        out_shape=(shaped(key_cache.shape, BF16), shaped(value_cache.shape, BF16)),
        in_specs=[VMEM] * 4,
        out_specs=(VMEM, VMEM),
        compiler_params=params(24),
        name="compact",
    )(targets, key_cache, value_cache, keys_values)
    return (hidden_out, new_key_cache, new_value_cache)


def across(column):
    rows = column.shape[0]
    eye = iota((rows, rows), 0) == iota((rows, rows), 1)
    return jnp.sum(jnp.where(eye, column, 0.0), axis=0, keepdims=True)


def upright(line):
    rows = line.shape[1]
    eye = iota((rows, rows), 0) == iota((rows, rows), 1)
    return jnp.sum(jnp.where(eye, line, 0.0), axis=1, keepdims=True)


def eye_of(size):
    return (iota((size, size), 0) == iota((size, size), 1)).astype(BF16)


def plane():
    return lax.axis_index("seq") // 2


def twin_project_qk(hidden, wq, wk, query_raw, key_raw, squares):
    rows = hidden[...]
    own = rows.shape[0]
    for at, (weight, raw) in enumerate(((wq, query_raw), (wk, key_raw))):
        product = dot(rows, weight[...])
        raw[...] = product
        line = across(sum_squares(product))
        line = jnp.concatenate([line, jnp.zeros((1, LANES - own), F32)], axis=1)
        squares[:, at * LANES : (at + 1) * LANES] = jnp.broadcast_to(
            line, (squares.shape[0], LANES)
        )


def twin_project_v(hidden, wv, value):
    value[...] = dot(hidden[...], wv[...]).astype(BF16)


def twin_tree(
    turns, lengths, leaves, parents, freqs, own_tree, targets, cosine, sine, limits, held
):
    requests, draft = parents.shape
    own = own_tree.shape[1]
    row, col = iota((draft, draft), 0), iota((draft, draft), 1)
    eye = eye_of(draft)

    def length_of(request):
        picked = iota(lengths.shape, 1) == request
        return jnp.sum(jnp.where(picked, lengths[...], 0), axis=1, keepdims=True)

    for at, turn in enumerate(turns):
        limits[at : at + 1, :] = jnp.broadcast_to(
            length_of(plane() ^ turn), (1, limits.shape[1])
        )
    trees = [
        jnp.where((parents[pl.ds(r, 1), :] == row) | (row == col), 1.0, 0.0).astype(BF16)
        for r in range(requests)
    ]
    for _ in range(max(1, (draft - 1).bit_length())):
        trees = [jnp.minimum(dot(tree, tree), 1.0).astype(BF16) for tree in trees]
    for r in range(requests):
        standing = lax.dot_general(
            trees[r], eye, (((0,), (0,)), ((), ())), preferred_element_type=F32
        )
        held[r] = standing
        level = jnp.sum(trees[r].astype(F32), axis=0, keepdims=True) - 1.0
        on_path = jnp.where(row == leaves[:, r : r + 1], standing, 0.0)
        on_path = jnp.sum(on_path, axis=0, keepdims=True)
        place = lengths[:, r : r + 1] + level.astype(jnp.int32)
        targets[r] = jnp.where(on_path > 0.5, place, -1)
    within = lax.rem(lax.axis_index("seq"), 2)
    for at in range(2):
        first = (within ^ at) * own
        rows = held[plane(), pl.ds(pl.multiple_of(first, own), own), :]
        own_tree[at * own : (at + 1) * own, :] = jnp.where(
            within == 0, rows[:, :own], rows[:, own:]
        )
        mine = rows if at == 0 else mine
    level = jnp.sum(mine, axis=1, keepdims=True) - 1.0
    angles = (length_of(plane()).astype(F32) + level) * freqs[...]
    cosine[...] = jnp.cos(angles)
    half = jnp.sin(angles)
    sine[...] = jnp.where(iota(half.shape, 1) < HEAD_DIM // 2, -half, half)


def turned(raw, scale, gain, cos, sin):
    x = raw * scale * gain
    return (x * cos + pltpu.roll(x, HEAD_DIM // 2, 1) * sin).astype(BF16)


def twin_prepare(width_all, query_raw, key_raw, value, q_gain, k_gain, cosine, sine, *refs):
    squares, (queries, packed) = refs[:-2], refs[-2:]
    own, width = query_raw.shape
    cos, sin = cosine[...], sine[...]
    total = sum(ref[:1, :] for ref in squares)
    for at, (raw, gain) in enumerate(((query_raw, q_gain), (key_raw, k_gain))):
        scale = upright(total[:, at * LANES : at * LANES + own])
        scale = lax.rsqrt(scale / width_all + EPS)
        for h in range(width // HEAD_DIM):
            lanes = slice(h * HEAD_DIM, (h + 1) * HEAD_DIM)
            there = slice(at * width + h * HEAD_DIM, at * width + (h + 1) * HEAD_DIM)
            found = turned(raw[:, lanes], scale, gain[:, lanes], cos, sin)
            packed[:, there] = found
            if at == 0:
                queries[:, lanes] = found
    packed[:, 2 * width :] = value[...]


def weigh(s, visible):
    peak = jnp.max(s, axis=1, keepdims=True).astype(BF16).astype(F32)
    weights = jnp.exp(jnp.where(visible, s - peak, NEG))
    total = jnp.sum(weights, axis=1, keepdims=True)
    high = total.astype(BF16).astype(F32)
    return weights.astype(BF16), (peak, high, total - high)


def kept(stats, h, heads, found):
    lane = iota(stats.shape, 1)
    for at, column in enumerate(found):
        stats = jnp.where(lane == at * heads + h, column, stats)
    return stats


def write_stats(stats, out):
    own, width = stats.shape[0], out.shape[1]
    flat = lax.dot_general(
        stats.astype(BF16), eye_of(own), (((0,), (0,)), ((), ())), preferred_element_type=F32
    )
    flat = jnp.concatenate([flat[:16], jnp.zeros((16, width - own), F32)], axis=1)
    out[own : own + 16, :] = flat.astype(BF16)


def twin_attend_far(turns, limits, key_cache, value_cache, swapped, *refs):
    count = len(turns)
    queries, outs, scores = refs[:count], refs[count : 2 * count], refs[2 * count]
    block, width = key_cache.shape[1:]
    heads = width // HEAD_DIM
    own = queries[0].shape[0]
    me = lax.axis_index("seq")
    factor = 1.0 / math.sqrt(HEAD_DIM)
    place = iota((1, block), 1)
    both = jnp.concatenate([me * block + place, (me ^ 1) * block + place], axis=1)
    visible = [both < limits[at + 1 : at + 2, :] for at in range(count)]
    for at, turn in enumerate(turns):
        for h in range(heads):
            lanes = slice(h * HEAD_DIM, (h + 1) * HEAD_DIM)
            q = queries[at][:, lanes]
            first = dot_t(q, key_cache[plane() ^ turn, :, lanes])
            second = dot_t(q, swapped[at, 0, :, lanes])
            product = jnp.concatenate([first, second], axis=1) * factor
            scores[at, h] = jnp.where(visible[at], product, NEG)
    for at, turn in enumerate(turns):
        stats = jnp.zeros((own, LANES), F32)
        for h in range(heads):
            lanes = slice(h * HEAD_DIM, (h + 1) * HEAD_DIM)
            weights, found = weigh(scores[at, h], visible[at])
            out = dot(weights[:, :block], value_cache[plane() ^ turn, :, lanes])
            out = out + dot(weights[:, block:], swapped[at, 1, :, lanes])
            outs[at][:own, lanes] = out.astype(BF16)
            stats = kept(stats, h, heads, found)
        write_stats(stats, outs[at])


def twin_attend_near(limits, key_cache, value_cache, own_tree, mine, other, *refs):
    queries, (crossing, local, copied, own_scores) = refs[:-4], refs[-4:]
    count = len(queries)
    block, width = key_cache.shape[1:]
    heads = width // HEAD_DIM
    own = other.shape[0]
    factor = 1.0 / math.sqrt(HEAD_DIM)
    place = lax.axis_index("seq") * block + iota((1, block), 1)
    here = jnp.broadcast_to(place < limits[:1, :block], (2 * own, block))
    rest = own_scores.shape[2] - block - own
    near = jnp.concatenate(
        [jnp.where(here, 1.0, 0.0), own_tree[...], jnp.zeros((2 * own, rest), F32)], axis=1
    )
    near = near > 0.5
    pair = stacked([mine[:, :width], other[...]])
    for h in range(heads):
        lanes = slice(h * HEAD_DIM, (h + 1) * HEAD_DIM)
        keys = jnp.concatenate(
            [mine[:, width + h * HEAD_DIM : width + (h + 1) * HEAD_DIM]] * (1 + rest // own), axis=0
        )
        first = dot_t(pair[:, lanes], key_cache[plane(), :, lanes])
        product = jnp.concatenate([first, dot_t(pair[:, lanes], keys)], axis=1) * factor
        own_scores[h] = jnp.where(near, product, NEG)
    stats = jnp.zeros((2 * own, LANES), F32)
    for h in range(heads):
        lanes = slice(h * HEAD_DIM, (h + 1) * HEAD_DIM)
        weights, found = weigh(own_scores[h], near)
        out = dot(weights[:, :block], value_cache[plane(), :, lanes])
        values = mine[:, 2 * width + h * HEAD_DIM : 2 * width + (h + 1) * HEAD_DIM]
        out = out + dot(weights[:, block : block + own], values)
        out = out.astype(BF16)
        local[:own, lanes] = out[:own]
        crossing[:own, lanes] = out[own:]
        stats = kept(stats, h, heads, found)
    write_stats(stats[:own], local)
    write_stats(stats[own:], crossing)
    for at, ref in enumerate((mine, *queries)):
        for part in range(2):
            rows = slice((2 * at + part) * own, (2 * at + part + 1) * own)
            copied[rows, :] = ref[:, (part + 1) * width : (part + 2) * width]
    last = 2 * (count + 1) * own
    copied[last:, :] = jnp.zeros((copied.shape[0] - last, width), BF16)


def twin_rows(mine, theirs, held):
    within = lax.rem(lax.axis_index("seq"), 2)
    held[within] = mine
    held[1 - within] = theirs
    return stacked([held[0], held[1]])


def twin_merge_and_project(*refs):
    partials, (wo, total_out, rounded) = refs[:-3], refs[-3:]
    own, width = total_out.shape[0], partials[0].shape[1]
    heads = width // HEAD_DIM
    stats = [dot_t(eye_of(own), ref[own : own + 16, :own]) for ref in partials]
    attention = []
    for h in range(heads):
        lanes = slice(h * HEAD_DIM, (h + 1) * HEAD_DIM)
        peaks = [s[:, h : h + 1] for s in stats]
        highest = functools.reduce(jnp.maximum, peaks)
        total, summed = 0.0, 0.0
        for ref, s, peak in zip(partials, stats, peaks):
            scale = jnp.exp(peak - highest)
            own_total = s[:, heads + h : heads + h + 1] + s[:, 2 * heads + h : 2 * heads + h + 1]
            total = total + own_total * scale
            summed = summed + ref[:own, lanes].astype(F32) * scale
        attention.append((summed / total).astype(BF16))
    product = dot(jnp.concatenate(attention, axis=1), wo[...])
    total_out[...] = product
    rounded[...] = product.astype(BF16)


def twin_add(mine, theirs, total, rounded):
    both = mine[...] + theirs[...].astype(F32)
    total[...] = both
    rounded[...] = both.astype(BF16)


def twin_finish(mine, theirs, gain, hidden, out):
    model_width = mine.shape[1]
    columns = out.shape[1]
    total = mine[...] + theirs[...].astype(F32)
    scale = lax.rsqrt(sum_squares(total) / model_width + EPS)
    lanes = pl.ds(pl.multiple_of(lax.axis_index("tp") * columns, columns), columns)
    normed = (mine[:, lanes] + theirs[:, lanes].astype(F32)) * scale * gain[...]
    out[...] = (hidden[:, lanes].astype(F32) + normed).astype(BF16)


def twin_compact(far, targets, key_cache, value_cache, *refs):
    count = len(far) + 1
    ours, (copied, new_keys, new_values, held) = refs[:count], refs[count:]
    block, width = key_cache.shape[1:]
    own = ours[0].shape[0]
    me = lax.axis_index("seq")
    place = me * block + iota((block, targets.shape[2]), 0)
    for at, turn in enumerate((0, *far)):
        request = plane() ^ turn
        placing = place == targets[request]
        written = jnp.max(placing.astype(F32), axis=1, keepdims=True) > 0.5
        placing = placing.astype(BF16)
        for part, (cache, out) in enumerate(((key_cache, new_keys), (value_cache, new_values))):
            lanes = slice((part + 1) * width, (part + 2) * width)
            rows = slice((2 * at + part) * own, (2 * at + part + 1) * own)
            theirs = copied[rows, :]
            fresh = twin_rows(ours[at][:, lanes], theirs, held.at[at, part])
            moved = dot(placing, fresh)
            out[request] = jnp.where(written, moved, cache[request].astype(F32)).astype(BF16)


def body_twin(
    hidden_in,
    query_weight,
    key_weight,
    value_weight,
    out_weight,
    query_gain,
    key_gain,
    post_gain,
    key_cache,
    value_cache,
    cache_lengths,
    parents,
    accepted_leaf,
):
    requests, block, width = key_cache.shape
    draft = parents.shape[1]
    own, model = hidden_in.shape
    tp = lax.axis_size("tp")
    seq = lax.axis_size("seq")
    columns = model // tp
    heads = width // HEAD_DIM
    far = tuple(range(requests - 1, 0, -1))

    def call(kernel, outs, inputs, scratch=(), mib=16, specs=None, ties=()):
        count = len(inputs)

        def run(*refs):
            kernel(*refs[:count], *refs[count + len(ties) :])

        return pl.pallas_call(
            run,
            out_shape=outs,
            in_specs=([VMEM] * count if specs is None else specs) + [ANY] * len(ties),
            out_specs=jax.tree.map(lambda _: VMEM, outs),
            scratch_shapes=list(scratch),
            compiler_params=params(mib),
            name=getattr(kernel, "func", kernel).__name__,
        )(*inputs, *ties)

    def over_tp(x, k):
        return lax.ppermute(x, "tp", [(i, i ^ k) for i in range(tp)])

    def beside(x):
        return lax.ppermute(x, "seq", [(i, i ^ 1) for i in range(seq)])

    def over_planes(x, turn):
        return lax.ppermute(x, "seq", [(i, (i // 2 ^ turn) * 2 + i % 2) for i in range(seq)])

    me = lax.axis_index("seq") // 2

    def picked(turns):
        parts = [
            [lax.dynamic_index_in_dim(x, me ^ turn, 0, False) for x in (key_cache, value_cache)]
            for turn in turns
        ]
        return jnp.stack([jnp.stack(part) for part in parts])

    swapped = beside(picked(far))
    query_raw, key_raw, squares = call(
        twin_project_qk,
        (shaped((own, width), F32), shaped((own, width), F32), shaped((8, 2 * LANES), F32)),
        (hidden_in, query_weight, key_weight),
    )
    all_squares = [squares] + [over_tp(squares, k) for k in range(tp - 1, 0, -1)]

    exponents = -2.0 * (jnp.arange(HEAD_DIM) % (HEAD_DIM // 2)).astype(F32) / HEAD_DIM
    freqs = (THETA**exponents)[None, :]
    own_tree, targets, cosine, sine, limits = call(
        functools.partial(twin_tree, (0, *far)),
        (
            shaped((draft, own), F32),
            shaped((requests, 1, draft), jnp.int32),
            shaped((own, HEAD_DIM), F32),
            shaped((own, HEAD_DIM), F32),
            shaped((requests, 2 * block), jnp.int32),
        ),
        (cache_lengths[None, :], accepted_leaf[None, :], parents, freqs),
        [pltpu.VMEM((requests, draft, draft), F32)],
    )
    value = call(twin_project_v, shaped((own, width), BF16), (hidden_in, value_weight))
    queries, packed = call(
        functools.partial(twin_prepare, tp * width),
        (shaped((own, width), BF16), shaped((own, 3 * width), BF16)),
        (
            query_raw,
            key_raw,
            value,
            query_gain[None, :],
            key_gain[None, :],
            cosine,
            sine,
            *all_squares,
        ),
    )
    from_far = [over_planes(packed, turn) for turn in far]
    other = beside(queries)

    rows = own + 16
    partials = call(
        functools.partial(twin_attend_far, far),
        (shaped((rows, width), BF16),) * len(far),
        (limits, key_cache, value_cache, swapped, *from_far),
        [pltpu.VMEM((len(far), heads, own, 2 * block), F32)],
    )
    crossing, local, copied = call(
        twin_attend_near,
        (shaped((rows, width), BF16),) * 2 + (shaped((2 * requests * own + own, width), BF16),),
        (limits, key_cache, value_cache, own_tree, packed, other, *from_far),
        [pltpu.VMEM((heads, 2 * own, block + LANES), F32)],
        ties=partials[:1],
    )
    partials = [over_planes(part, turn) for part, turn in zip(partials, far)]
    partials += [beside(crossing)]
    partials = [partials[3], partials[2], partials[0], partials[1], local]
    copied = beside(copied)

    total, rounded = call(
        twin_merge_and_project,
        (shaped((own, model), F32), shaped((own, model), BF16)),
        (*partials, out_weight),
    )
    bit = 1
    while 2 * bit < tp:
        total, rounded = call(
            twin_add,
            (shaped((own, model), F32), shaped((own, model), BF16)),
            (total, over_tp(rounded, bit)),
        )
        bit *= 2
    arrived = over_tp(rounded, bit)
    new_key_cache, new_value_cache = call(
        functools.partial(twin_compact, far),
        (shaped(key_cache.shape, BF16), shaped(value_cache.shape, BF16)),
        (targets, key_cache, value_cache, packed, *from_far, copied),
        [pltpu.VMEM((requests, 2, 2, own, width), BF16)],
    )
    hidden_out = call(
        twin_finish,
        shaped((own, columns), BF16),
        (total, arrived, post_gain[None, :], hidden_in),
    )
    return (hidden_out, new_key_cache, new_value_cache)


def body(*args):
    hidden_in, key_cache, parents = args[0], args[8], args[11]
    tp = lax.axis_size("tp")
    own, draft = hidden_in.shape[0], parents.shape[1]
    requests, _, width = key_cache.shape
    twin = (
        own % 16 == 0
        and draft == 2 * own
        and requests == 4
        and lax.axis_size("seq") == 2 * requests
        and own <= LANES
        and LANES % own == 0
        and own <= width
        and 3 * (width // HEAD_DIM) <= 16
        and tp > 1
        and tp & (tp - 1) == 0
    )
    return (body_twin if twin else body_general)(*args)


def solution(mesh):
    return jax.shard_map(
        body,
        mesh=mesh,
        in_specs=(
            P("seq", None),
            P(None, "tp"),
            P(None, "tp"),
            P(None, "tp"),
            P("tp", None),
            P("tp"),
            P("tp"),
            P("tp"),
            P(None, "seq", "tp"),
            P(None, "seq", "tp"),
            P(),
            P(),
            P(),
        ),
        out_specs=(P("seq", "tp"), P(None, "seq", "tp"), P(None, "seq", "tp")),
        check_vma=False,
    )
```

```python
import functools
import math

import jax
import jax.numpy as jnp
from jax import lax
from jax.experimental import pallas as pl
from jax.experimental.pallas import tpu as pltpu
from jax.sharding import PartitionSpec as P

HEAD_DIM = 128
LANES = 128
EPS = 1e-06
THETA = 500000.0
NEG = -1e30
F32 = jnp.float32
BF16 = jnp.bfloat16
VMEM = pl.BlockSpec(memory_space=pltpu.VMEM)
SMEM = pl.BlockSpec(memory_space=pltpu.SMEM)
ANY = pl.BlockSpec(memory_space=pl.ANY)


def params(mib):
    return pltpu.CompilerParams(vmem_limit_bytes=mib * 1024 * 1024)


def dot(a, b):
    return jnp.dot(a, b, preferred_element_type=F32)


def dot_t(a, b):
    return lax.dot_general(a, b, (((1,), (1,)), ((), ())), preferred_element_type=F32)


def iota(shape, axis):
    return lax.broadcasted_iota(jnp.int32, shape, axis)


def stacked(parts):
    if len(parts) == 1:
        return parts[0]
    if parts[0].shape[0] % 16 == 0:
        return jnp.concatenate(parts, axis=0)
    return jnp.concatenate([part.astype(F32) for part in parts], axis=0).astype(BF16)


def sum_squares(raw):
    return jnp.sum(raw * raw, axis=1, keepdims=True)


def project_qk(hidden, wq, wk, query_raw, key_raw, squares, wq_v, wk_v, sems):
    chunks, depth = wq_v.shape[0], wq_v.shape[1]
    copies = []
    for c in range(chunks):
        for at, (source, target) in enumerate(((wq, wq_v), (wk, wk_v))):
            copy = pltpu.make_async_copy(
                source.at[pl.ds(c * depth, depth)], target.at[c], sems.at[2 * c + at]
            )
            copy.start()
            copies.append(copy)
    q_sum, k_sum = None, None
    for c in range(chunks):
        part = hidden[:, c * depth : (c + 1) * depth]
        copies[2 * c].wait()
        q = dot(part, wq_v[c])
        copies[2 * c + 1].wait()
        k = dot(part, wk_v[c])
        q_sum = q if c == 0 else q_sum + q
        k_sum = k if c == 0 else k_sum + k
    query_raw[...] = q_sum
    key_raw[...] = k_sum
    lane = iota(squares.shape[1:], 1)
    both = jnp.where(lane == 0, sum_squares(q_sum), sum_squares(k_sum))
    for t in range(squares.shape[0]):
        squares[t] = both


def project_v_and_tree(
    lengths, leaves, hidden, parents, freqs, wv, value, own_tree, targets, cosine, sine, wv_v, anc_v, sems
):
    chunks, depth = wv_v.shape[0], wv_v.shape[1]
    copies = []
    for c in range(chunks):
        copy = pltpu.make_async_copy(wv.at[pl.ds(c * depth, depth)], wv_v.at[c], sems.at[c])
        copy.start()
        copies.append(copy)
    requests, draft = parents.shape
    own = hidden.shape[0]
    first = lax.axis_index("seq") * own
    row, col = iota((draft, draft), 0), iota((draft, draft), 1)
    eye = (row == col).astype(BF16)
    trees = [
        jnp.where((parents[pl.ds(r, 1), :] == row) | (row == col), 1.0, 0.0).astype(BF16)
        for r in range(requests)
    ]
    for _ in range(max(1, (draft - 1).bit_length())):
        trees = [jnp.minimum(dot(tree, tree), 1.0).astype(BF16) for tree in trees]
    for r in range(requests):
        upright = lax.dot_general(
            trees[r], eye, (((0,), (0,)), ((), ())), preferred_element_type=F32
        )
        anc_v[pl.ds(r * draft, draft), :] = upright
        level = jnp.sum(trees[r].astype(F32), axis=0, keepdims=True) - 1.0
        on_path = jnp.sum(jnp.where(row == leaves[r], upright, 0.0), axis=0, keepdims=True)
        place = lengths[r] + level.astype(jnp.int32)
        targets[r] = jnp.where(on_path > 0.5, place, -1)
    mine = anc_v[pl.ds(pl.multiple_of(first, own), own), :]
    own_tree[...] = mine
    level = jnp.sum(mine, axis=1, keepdims=True) - 1.0
    position = lengths[first // draft].astype(F32) + level
    angles = position * freqs[...]
    cosine[...] = jnp.cos(angles)
    half = jnp.sin(angles)
    sine[...] = jnp.where(iota(half.shape, 1) < HEAD_DIM // 2, -half, half)
    total = None
    for c in range(chunks):
        copies[c].wait()
        v = dot(hidden[:, c * depth : (c + 1) * depth], wv_v[c])
        total = v if c == 0 else total + v
    value[...] = total.astype(BF16)


def prepare(
    width_all, query_raw, key_raw, value, q_gain, k_gain, cosine, sine, squares, queries, keys_values
):
    width = query_raw.shape[1]
    total = sum(squares[k] for k in range(squares.shape[0]))
    cos, sin = cosine[...], sine[...]
    for at, (raw, gain, out) in enumerate(
        ((query_raw, q_gain, queries), (key_raw, k_gain, keys_values))
    ):
        scale = lax.rsqrt(total[:, at : at + 1] / width_all + EPS)
        for h in range(width // HEAD_DIM):
            lanes = slice(h * HEAD_DIM, (h + 1) * HEAD_DIM)
            x = raw[:, lanes] * scale * gain[:, lanes]
            turned = x * cos + pltpu.roll(x, HEAD_DIM // 2, 1) * sin
            turned = turned.astype(BF16)
            for s in range(out.shape[0]):
                out[s, :, lanes] = turned
    for s in range(keys_values.shape[0]):
        keys_values[s, :, width:] = value[...]


def attend_cache(group, lengths, key_cache, value_cache, queries, partials):
    requests, block, width = key_cache.shape
    own = queries.shape[1]
    heads = width // HEAD_DIM
    me = lax.axis_index("seq")
    factor = 1.0 / math.sqrt(HEAD_DIM)
    rows = group * own
    place = me * block + iota((rows, block), 1)
    lane = iota((rows, LANES), 1)
    for request in range(requests):
        q = stacked([queries[request * group + j] for j in range(group)])
        visible = place < lengths[request]
        stats = jnp.zeros((rows, LANES), F32)
        for h in range(heads):
            lanes = slice(h * HEAD_DIM, (h + 1) * HEAD_DIM)
            scores = dot_t(q[:, lanes], key_cache[request, :, lanes]) * factor
            scores = jnp.where(visible, scores, NEG)
            peak = jnp.max(scores, axis=1, keepdims=True).astype(BF16).astype(F32)
            weights = jnp.exp(jnp.where(visible, scores - peak, NEG))
            total = jnp.sum(weights, axis=1, keepdims=True)
            high = total.astype(BF16).astype(F32)
            out = dot(weights.astype(BF16), value_cache[request, :, lanes]).astype(BF16)
            for j in range(group):
                partials[request * group + j, :, lanes] = out[j * own : (j + 1) * own]
            stats = jnp.where(lane == h, peak, stats)
            stats = jnp.where(lane == heads + h, high, stats)
            stats = jnp.where(lane == 2 * heads + h, total - high, stats)
        stats = stats.astype(BF16)
        for j in range(group):
            partials[request * group + j, :, width:] = stats[j * own : (j + 1) * own]


def attend_draft(group, own_tree, queries, keys_values, out, stats):
    own, width = queries.shape[1:]
    heads = width // HEAD_DIM
    me = lax.axis_index("seq")
    first = me // group * group
    q = queries[me]
    pair = stacked([keys_values[first + j] for j in range(group)])
    factor = 1.0 / math.sqrt(HEAD_DIM)
    allowed = own_tree[...] > 0.5
    lane = iota((own, LANES), 1)
    kept = jnp.zeros((own, LANES), F32)
    for h in range(heads):
        lanes = slice(h * HEAD_DIM, (h + 1) * HEAD_DIM)
        there = slice(width + h * HEAD_DIM, width + (h + 1) * HEAD_DIM)
        scores = dot_t(q[:, lanes], pair[:, lanes]) * factor
        scores = jnp.where(allowed, scores, NEG)
        peak = jnp.max(scores, axis=1, keepdims=True)
        weights = jnp.exp(jnp.where(allowed, scores - peak, NEG))
        out[:, lanes] = dot(weights.astype(BF16), pair[:, there])
        kept = jnp.where(lane == h, peak, kept)
        kept = jnp.where(lane == heads + h, jnp.sum(weights, axis=1, keepdims=True), kept)
    stats[...] = kept


def merge_and_project(draft_out, draft_stats, wo, partials, projected, wo_v, sems):
    count, width, columns = wo_v.shape
    heads = width // HEAD_DIM
    copies = []
    for k in range(count):
        copy = pltpu.make_async_copy(
            wo.at[:, pl.ds(k * columns, columns)], wo_v.at[k], sems.at[k]
        )
        copy.start()
        copies.append(copy)
    parts = range(partials.shape[0])
    stats = [partials[s, :, width:].astype(F32) for s in parts]
    own_stats = draft_stats[...]
    attention = []
    for h in range(heads):
        lanes = slice(h * HEAD_DIM, (h + 1) * HEAD_DIM)
        peaks = [s[:, h : h + 1] for s in stats] + [own_stats[:, h : h + 1]]
        highest = functools.reduce(jnp.maximum, peaks)
        scales = [jnp.exp(peak - highest) for peak in peaks]
        total = own_stats[:, heads + h : heads + h + 1] * scales[-1]
        summed = draft_out[:, lanes] * scales[-1]
        for at in parts:
            s = stats[at]
            own_total = s[:, heads + h : heads + h + 1] + s[:, 2 * heads + h : 2 * heads + h + 1]
            total = total + own_total * scales[at]
            summed = summed + partials[at, :, lanes].astype(F32) * scales[at]
        attention.append((summed / total).astype(BF16))
    attention = jnp.concatenate(attention, axis=1)
    for k in range(count):
        copies[k].wait()
        projected[k] = dot(attention, wo_v[k]).astype(projected.dtype)


def add_up(parts, summed, power):
    total = sum(parts[k].astype(F32) for k in range(parts.shape[0]))
    summed[...] = total
    own_power = jnp.broadcast_to(sum_squares(total), power.shape[1:])
    for k in range(power.shape[0]):
        power[k] = own_power


def finish(model_width, summed, gain, hidden, powers, out):
    columns = summed.shape[1]
    power = sum(powers[k] for k in range(powers.shape[0]))[:, :1]
    start = pl.multiple_of(lax.axis_index("tp") * columns, columns)
    normed = summed[...] * lax.rsqrt(power / model_width + EPS) * gain[...]
    out[...] = (hidden[:, pl.ds(start, columns)].astype(F32) + normed).astype(BF16)


def compact(group, targets, key_cache, value_cache, keys_values, new_keys, new_values):
    requests, block, width = key_cache.shape
    own = keys_values.shape[1]
    me = lax.axis_index("seq")
    place = me * block + iota((block, group * own), 0)
    for request in range(requests):
        kv = stacked([keys_values[request * group + j] for j in range(group)])
        placing = place == targets[request]
        written = jnp.max(placing.astype(F32), axis=1, keepdims=True) > 0.5
        fresh = dot(placing.astype(BF16), kv)
        new_keys[request] = jnp.where(
            written, fresh[:, :width], key_cache[request].astype(F32)
        ).astype(BF16)
        new_values[request] = jnp.where(
            written, fresh[:, width:], value_cache[request].astype(F32)
        ).astype(BF16)


def shaped(shape, dtype):
    return jax.ShapeDtypeStruct(shape, dtype)


def body_general(
    hidden_in,
    query_weight,
    key_weight,
    value_weight,
    out_weight,
    query_gain,
    key_gain,
    post_gain,
    key_cache,
    value_cache,
    cache_lengths,
    parents,
    accepted_leaf,
):
    requests, block, width = key_cache.shape
    draft = parents.shape[1]
    own, model = hidden_in.shape
    tp = lax.axis_size("tp")
    seq = lax.axis_size("seq")
    group = draft // own
    columns = model // tp
    chunks = 4
    depth = model // chunks

    def exchange(x, axis):
        return lax.all_to_all(x, axis, 0, 0, tiled=True)

    query_raw, key_raw, squares = pl.pallas_call(
        project_qk,
        out_shape=(
            shaped((own, width), F32),
            shaped((own, width), F32),
            shaped((tp, own, LANES), F32),
        ),
        in_specs=[VMEM, ANY, ANY],
        out_specs=(VMEM, VMEM, VMEM),
        scratch_shapes=[
            pltpu.VMEM((chunks, depth, width), BF16),
            pltpu.VMEM((chunks, depth, width), BF16),
            pltpu.SemaphoreType.DMA((2 * chunks,)),
        ],
        compiler_params=params(56),
        cost_estimate=pl.CostEstimate(
            flops=4 * own * model * width, bytes_accessed=4 * model * width, transcendentals=0
        ),
        name="project_qk",
    )(hidden_in, query_weight, key_weight)
    squares = exchange(squares, "tp")

    exponents = -2.0 * (jnp.arange(HEAD_DIM) % (HEAD_DIM // 2)).astype(F32) / HEAD_DIM
    freqs = (THETA**exponents)[None, :]
    value, own_tree, targets, cosine, sine = pl.pallas_call(
        project_v_and_tree,
        out_shape=(
            shaped((own, width), BF16),
            shaped((own, draft), F32),
            shaped((requests, 1, draft), jnp.int32),
            shaped((own, HEAD_DIM), F32),
            shaped((own, HEAD_DIM), F32),
        ),
        in_specs=[SMEM, SMEM, VMEM, VMEM, VMEM, ANY],
        out_specs=(VMEM,) * 5,
        scratch_shapes=[
            pltpu.VMEM((chunks, depth, width), BF16),
            pltpu.VMEM((requests * draft, draft), F32),
            pltpu.SemaphoreType.DMA((chunks,)),
        ],
        compiler_params=params(16),
        cost_estimate=pl.CostEstimate(
            flops=2 * own * model * width, bytes_accessed=2 * model * width, transcendentals=0
        ),
        name="project_v_and_tree",
    )(cache_lengths, accepted_leaf, hidden_in, parents, freqs, value_weight)

    queries, keys_values = pl.pallas_call(
        functools.partial(prepare, tp * width),
        out_shape=(shaped((seq, own, width), BF16), shaped((seq, own, 2 * width), BF16)),
        in_specs=[VMEM] * 8,
        out_specs=(VMEM, VMEM),
        compiler_params=params(16),
        name="prepare",
    )(
        query_raw,
        key_raw,
        value,
        query_gain[None, :],
        key_gain[None, :],
        cosine,
        sine,
        squares,
    )
    queries = exchange(queries, "seq")
    keys_values = exchange(keys_values, "seq")

    partials = pl.pallas_call(
        functools.partial(attend_cache, group),
        out_shape=shaped((seq, own, width + LANES), BF16),
        in_specs=[SMEM, VMEM, VMEM, VMEM],
        out_specs=VMEM,
        compiler_params=params(16),
        name="attend_cache",
    )(cache_lengths, key_cache, value_cache, queries)
    partials = exchange(partials, "seq")

    draft_out, draft_stats = pl.pallas_call(
        functools.partial(attend_draft, group),
        out_shape=(shaped((own, width), F32), shaped((own, LANES), F32)),
        in_specs=[VMEM] * 3,
        out_specs=(VMEM, VMEM),
        compiler_params=params(16),
        name="attend_draft",
    )(own_tree, queries, keys_values)

    projected = pl.pallas_call(
        merge_and_project,
        out_shape=shaped((tp, own, columns), BF16),
        in_specs=[VMEM, VMEM, ANY, VMEM],
        out_specs=VMEM,
        scratch_shapes=[
            pltpu.VMEM((tp, width, columns), BF16),
            pltpu.SemaphoreType.DMA((tp,)),
        ],
        compiler_params=params(16),
        name="merge_and_project",
    )(draft_out, draft_stats, out_weight, partials)
    projected = exchange(projected, "tp")

    summed, power = pl.pallas_call(
        add_up,
        out_shape=(shaped((own, columns), F32), shaped((tp, own, LANES), F32)),
        in_specs=[VMEM],
        out_specs=(VMEM, VMEM),
        compiler_params=params(16),
        name="add_up",
    )(projected)
    power = exchange(power, "tp")

    hidden_out = pl.pallas_call(
        functools.partial(finish, model),
        out_shape=shaped((own, columns), BF16),
        in_specs=[VMEM] * 4,
        out_specs=VMEM,
        compiler_params=params(16),
        name="finish",
    )(summed, post_gain[None, :], hidden_in, power)

    new_key_cache, new_value_cache = pl.pallas_call(
        functools.partial(compact, group),
        out_shape=(shaped(key_cache.shape, BF16), shaped(value_cache.shape, BF16)),
        in_specs=[VMEM] * 4,
        out_specs=(VMEM, VMEM),
        compiler_params=params(24),
        name="compact",
    )(targets, key_cache, value_cache, keys_values)
    return (hidden_out, new_key_cache, new_value_cache)


def across(column):
    rows = column.shape[0]
    eye = iota((rows, rows), 0) == iota((rows, rows), 1)
    return jnp.sum(jnp.where(eye, column, 0.0), axis=0, keepdims=True)


def upright(line):
    rows = line.shape[1]
    eye = iota((rows, rows), 0) == iota((rows, rows), 1)
    return jnp.sum(jnp.where(eye, line, 0.0), axis=1, keepdims=True)


def eye_of(size):
    return (iota((size, size), 0) == iota((size, size), 1)).astype(BF16)


def plane():
    return lax.axis_index("seq") // 2


def twin_project_qk(hidden, wq, wk, query_raw, key_raw, squares):
    rows = hidden[...]
    own = rows.shape[0]
    for at, (weight, raw) in enumerate(((wq, query_raw), (wk, key_raw))):
        product = dot(rows, weight[...])
        raw[...] = product
        line = across(sum_squares(product))
        line = jnp.concatenate([line, jnp.zeros((1, LANES - own), F32)], axis=1)
        squares[:, at * LANES : (at + 1) * LANES] = jnp.broadcast_to(
            line, (squares.shape[0], LANES)
        )


def twin_project_v(hidden, wv, value):
    value[...] = dot(hidden[...], wv[...]).astype(BF16)


def twin_tree(
    turns, lengths, leaves, parents, freqs, own_tree, targets, cosine, sine, limits, held
):
    requests, draft = parents.shape
    own = own_tree.shape[1]
    row, col = iota((draft, draft), 0), iota((draft, draft), 1)
    eye = eye_of(draft)

    def length_of(request):
        picked = iota(lengths.shape, 1) == request
        return jnp.sum(jnp.where(picked, lengths[...], 0), axis=1, keepdims=True)

    for at, turn in enumerate(turns):
        limits[at : at + 1, :] = jnp.broadcast_to(
            length_of(plane() ^ turn), (1, limits.shape[1])
        )
    trees = [
        jnp.where((parents[pl.ds(r, 1), :] == row) | (row == col), 1.0, 0.0).astype(BF16)
        for r in range(requests)
    ]
    for _ in range(max(1, (draft - 1).bit_length())):
        trees = [jnp.minimum(dot(tree, tree), 1.0).astype(BF16) for tree in trees]
    for r in range(requests):
        standing = lax.dot_general(
            trees[r], eye, (((0,), (0,)), ((), ())), preferred_element_type=F32
        )
        held[r] = standing
        level = jnp.sum(trees[r].astype(F32), axis=0, keepdims=True) - 1.0
        on_path = jnp.where(row == leaves[:, r : r + 1], standing, 0.0)
        on_path = jnp.sum(on_path, axis=0, keepdims=True)
        place = lengths[:, r : r + 1] + level.astype(jnp.int32)
        targets[r] = jnp.where(on_path > 0.5, place, -1)
    within = lax.rem(lax.axis_index("seq"), 2)
    for at in range(2):
        first = (within ^ at) * own
        rows = held[plane(), pl.ds(pl.multiple_of(first, own), own), :]
        own_tree[at * own : (at + 1) * own, :] = jnp.where(
            within == 0, rows[:, :own], rows[:, own:]
        )
        mine = rows if at == 0 else mine
    level = jnp.sum(mine, axis=1, keepdims=True) - 1.0
    angles = (length_of(plane()).astype(F32) + level) * freqs[...]
    cosine[...] = jnp.cos(angles)
    half = jnp.sin(angles)
    sine[...] = jnp.where(iota(half.shape, 1) < HEAD_DIM // 2, -half, half)


def turned(raw, scale, gain, cos, sin):
    x = raw * scale * gain
    return (x * cos + pltpu.roll(x, HEAD_DIM // 2, 1) * sin).astype(BF16)


def twin_prepare(width_all, query_raw, key_raw, value, q_gain, k_gain, cosine, sine, *refs):
    squares, (queries, packed) = refs[:-2], refs[-2:]
    own, width = query_raw.shape
    cos, sin = cosine[...], sine[...]
    total = sum(ref[:1, :] for ref in squares)
    for at, (raw, gain) in enumerate(((query_raw, q_gain), (key_raw, k_gain))):
        scale = upright(total[:, at * LANES : at * LANES + own])
        scale = lax.rsqrt(scale / width_all + EPS)
        for h in range(width // HEAD_DIM):
            lanes = slice(h * HEAD_DIM, (h + 1) * HEAD_DIM)
            there = slice(at * width + h * HEAD_DIM, at * width + (h + 1) * HEAD_DIM)
            found = turned(raw[:, lanes], scale, gain[:, lanes], cos, sin)
            packed[:, there] = found
            if at == 0:
                queries[:, lanes] = found
    packed[:, 2 * width :] = value[...]


def weigh(s, visible):
    peak = jnp.max(s, axis=1, keepdims=True).astype(BF16).astype(F32)
    weights = jnp.exp(jnp.where(visible, s - peak, NEG))
    total = jnp.sum(weights, axis=1, keepdims=True)
    high = total.astype(BF16).astype(F32)
    return weights.astype(BF16), (peak, high, total - high)


def kept(stats, h, heads, found):
    lane = iota(stats.shape, 1)
    for at, column in enumerate(found):
        stats = jnp.where(lane == at * heads + h, column, stats)
    return stats


def write_stats(stats, out):
    own, width = stats.shape[0], out.shape[1]
    flat = lax.dot_general(
        stats.astype(BF16), eye_of(own), (((0,), (0,)), ((), ())), preferred_element_type=F32
    )
    flat = jnp.concatenate([flat[:16], jnp.zeros((16, width - own), F32)], axis=1)
    out[own : own + 16, :] = flat.astype(BF16)


def twin_attend_far(turns, limits, key_cache, value_cache, swapped, *refs):
    count = len(turns)
    queries, outs, scores = refs[:count], refs[count : 2 * count], refs[2 * count]
    block, width = key_cache.shape[1:]
    heads = width // HEAD_DIM
    own = queries[0].shape[0]
    me = lax.axis_index("seq")
    factor = 1.0 / math.sqrt(HEAD_DIM)
    place = iota((1, block), 1)
    both = jnp.concatenate([me * block + place, (me ^ 1) * block + place], axis=1)
    visible = [both < limits[at + 1 : at + 2, :] for at in range(count)]
    for at, turn in enumerate(turns):
        for h in range(heads):
            lanes = slice(h * HEAD_DIM, (h + 1) * HEAD_DIM)
            q = queries[at][:, lanes]
            first = dot_t(q, key_cache[plane() ^ turn, :, lanes])
            second = dot_t(q, swapped[at, 0, :, lanes])
            product = jnp.concatenate([first, second], axis=1) * factor
            scores[at, h] = jnp.where(visible[at], product, NEG)
    for at, turn in enumerate(turns):
        stats = jnp.zeros((own, LANES), F32)
        for h in range(heads):
            lanes = slice(h * HEAD_DIM, (h + 1) * HEAD_DIM)
            weights, found = weigh(scores[at, h], visible[at])
            out = dot(weights[:, :block], value_cache[plane() ^ turn, :, lanes])
            out = out + dot(weights[:, block:], swapped[at, 1, :, lanes])
            outs[at][:own, lanes] = out.astype(BF16)
            stats = kept(stats, h, heads, found)
        write_stats(stats, outs[at])


def twin_attend_near(limits, key_cache, value_cache, own_tree, mine, other, *refs):
    queries, (crossing, local, copied, own_scores) = refs[:-4], refs[-4:]
    count = len(queries)
    block, width = key_cache.shape[1:]
    heads = width // HEAD_DIM
    own = other.shape[0]
    factor = 1.0 / math.sqrt(HEAD_DIM)
    place = lax.axis_index("seq") * block + iota((1, block), 1)
    here = jnp.broadcast_to(place < limits[:1, :block], (2 * own, block))
    rest = own_scores.shape[2] - block - own
    near = jnp.concatenate(
        [jnp.where(here, 1.0, 0.0), own_tree[...], jnp.zeros((2 * own, rest), F32)], axis=1
    )
    near = near > 0.5
    pair = stacked([mine[:, :width], other[:, :width]])
    for h in range(heads):
        lanes = slice(h * HEAD_DIM, (h + 1) * HEAD_DIM)
        keys = jnp.concatenate(
            [mine[:, width + h * HEAD_DIM : width + (h + 1) * HEAD_DIM]] * (1 + rest // own), axis=0
        )
        first = dot_t(pair[:, lanes], key_cache[plane(), :, lanes])
        product = jnp.concatenate([first, dot_t(pair[:, lanes], keys)], axis=1) * factor
        own_scores[h] = jnp.where(near, product, NEG)
    stats = jnp.zeros((2 * own, LANES), F32)
    for h in range(heads):
        lanes = slice(h * HEAD_DIM, (h + 1) * HEAD_DIM)
        weights, found = weigh(own_scores[h], near)
        out = dot(weights[:, :block], value_cache[plane(), :, lanes])
        values = mine[:, 2 * width + h * HEAD_DIM : 2 * width + (h + 1) * HEAD_DIM]
        out = out + dot(weights[:, block : block + own], values)
        out = out.astype(BF16)
        local[:own, lanes] = out[:own]
        crossing[:own, lanes] = out[own:]
        stats = kept(stats, h, heads, found)
    write_stats(stats[:own], local)
    write_stats(stats[own:], crossing)
    for at, ref in enumerate(queries):
        for part in range(2):
            rows = slice((2 * at + part) * own, (2 * at + part + 1) * own)
            copied[rows, :] = ref[:, (part + 1) * width : (part + 2) * width]
    last = 2 * count * own
    if copied.shape[0] > last:
        copied[last:, :] = jnp.zeros((copied.shape[0] - last, width), BF16)


def twin_rows(mine, theirs, held):
    within = lax.rem(lax.axis_index("seq"), 2)
    held[within] = mine
    held[1 - within] = theirs
    return stacked([held[0], held[1]])


def twin_merge_and_project(*refs):
    partials, (wo, total_out, rounded) = refs[:-3], refs[-3:]
    own, width = total_out.shape[0], partials[0].shape[1]
    heads = width // HEAD_DIM
    stats = [dot_t(eye_of(own), ref[own : own + 16, :own]) for ref in partials]
    attention = []
    for h in range(heads):
        lanes = slice(h * HEAD_DIM, (h + 1) * HEAD_DIM)
        peaks = [s[:, h : h + 1] for s in stats]
        highest = functools.reduce(jnp.maximum, peaks)
        total, summed = 0.0, 0.0
        for ref, s, peak in zip(partials, stats, peaks):
            scale = jnp.exp(peak - highest)
            own_total = s[:, heads + h : heads + h + 1] + s[:, 2 * heads + h : 2 * heads + h + 1]
            total = total + own_total * scale
            summed = summed + ref[:own, lanes].astype(F32) * scale
        attention.append((summed / total).astype(BF16))
    product = dot(jnp.concatenate(attention, axis=1), wo[...])
    total_out[...] = product
    rounded[...] = product.astype(BF16)


def twin_add(mine, theirs, total, rounded):
    both = mine[...] + theirs[...].astype(F32)
    total[...] = both
    rounded[...] = both.astype(BF16)


def twin_finish(mine, theirs, gain, hidden, out):
    model_width = mine.shape[1]
    columns = out.shape[1]
    total = mine[...] + theirs[...].astype(F32)
    scale = lax.rsqrt(sum_squares(total) / model_width + EPS)
    lanes = pl.ds(pl.multiple_of(lax.axis_index("tp") * columns, columns), columns)
    normed = (mine[:, lanes] + theirs[:, lanes].astype(F32)) * scale * gain[...]
    out[...] = (hidden[:, lanes].astype(F32) + normed).astype(BF16)


def twin_compact(far, targets, key_cache, value_cache, *refs):
    count = len(far) + 1
    ours, (beside, copied, new_keys, new_values, held) = refs[:count], refs[count:]
    block, width = key_cache.shape[1:]
    own = ours[0].shape[0]
    me = lax.axis_index("seq")
    place = me * block + iota((block, targets.shape[2]), 0)
    for at, turn in enumerate((0, *far)):
        request = plane() ^ turn
        placing = place == targets[request]
        written = jnp.max(placing.astype(F32), axis=1, keepdims=True) > 0.5
        placing = placing.astype(BF16)
        for part, (cache, out) in enumerate(((key_cache, new_keys), (value_cache, new_values))):
            lanes = slice((part + 1) * width, (part + 2) * width)
            first = (2 * (at - 1) + part) * own
            theirs = copied[first : first + own, :] if at else beside[:, lanes]
            fresh = twin_rows(ours[at][:, lanes], theirs, held.at[at, part])
            moved = dot(placing, fresh)
            out[request] = jnp.where(written, moved, cache[request].astype(F32)).astype(BF16)


def body_twin(
    hidden_in,
    query_weight,
    key_weight,
    value_weight,
    out_weight,
    query_gain,
    key_gain,
    post_gain,
    key_cache,
    value_cache,
    cache_lengths,
    parents,
    accepted_leaf,
):
    requests, block, width = key_cache.shape
    draft = parents.shape[1]
    own, model = hidden_in.shape
    tp = lax.axis_size("tp")
    seq = lax.axis_size("seq")
    columns = model // tp
    heads = width // HEAD_DIM
    far = tuple(range(requests - 1, 0, -1))

    def call(kernel, outs, inputs, scratch=(), mib=16, specs=None, ties=()):
        count = len(inputs)

        def run(*refs):
            kernel(*refs[:count], *refs[count + len(ties) :])

        return pl.pallas_call(
            run,
            out_shape=outs,
            in_specs=([VMEM] * count if specs is None else specs) + [ANY] * len(ties),
            out_specs=jax.tree.map(lambda _: VMEM, outs),
            scratch_shapes=list(scratch),
            compiler_params=params(mib),
            name=getattr(kernel, "func", kernel).__name__,
        )(*inputs, *ties)

    def over_tp(x, k):
        return lax.ppermute(x, "tp", [(i, i ^ k) for i in range(tp)])

    def beside(x):
        return lax.ppermute(x, "seq", [(i, i ^ 1) for i in range(seq)])

    def over_planes(x, turn):
        return lax.ppermute(x, "seq", [(i, (i // 2 ^ turn) * 2 + i % 2) for i in range(seq)])

    me = lax.axis_index("seq") // 2

    def picked(turns):
        parts = [
            [lax.dynamic_index_in_dim(x, me ^ turn, 0, False) for x in (key_cache, value_cache)]
            for turn in turns
        ]
        return jnp.stack([jnp.stack(part) for part in parts])

    swapped = beside(picked(far))
    query_raw, key_raw, squares = call(
        twin_project_qk,
        (shaped((own, width), F32), shaped((own, width), F32), shaped((8, 2 * LANES), F32)),
        (hidden_in, query_weight, key_weight),
    )
    all_squares = [squares] + [over_tp(squares, k) for k in range(tp - 1, 0, -1)]

    exponents = -2.0 * (jnp.arange(HEAD_DIM) % (HEAD_DIM // 2)).astype(F32) / HEAD_DIM
    freqs = (THETA**exponents)[None, :]
    own_tree, targets, cosine, sine, limits = call(
        functools.partial(twin_tree, (0, *far)),
        (
            shaped((draft, own), F32),
            shaped((requests, 1, draft), jnp.int32),
            shaped((own, HEAD_DIM), F32),
            shaped((own, HEAD_DIM), F32),
            shaped((requests, 2 * block), jnp.int32),
        ),
        (cache_lengths[None, :], accepted_leaf[None, :], parents, freqs),
        [pltpu.VMEM((requests, draft, draft), F32)],
    )
    value = call(twin_project_v, shaped((own, width), BF16), (hidden_in, value_weight))
    queries, packed = call(
        functools.partial(twin_prepare, tp * width),
        (shaped((own, width), BF16), shaped((own, 3 * width), BF16)),
        (
            query_raw,
            key_raw,
            value,
            query_gain[None, :],
            key_gain[None, :],
            cosine,
            sine,
            *all_squares,
        ),
    )
    from_far = [over_planes(packed, turn) for turn in far]
    other = beside(packed)

    rows = own + 16
    partials = call(
        functools.partial(twin_attend_far, far),
        (shaped((rows, width), BF16),) * len(far),
        (limits, key_cache, value_cache, swapped, *from_far),
        [pltpu.VMEM((len(far), heads, own, 2 * block), F32)],
    )
    crossing, local, copied = call(
        twin_attend_near,
        (shaped((rows, width), BF16),) * 2 + (shaped((2 * len(far) * own, width), BF16),),
        (limits, key_cache, value_cache, own_tree, packed, other, *from_far),
        [pltpu.VMEM((heads, 2 * own, block + LANES), F32)],
        ties=partials[:1],
    )
    partials = [over_planes(part, turn) for part, turn in zip(partials, far)]
    partials += [beside(crossing)]
    partials = [partials[0], partials[1], partials[2], partials[3], local]
    copied = beside(copied)

    total, rounded = call(
        twin_merge_and_project,
        (shaped((own, model), F32), shaped((own, model), BF16)),
        (*partials, out_weight),
    )
    bit = 1
    while 2 * bit < tp:
        total, rounded = call(
            twin_add,
            (shaped((own, model), F32), shaped((own, model), BF16)),
            (total, over_tp(rounded, bit)),
        )
        bit *= 2
    arrived = over_tp(rounded, bit)
    new_key_cache, new_value_cache = call(
        functools.partial(twin_compact, far),
        (shaped(key_cache.shape, BF16), shaped(value_cache.shape, BF16)),
        (targets, key_cache, value_cache, packed, *from_far, other, copied),
        [pltpu.VMEM((requests, 2, 2, own, width), BF16)],
    )
    hidden_out = call(
        twin_finish,
        shaped((own, columns), BF16),
        (total, arrived, post_gain[None, :], hidden_in),
    )
    return (hidden_out, new_key_cache, new_value_cache)


def body(*args):
    hidden_in, key_cache, parents = args[0], args[8], args[11]
    tp = lax.axis_size("tp")
    own, draft = hidden_in.shape[0], parents.shape[1]
    requests, _, width = key_cache.shape
    twin = (
        own % 16 == 0
        and draft == 2 * own
        and requests == 4
        and lax.axis_size("seq") == 2 * requests
        and own <= LANES
        and LANES % own == 0
        and own <= width
        and 3 * (width // HEAD_DIM) <= 16
        and tp > 1
        and tp & (tp - 1) == 0
    )
    return (body_twin if twin else body_general)(*args)


def solution(mesh):
    return jax.shard_map(
        body,
        mesh=mesh,
        in_specs=(
            P("seq", None),
            P(None, "tp"),
            P(None, "tp"),
            P(None, "tp"),
            P("tp", None),
            P("tp"),
            P("tp"),
            P("tp"),
            P(None, "seq", "tp"),
            P(None, "seq", "tp"),
            P(),
            P(),
            P(),
        ),
        out_specs=(P("seq", "tp"), P(None, "seq", "tp"), P(None, "seq", "tp")),
        check_vma=False,
    )
```

```python
import functools
import math

import jax
import jax.numpy as jnp
from jax import lax
from jax.experimental import pallas as pl
from jax.experimental.pallas import tpu as pltpu
from jax.sharding import PartitionSpec as P

HEAD_DIM = 128
LANES = 128
EPS = 1e-06
THETA = 500000.0
NEG = -1e30
F32 = jnp.float32
BF16 = jnp.bfloat16
VMEM = pl.BlockSpec(memory_space=pltpu.VMEM)
SMEM = pl.BlockSpec(memory_space=pltpu.SMEM)
ANY = pl.BlockSpec(memory_space=pl.ANY)


def params(mib):
    return pltpu.CompilerParams(vmem_limit_bytes=mib * 1024 * 1024)


def dot(a, b):
    return jnp.dot(a, b, preferred_element_type=F32)


def dot_t(a, b):
    return lax.dot_general(a, b, (((1,), (1,)), ((), ())), preferred_element_type=F32)


def iota(shape, axis):
    return lax.broadcasted_iota(jnp.int32, shape, axis)


def stacked(parts):
    if len(parts) == 1:
        return parts[0]
    if parts[0].shape[0] % 16 == 0:
        return jnp.concatenate(parts, axis=0)
    return jnp.concatenate([part.astype(F32) for part in parts], axis=0).astype(BF16)


def sum_squares(raw):
    return jnp.sum(raw * raw, axis=1, keepdims=True)


def project_qk(hidden, wq, wk, query_raw, key_raw, squares, wq_v, wk_v, sems):
    chunks, depth = wq_v.shape[0], wq_v.shape[1]
    copies = []
    for c in range(chunks):
        for at, (source, target) in enumerate(((wq, wq_v), (wk, wk_v))):
            copy = pltpu.make_async_copy(
                source.at[pl.ds(c * depth, depth)], target.at[c], sems.at[2 * c + at]
            )
            copy.start()
            copies.append(copy)
    q_sum, k_sum = None, None
    for c in range(chunks):
        part = hidden[:, c * depth : (c + 1) * depth]
        copies[2 * c].wait()
        q = dot(part, wq_v[c])
        copies[2 * c + 1].wait()
        k = dot(part, wk_v[c])
        q_sum = q if c == 0 else q_sum + q
        k_sum = k if c == 0 else k_sum + k
    query_raw[...] = q_sum
    key_raw[...] = k_sum
    lane = iota(squares.shape[1:], 1)
    both = jnp.where(lane == 0, sum_squares(q_sum), sum_squares(k_sum))
    for t in range(squares.shape[0]):
        squares[t] = both


def project_v_and_tree(
    lengths, leaves, hidden, parents, freqs, wv, value, own_tree, targets, cosine, sine, wv_v, anc_v, sems
):
    chunks, depth = wv_v.shape[0], wv_v.shape[1]
    copies = []
    for c in range(chunks):
        copy = pltpu.make_async_copy(wv.at[pl.ds(c * depth, depth)], wv_v.at[c], sems.at[c])
        copy.start()
        copies.append(copy)
    requests, draft = parents.shape
    own = hidden.shape[0]
    first = lax.axis_index("seq") * own
    row, col = iota((draft, draft), 0), iota((draft, draft), 1)
    eye = (row == col).astype(BF16)
    trees = [
        jnp.where((parents[pl.ds(r, 1), :] == row) | (row == col), 1.0, 0.0).astype(BF16)
        for r in range(requests)
    ]
    for _ in range(max(1, (draft - 1).bit_length())):
        trees = [jnp.minimum(dot(tree, tree), 1.0).astype(BF16) for tree in trees]
    for r in range(requests):
        upright = lax.dot_general(
            trees[r], eye, (((0,), (0,)), ((), ())), preferred_element_type=F32
        )
        anc_v[pl.ds(r * draft, draft), :] = upright
        level = jnp.sum(trees[r].astype(F32), axis=0, keepdims=True) - 1.0
        on_path = jnp.sum(jnp.where(row == leaves[r], upright, 0.0), axis=0, keepdims=True)
        place = lengths[r] + level.astype(jnp.int32)
        targets[r] = jnp.where(on_path > 0.5, place, -1)
    mine = anc_v[pl.ds(pl.multiple_of(first, own), own), :]
    own_tree[...] = mine
    level = jnp.sum(mine, axis=1, keepdims=True) - 1.0
    position = lengths[first // draft].astype(F32) + level
    angles = position * freqs[...]
    cosine[...] = jnp.cos(angles)
    half = jnp.sin(angles)
    sine[...] = jnp.where(iota(half.shape, 1) < HEAD_DIM // 2, -half, half)
    total = None
    for c in range(chunks):
        copies[c].wait()
        v = dot(hidden[:, c * depth : (c + 1) * depth], wv_v[c])
        total = v if c == 0 else total + v
    value[...] = total.astype(BF16)


def prepare(
    width_all, query_raw, key_raw, value, q_gain, k_gain, cosine, sine, squares, queries, keys_values
):
    width = query_raw.shape[1]
    total = sum(squares[k] for k in range(squares.shape[0]))
    cos, sin = cosine[...], sine[...]
    for at, (raw, gain, out) in enumerate(
        ((query_raw, q_gain, queries), (key_raw, k_gain, keys_values))
    ):
        scale = lax.rsqrt(total[:, at : at + 1] / width_all + EPS)
        for h in range(width // HEAD_DIM):
            lanes = slice(h * HEAD_DIM, (h + 1) * HEAD_DIM)
            x = raw[:, lanes] * scale * gain[:, lanes]
            turned = x * cos + pltpu.roll(x, HEAD_DIM // 2, 1) * sin
            turned = turned.astype(BF16)
            for s in range(out.shape[0]):
                out[s, :, lanes] = turned
    for s in range(keys_values.shape[0]):
        keys_values[s, :, width:] = value[...]


def attend_cache(group, lengths, key_cache, value_cache, queries, partials):
    requests, block, width = key_cache.shape
    own = queries.shape[1]
    heads = width // HEAD_DIM
    me = lax.axis_index("seq")
    factor = 1.0 / math.sqrt(HEAD_DIM)
    rows = group * own
    place = me * block + iota((rows, block), 1)
    lane = iota((rows, LANES), 1)
    for request in range(requests):
        q = stacked([queries[request * group + j] for j in range(group)])
        visible = place < lengths[request]
        stats = jnp.zeros((rows, LANES), F32)
        for h in range(heads):
            lanes = slice(h * HEAD_DIM, (h + 1) * HEAD_DIM)
            scores = dot_t(q[:, lanes], key_cache[request, :, lanes]) * factor
            scores = jnp.where(visible, scores, NEG)
            peak = jnp.max(scores, axis=1, keepdims=True).astype(BF16).astype(F32)
            weights = jnp.exp(jnp.where(visible, scores - peak, NEG))
            total = jnp.sum(weights, axis=1, keepdims=True)
            high = total.astype(BF16).astype(F32)
            out = dot(weights.astype(BF16), value_cache[request, :, lanes]).astype(BF16)
            for j in range(group):
                partials[request * group + j, :, lanes] = out[j * own : (j + 1) * own]
            stats = jnp.where(lane == h, peak, stats)
            stats = jnp.where(lane == heads + h, high, stats)
            stats = jnp.where(lane == 2 * heads + h, total - high, stats)
        stats = stats.astype(BF16)
        for j in range(group):
            partials[request * group + j, :, width:] = stats[j * own : (j + 1) * own]


def attend_draft(group, own_tree, queries, keys_values, out, stats):
    own, width = queries.shape[1:]
    heads = width // HEAD_DIM
    me = lax.axis_index("seq")
    first = me // group * group
    q = queries[me]
    pair = stacked([keys_values[first + j] for j in range(group)])
    factor = 1.0 / math.sqrt(HEAD_DIM)
    allowed = own_tree[...] > 0.5
    lane = iota((own, LANES), 1)
    kept = jnp.zeros((own, LANES), F32)
    for h in range(heads):
        lanes = slice(h * HEAD_DIM, (h + 1) * HEAD_DIM)
        there = slice(width + h * HEAD_DIM, width + (h + 1) * HEAD_DIM)
        scores = dot_t(q[:, lanes], pair[:, lanes]) * factor
        scores = jnp.where(allowed, scores, NEG)
        peak = jnp.max(scores, axis=1, keepdims=True)
        weights = jnp.exp(jnp.where(allowed, scores - peak, NEG))
        out[:, lanes] = dot(weights.astype(BF16), pair[:, there])
        kept = jnp.where(lane == h, peak, kept)
        kept = jnp.where(lane == heads + h, jnp.sum(weights, axis=1, keepdims=True), kept)
    stats[...] = kept


def merge_and_project(draft_out, draft_stats, wo, partials, projected, wo_v, sems):
    count, width, columns = wo_v.shape
    heads = width // HEAD_DIM
    copies = []
    for k in range(count):
        copy = pltpu.make_async_copy(
            wo.at[:, pl.ds(k * columns, columns)], wo_v.at[k], sems.at[k]
        )
        copy.start()
        copies.append(copy)
    parts = range(partials.shape[0])
    stats = [partials[s, :, width:].astype(F32) for s in parts]
    own_stats = draft_stats[...]
    attention = []
    for h in range(heads):
        lanes = slice(h * HEAD_DIM, (h + 1) * HEAD_DIM)
        peaks = [s[:, h : h + 1] for s in stats] + [own_stats[:, h : h + 1]]
        highest = functools.reduce(jnp.maximum, peaks)
        scales = [jnp.exp(peak - highest) for peak in peaks]
        total = own_stats[:, heads + h : heads + h + 1] * scales[-1]
        summed = draft_out[:, lanes] * scales[-1]
        for at in parts:
            s = stats[at]
            own_total = s[:, heads + h : heads + h + 1] + s[:, 2 * heads + h : 2 * heads + h + 1]
            total = total + own_total * scales[at]
            summed = summed + partials[at, :, lanes].astype(F32) * scales[at]
        attention.append((summed / total).astype(BF16))
    attention = jnp.concatenate(attention, axis=1)
    for k in range(count):
        copies[k].wait()
        projected[k] = dot(attention, wo_v[k]).astype(projected.dtype)


def add_up(parts, summed, power):
    total = sum(parts[k].astype(F32) for k in range(parts.shape[0]))
    summed[...] = total
    own_power = jnp.broadcast_to(sum_squares(total), power.shape[1:])
    for k in range(power.shape[0]):
        power[k] = own_power


def finish(model_width, summed, gain, hidden, powers, out):
    columns = summed.shape[1]
    power = sum(powers[k] for k in range(powers.shape[0]))[:, :1]
    start = pl.multiple_of(lax.axis_index("tp") * columns, columns)
    normed = summed[...] * lax.rsqrt(power / model_width + EPS) * gain[...]
    out[...] = (hidden[:, pl.ds(start, columns)].astype(F32) + normed).astype(BF16)


def compact(group, targets, key_cache, value_cache, keys_values, new_keys, new_values):
    requests, block, width = key_cache.shape
    own = keys_values.shape[1]
    me = lax.axis_index("seq")
    place = me * block + iota((block, group * own), 0)
    for request in range(requests):
        kv = stacked([keys_values[request * group + j] for j in range(group)])
        placing = place == targets[request]
        written = jnp.max(placing.astype(F32), axis=1, keepdims=True) > 0.5
        fresh = dot(placing.astype(BF16), kv)
        new_keys[request] = jnp.where(
            written, fresh[:, :width], key_cache[request].astype(F32)
        ).astype(BF16)
        new_values[request] = jnp.where(
            written, fresh[:, width:], value_cache[request].astype(F32)
        ).astype(BF16)


def shaped(shape, dtype):
    return jax.ShapeDtypeStruct(shape, dtype)


def body_general(
    hidden_in,
    query_weight,
    key_weight,
    value_weight,
    out_weight,
    query_gain,
    key_gain,
    post_gain,
    key_cache,
    value_cache,
    cache_lengths,
    parents,
    accepted_leaf,
):
    requests, block, width = key_cache.shape
    draft = parents.shape[1]
    own, model = hidden_in.shape
    tp = lax.axis_size("tp")
    seq = lax.axis_size("seq")
    group = draft // own
    columns = model // tp
    chunks = 4
    depth = model // chunks

    def exchange(x, axis):
        return lax.all_to_all(x, axis, 0, 0, tiled=True)

    query_raw, key_raw, squares = pl.pallas_call(
        project_qk,
        out_shape=(
            shaped((own, width), F32),
            shaped((own, width), F32),
            shaped((tp, own, LANES), F32),
        ),
        in_specs=[VMEM, ANY, ANY],
        out_specs=(VMEM, VMEM, VMEM),
        scratch_shapes=[
            pltpu.VMEM((chunks, depth, width), BF16),
            pltpu.VMEM((chunks, depth, width), BF16),
            pltpu.SemaphoreType.DMA((2 * chunks,)),
        ],
        compiler_params=params(56),
        cost_estimate=pl.CostEstimate(
            flops=4 * own * model * width, bytes_accessed=4 * model * width, transcendentals=0
        ),
        name="project_qk",
    )(hidden_in, query_weight, key_weight)
    squares = exchange(squares, "tp")

    exponents = -2.0 * (jnp.arange(HEAD_DIM) % (HEAD_DIM // 2)).astype(F32) / HEAD_DIM
    freqs = (THETA**exponents)[None, :]
    value, own_tree, targets, cosine, sine = pl.pallas_call(
        project_v_and_tree,
        out_shape=(
            shaped((own, width), BF16),
            shaped((own, draft), F32),
            shaped((requests, 1, draft), jnp.int32),
            shaped((own, HEAD_DIM), F32),
            shaped((own, HEAD_DIM), F32),
        ),
        in_specs=[SMEM, SMEM, VMEM, VMEM, VMEM, ANY],
        out_specs=(VMEM,) * 5,
        scratch_shapes=[
            pltpu.VMEM((chunks, depth, width), BF16),
            pltpu.VMEM((requests * draft, draft), F32),
            pltpu.SemaphoreType.DMA((chunks,)),
        ],
        compiler_params=params(16),
        cost_estimate=pl.CostEstimate(
            flops=2 * own * model * width, bytes_accessed=2 * model * width, transcendentals=0
        ),
        name="project_v_and_tree",
    )(cache_lengths, accepted_leaf, hidden_in, parents, freqs, value_weight)

    queries, keys_values = pl.pallas_call(
        functools.partial(prepare, tp * width),
        out_shape=(shaped((seq, own, width), BF16), shaped((seq, own, 2 * width), BF16)),
        in_specs=[VMEM] * 8,
        out_specs=(VMEM, VMEM),
        compiler_params=params(16),
        name="prepare",
    )(
        query_raw,
        key_raw,
        value,
        query_gain[None, :],
        key_gain[None, :],
        cosine,
        sine,
        squares,
    )
    queries = exchange(queries, "seq")
    keys_values = exchange(keys_values, "seq")

    partials = pl.pallas_call(
        functools.partial(attend_cache, group),
        out_shape=shaped((seq, own, width + LANES), BF16),
        in_specs=[SMEM, VMEM, VMEM, VMEM],
        out_specs=VMEM,
        compiler_params=params(16),
        name="attend_cache",
    )(cache_lengths, key_cache, value_cache, queries)
    partials = exchange(partials, "seq")

    draft_out, draft_stats = pl.pallas_call(
        functools.partial(attend_draft, group),
        out_shape=(shaped((own, width), F32), shaped((own, LANES), F32)),
        in_specs=[VMEM] * 3,
        out_specs=(VMEM, VMEM),
        compiler_params=params(16),
        name="attend_draft",
    )(own_tree, queries, keys_values)

    projected = pl.pallas_call(
        merge_and_project,
        out_shape=shaped((tp, own, columns), BF16),
        in_specs=[VMEM, VMEM, ANY, VMEM],
        out_specs=VMEM,
        scratch_shapes=[
            pltpu.VMEM((tp, width, columns), BF16),
            pltpu.SemaphoreType.DMA((tp,)),
        ],
        compiler_params=params(16),
        name="merge_and_project",
    )(draft_out, draft_stats, out_weight, partials)
    projected = exchange(projected, "tp")

    summed, power = pl.pallas_call(
        add_up,
        out_shape=(shaped((own, columns), F32), shaped((tp, own, LANES), F32)),
        in_specs=[VMEM],
        out_specs=(VMEM, VMEM),
        compiler_params=params(16),
        name="add_up",
    )(projected)
    power = exchange(power, "tp")

    hidden_out = pl.pallas_call(
        functools.partial(finish, model),
        out_shape=shaped((own, columns), BF16),
        in_specs=[VMEM] * 4,
        out_specs=VMEM,
        compiler_params=params(16),
        name="finish",
    )(summed, post_gain[None, :], hidden_in, power)

    new_key_cache, new_value_cache = pl.pallas_call(
        functools.partial(compact, group),
        out_shape=(shaped(key_cache.shape, BF16), shaped(value_cache.shape, BF16)),
        in_specs=[VMEM] * 4,
        out_specs=(VMEM, VMEM),
        compiler_params=params(24),
        name="compact",
    )(targets, key_cache, value_cache, keys_values)
    return (hidden_out, new_key_cache, new_value_cache)


def across(column):
    rows = column.shape[0]
    eye = iota((rows, rows), 0) == iota((rows, rows), 1)
    return jnp.sum(jnp.where(eye, column, 0.0), axis=0, keepdims=True)


def upright(line):
    rows = line.shape[1]
    eye = iota((rows, rows), 0) == iota((rows, rows), 1)
    return jnp.sum(jnp.where(eye, line, 0.0), axis=1, keepdims=True)


def eye_of(size):
    return (iota((size, size), 0) == iota((size, size), 1)).astype(BF16)


def plane():
    return lax.axis_index("seq") // 2


def twin_project_qk(hidden, wq, wk, query_raw, key_raw, squares):
    rows = hidden[...]
    own = rows.shape[0]
    for at, (weight, raw) in enumerate(((wq, query_raw), (wk, key_raw))):
        product = dot(rows, weight[...])
        raw[...] = product
        line = across(sum_squares(product))
        line = jnp.concatenate([line, jnp.zeros((1, LANES - own), F32)], axis=1)
        squares[:, at * LANES : (at + 1) * LANES] = jnp.broadcast_to(
            line, (squares.shape[0], LANES)
        )


def twin_project_v(hidden, wv, value):
    value[...] = dot(hidden[...], wv[...]).astype(BF16)


def twin_tree(
    turns, lengths, leaves, parents, freqs, own_tree, targets, cosine, sine, limits, held
):
    requests, draft = parents.shape
    own = own_tree.shape[1]
    row, col = iota((draft, draft), 0), iota((draft, draft), 1)
    eye = eye_of(draft)

    def length_of(request):
        picked = iota(lengths.shape, 1) == request
        return jnp.sum(jnp.where(picked, lengths[...], 0), axis=1, keepdims=True)

    for at, turn in enumerate(turns):
        limits[at : at + 1, :] = jnp.broadcast_to(
            length_of(plane() ^ turn), (1, limits.shape[1])
        )
    trees = [
        jnp.where((parents[pl.ds(r, 1), :] == row) | (row == col), 1.0, 0.0).astype(BF16)
        for r in range(requests)
    ]
    for _ in range(max(1, (draft - 1).bit_length())):
        trees = [jnp.minimum(dot(tree, tree), 1.0).astype(BF16) for tree in trees]
    for r in range(requests):
        standing = lax.dot_general(
            trees[r], eye, (((0,), (0,)), ((), ())), preferred_element_type=F32
        )
        held[r] = standing
        level = jnp.sum(trees[r].astype(F32), axis=0, keepdims=True) - 1.0
        on_path = jnp.where(row == leaves[:, r : r + 1], standing, 0.0)
        on_path = jnp.sum(on_path, axis=0, keepdims=True)
        place = lengths[:, r : r + 1] + level.astype(jnp.int32)
        targets[r] = jnp.where(on_path > 0.5, place, -1)
    within = lax.rem(lax.axis_index("seq"), 2)
    for at in range(2):
        first = (within ^ at) * own
        rows = held[plane(), pl.ds(pl.multiple_of(first, own), own), :]
        own_tree[at * own : (at + 1) * own, :] = jnp.where(
            within == 0, rows[:, :own], rows[:, own:]
        )
        mine = rows if at == 0 else mine
    level = jnp.sum(mine, axis=1, keepdims=True) - 1.0
    angles = (length_of(plane()).astype(F32) + level) * freqs[...]
    cosine[...] = jnp.cos(angles)
    half = jnp.sin(angles)
    sine[...] = jnp.where(iota(half.shape, 1) < HEAD_DIM // 2, -half, half)


def turned(raw, scale, gain, cos, sin):
    x = raw * scale * gain
    return (x * cos + pltpu.roll(x, HEAD_DIM // 2, 1) * sin).astype(BF16)


def twin_prepare(width_all, query_raw, key_raw, value, q_gain, k_gain, cosine, sine, *refs):
    squares, (queries, packed) = refs[:-2], refs[-2:]
    own, width = query_raw.shape
    cos, sin = cosine[...], sine[...]
    total = sum(ref[:1, :] for ref in squares)
    for at, (raw, gain) in enumerate(((query_raw, q_gain), (key_raw, k_gain))):
        scale = upright(total[:, at * LANES : at * LANES + own])
        scale = lax.rsqrt(scale / width_all + EPS)
        for h in range(width // HEAD_DIM):
            lanes = slice(h * HEAD_DIM, (h + 1) * HEAD_DIM)
            there = slice(at * width + h * HEAD_DIM, at * width + (h + 1) * HEAD_DIM)
            found = turned(raw[:, lanes], scale, gain[:, lanes], cos, sin)
            packed[:, there] = found
            if at == 0:
                queries[:, lanes] = found
    packed[:, 2 * width :] = value[...]


def weigh(s, visible):
    peak = jnp.max(s, axis=1, keepdims=True).astype(BF16).astype(F32)
    weights = jnp.exp(jnp.where(visible, s - peak, NEG))
    total = jnp.sum(weights, axis=1, keepdims=True)
    high = total.astype(BF16).astype(F32)
    return weights.astype(BF16), (peak, high, total - high)


def kept(stats, h, heads, found):
    lane = iota(stats.shape, 1)
    for at, column in enumerate(found):
        stats = jnp.where(lane == at * heads + h, column, stats)
    return stats


def write_stats(stats, out):
    own, width = stats.shape[0], out.shape[1]
    flat = lax.dot_general(
        stats.astype(BF16), eye_of(own), (((0,), (0,)), ((), ())), preferred_element_type=F32
    )
    flat = jnp.concatenate([flat[:16], jnp.zeros((16, width - own), F32)], axis=1)
    out[own : own + 16, :] = flat.astype(BF16)


def twin_attend_far(turns, limits, key_cache, value_cache, swapped, *refs):
    count = len(turns)
    queries, outs, scores = refs[:count], refs[count : 2 * count], refs[2 * count]
    block, width = key_cache.shape[1:]
    heads = width // HEAD_DIM
    own = queries[0].shape[0]
    me = lax.axis_index("seq")
    factor = 1.0 / math.sqrt(HEAD_DIM)
    place = iota((1, block), 1)
    both = jnp.concatenate([me * block + place, (me ^ 1) * block + place], axis=1)
    visible = [both < limits[at + 1 : at + 2, :] for at in range(count)]
    for at, turn in enumerate(turns):
        for h in range(heads):
            lanes = slice(h * HEAD_DIM, (h + 1) * HEAD_DIM)
            q = queries[at][:, lanes]
            first = dot_t(q, key_cache[plane() ^ turn, :, lanes])
            second = dot_t(q, swapped[at, 0, :, lanes])
            product = jnp.concatenate([first, second], axis=1) * factor
            scores[at, h] = jnp.where(visible[at], product, NEG)
    for at, turn in enumerate(turns):
        stats = jnp.zeros((own, LANES), F32)
        for h in range(heads):
            lanes = slice(h * HEAD_DIM, (h + 1) * HEAD_DIM)
            weights, found = weigh(scores[at, h], visible[at])
            out = dot(weights[:, :block], value_cache[plane() ^ turn, :, lanes])
            out = out + dot(weights[:, block:], swapped[at, 1, :, lanes])
            outs[at][:own, lanes] = out.astype(BF16)
            stats = kept(stats, h, heads, found)
        write_stats(stats, outs[at])


def twin_attend_near(limits, key_cache, value_cache, own_tree, mine, other, *refs):
    queries, (crossing, local, copied, own_scores) = refs[:-4], refs[-4:]
    count = len(queries)
    block, width = key_cache.shape[1:]
    heads = width // HEAD_DIM
    own = other.shape[0]
    factor = 1.0 / math.sqrt(HEAD_DIM)
    place = lax.axis_index("seq") * block + iota((1, block), 1)
    here = jnp.broadcast_to(place < limits[:1, :block], (2 * own, block))
    rest = own_scores.shape[2] - block - own
    near = jnp.concatenate(
        [jnp.where(here, 1.0, 0.0), own_tree[...], jnp.zeros((2 * own, rest), F32)], axis=1
    )
    near = near > 0.5
    pair = stacked([mine[:, :width], other[...]])
    for h in range(heads):
        lanes = slice(h * HEAD_DIM, (h + 1) * HEAD_DIM)
        keys = jnp.concatenate(
            [mine[:, width + h * HEAD_DIM : width + (h + 1) * HEAD_DIM]] * (1 + rest // own), axis=0
        )
        first = dot_t(pair[:, lanes], key_cache[plane(), :, lanes])
        product = jnp.concatenate([first, dot_t(pair[:, lanes], keys)], axis=1) * factor
        own_scores[h] = jnp.where(near, product, NEG)
    stats = jnp.zeros((2 * own, LANES), F32)
    for h in range(heads):
        lanes = slice(h * HEAD_DIM, (h + 1) * HEAD_DIM)
        weights, found = weigh(own_scores[h], near)
        out = dot(weights[:, :block], value_cache[plane(), :, lanes])
        values = mine[:, 2 * width + h * HEAD_DIM : 2 * width + (h + 1) * HEAD_DIM]
        out = out + dot(weights[:, block : block + own], values)
        out = out.astype(BF16)
        local[:own, lanes] = out[:own]
        crossing[:own, lanes] = out[own:]
        stats = kept(stats, h, heads, found)
    write_stats(stats[:own], local)
    write_stats(stats[own:], crossing)
    for at, ref in enumerate((mine, *queries)):
        for part in range(2):
            rows = slice((2 * at + part) * own, (2 * at + part + 1) * own)
            copied[rows, :] = ref[:, (part + 1) * width : (part + 2) * width]
    last = 2 * (count + 1) * own
    copied[last:, :] = jnp.zeros((copied.shape[0] - last, width), BF16)


def twin_rows(mine, theirs, held):
    within = lax.rem(lax.axis_index("seq"), 2)
    held[within] = mine
    held[1 - within] = theirs
    return stacked([held[0], held[1]])


def twin_merge_and_project(*refs):
    partials, (wo, total_out, rounded) = refs[:-3], refs[-3:]
    own, width = total_out.shape[0], partials[0].shape[1]
    heads = width // HEAD_DIM
    stats = [dot_t(eye_of(own), ref[own : own + 16, :own]) for ref in partials]
    attention = []
    for h in range(heads):
        lanes = slice(h * HEAD_DIM, (h + 1) * HEAD_DIM)
        peaks = [s[:, h : h + 1] for s in stats]
        highest = functools.reduce(jnp.maximum, peaks)
        total, summed = 0.0, 0.0
        for ref, s, peak in zip(partials, stats, peaks):
            scale = jnp.exp(peak - highest)
            own_total = s[:, heads + h : heads + h + 1] + s[:, 2 * heads + h : 2 * heads + h + 1]
            total = total + own_total * scale
            summed = summed + ref[:own, lanes].astype(F32) * scale
        attention.append((summed / total).astype(BF16))
    product = dot(jnp.concatenate(attention, axis=1), wo[...])
    total_out[...] = product
    rounded[...] = product.astype(BF16)


def twin_add(mine, theirs, total, rounded):
    both = mine[...] + theirs[...].astype(F32)
    total[...] = both
    rounded[...] = both.astype(BF16)


def twin_finish(mine, theirs, gain, hidden, out):
    model_width = mine.shape[1]
    columns = out.shape[1]
    total = mine[...] + theirs[...].astype(F32)
    scale = lax.rsqrt(sum_squares(total) / model_width + EPS)
    lanes = pl.ds(pl.multiple_of(lax.axis_index("tp") * columns, columns), columns)
    normed = (mine[:, lanes] + theirs[:, lanes].astype(F32)) * scale * gain[...]
    out[...] = (hidden[:, lanes].astype(F32) + normed).astype(BF16)


def twin_compact(far, targets, key_cache, value_cache, *refs):
    count = len(far) + 1
    ours, (copied, new_keys, new_values, held) = refs[:count], refs[count:]
    block, width = key_cache.shape[1:]
    own = ours[0].shape[0]
    me = lax.axis_index("seq")
    place = me * block + iota((block, targets.shape[2]), 0)
    for at, turn in enumerate((0, *far)):
        request = plane() ^ turn
        placing = place == targets[request]
        written = jnp.max(placing.astype(F32), axis=1, keepdims=True) > 0.5
        placing = placing.astype(BF16)
        for part, (cache, out) in enumerate(((key_cache, new_keys), (value_cache, new_values))):
            lanes = slice((part + 1) * width, (part + 2) * width)
            rows = slice((2 * at + part) * own, (2 * at + part + 1) * own)
            theirs = copied[rows, :]
            fresh = twin_rows(ours[at][:, lanes], theirs, held.at[at, part])
            moved = dot(placing, fresh)
            out[request] = jnp.where(written, moved, cache[request].astype(F32)).astype(BF16)


def body_twin(
    hidden_in,
    query_weight,
    key_weight,
    value_weight,
    out_weight,
    query_gain,
    key_gain,
    post_gain,
    key_cache,
    value_cache,
    cache_lengths,
    parents,
    accepted_leaf,
):
    requests, block, width = key_cache.shape
    draft = parents.shape[1]
    own, model = hidden_in.shape
    tp = lax.axis_size("tp")
    seq = lax.axis_size("seq")
    columns = model // tp
    heads = width // HEAD_DIM
    far = tuple(range(requests - 1, 0, -1))

    def call(kernel, outs, inputs, scratch=(), mib=16, specs=None, ties=()):
        count = len(inputs)

        def run(*refs):
            kernel(*refs[:count], *refs[count + len(ties) :])

        return pl.pallas_call(
            run,
            out_shape=outs,
            in_specs=([VMEM] * count if specs is None else specs) + [ANY] * len(ties),
            out_specs=jax.tree.map(lambda _: VMEM, outs),
            scratch_shapes=list(scratch),
            compiler_params=params(mib),
            name=getattr(kernel, "func", kernel).__name__,
        )(*inputs, *ties)

    def over_tp(x, k):
        return lax.ppermute(x, "tp", [(i, i ^ k) for i in range(tp)])

    def beside(x):
        return lax.ppermute(x, "seq", [(i, i ^ 1) for i in range(seq)])

    def over_planes(x, turn):
        return lax.ppermute(x, "seq", [(i, (i // 2 ^ turn) * 2 + i % 2) for i in range(seq)])

    me = lax.axis_index("seq") // 2

    def picked(turns):
        parts = [
            [lax.dynamic_index_in_dim(x, me ^ turn, 0, False) for x in (key_cache, value_cache)]
            for turn in turns
        ]
        return jnp.stack([jnp.stack(part) for part in parts])

    swapped = beside(picked(far))
    query_raw, key_raw, squares = call(
        twin_project_qk,
        (shaped((own, width), F32), shaped((own, width), F32), shaped((8, 2 * LANES), F32)),
        (hidden_in, query_weight, key_weight),
    )
    all_squares = [squares] + [over_tp(squares, k) for k in range(tp - 1, 0, -1)]

    exponents = -2.0 * (jnp.arange(HEAD_DIM) % (HEAD_DIM // 2)).astype(F32) / HEAD_DIM
    freqs = (THETA**exponents)[None, :]
    own_tree, targets, cosine, sine, limits = call(
        functools.partial(twin_tree, (0, *far)),
        (
            shaped((draft, own), F32),
            shaped((requests, 1, draft), jnp.int32),
            shaped((own, HEAD_DIM), F32),
            shaped((own, HEAD_DIM), F32),
            shaped((requests, 2 * block), jnp.int32),
        ),
        (cache_lengths[None, :], accepted_leaf[None, :], parents, freqs),
        [pltpu.VMEM((requests, draft, draft), F32)],
    )
    value = call(twin_project_v, shaped((own, width), BF16), (hidden_in, value_weight))
    queries, packed = call(
        functools.partial(twin_prepare, tp * width),
        (shaped((own, width), BF16), shaped((own, 3 * width), BF16)),
        (
            query_raw,
            key_raw,
            value,
            query_gain[None, :],
            key_gain[None, :],
            cosine,
            sine,
            *all_squares,
        ),
    )
    from_far = [over_planes(packed, turn) for turn in far]
    other = beside(queries)

    rows = own + 16
    partials = call(
        functools.partial(twin_attend_far, far),
        (shaped((rows, width), BF16),) * len(far),
        (limits, key_cache, value_cache, swapped, *from_far),
        [pltpu.VMEM((len(far), heads, own, 2 * block), F32)],
    )
    crossing, local, copied = call(
        twin_attend_near,
        (shaped((rows, width), BF16),) * 2 + (shaped((2 * requests * own + own, width), BF16),),
        (limits, key_cache, value_cache, own_tree, packed, other, *from_far),
        [pltpu.VMEM((heads, 2 * own, block + LANES), F32)],
        ties=partials[:1],
    )
    partials = [over_planes(part, turn) for part, turn in zip(partials, far)]
    partials += [beside(crossing)]
    partials = [partials[1], partials[0], partials[3], partials[2], local]
    copied = beside(copied)

    total, rounded = call(
        twin_merge_and_project,
        (shaped((own, model), F32), shaped((own, model), BF16)),
        (*partials, out_weight),
    )
    bit = 1
    while 2 * bit < tp:
        total, rounded = call(
            twin_add,
            (shaped((own, model), F32), shaped((own, model), BF16)),
            (total, over_tp(rounded, bit)),
        )
        bit *= 2
    arrived = over_tp(rounded, bit)
    new_key_cache, new_value_cache = call(
        functools.partial(twin_compact, far),
        (shaped(key_cache.shape, BF16), shaped(value_cache.shape, BF16)),
        (targets, key_cache, value_cache, packed, *from_far, copied),
        [pltpu.VMEM((requests, 2, 2, own, width), BF16)],
    )
    hidden_out = call(
        twin_finish,
        shaped((own, columns), BF16),
        (total, arrived, post_gain[None, :], hidden_in),
    )
    return (hidden_out, new_key_cache, new_value_cache)


def body(*args):
    hidden_in, key_cache, parents = args[0], args[8], args[11]
    tp = lax.axis_size("tp")
    own, draft = hidden_in.shape[0], parents.shape[1]
    requests, _, width = key_cache.shape
    twin = (
        own % 16 == 0
        and draft == 2 * own
        and requests == 4
        and lax.axis_size("seq") == 2 * requests
        and own <= LANES
        and LANES % own == 0
        and own <= width
        and 3 * (width // HEAD_DIM) <= 16
        and tp > 1
        and tp & (tp - 1) == 0
    )
    return (body_twin if twin else body_general)(*args)


def solution(mesh):
    return jax.shard_map(
        body,
        mesh=mesh,
        in_specs=(
            P("seq", None),
            P(None, "tp"),
            P(None, "tp"),
            P(None, "tp"),
            P("tp", None),
            P("tp"),
            P("tp"),
            P("tp"),
            P(None, "seq", "tp"),
            P(None, "seq", "tp"),
            P(),
            P(),
            P(),
        ),
        out_specs=(P("seq", "tp"), P(None, "seq", "tp"), P(None, "seq", "tp")),
        check_vma=False,
    )
```

```python
import functools
import math

import jax
import jax.numpy as jnp
from jax import lax
from jax.experimental import pallas as pl
from jax.experimental.pallas import tpu as pltpu
from jax.sharding import PartitionSpec as P

HEAD_DIM = 128
LANES = 128
EPS = 1e-06
THETA = 500000.0
NEG = -1e30
F32 = jnp.float32
BF16 = jnp.bfloat16
VMEM = pl.BlockSpec(memory_space=pltpu.VMEM)
SMEM = pl.BlockSpec(memory_space=pltpu.SMEM)
ANY = pl.BlockSpec(memory_space=pl.ANY)


def params(mib):
    return pltpu.CompilerParams(vmem_limit_bytes=mib * 1024 * 1024)


def dot(a, b):
    return jnp.dot(a, b, preferred_element_type=F32)


def dot_t(a, b):
    return lax.dot_general(a, b, (((1,), (1,)), ((), ())), preferred_element_type=F32)


def iota(shape, axis):
    return lax.broadcasted_iota(jnp.int32, shape, axis)


def stacked(parts):
    if len(parts) == 1:
        return parts[0]
    if parts[0].shape[0] % 16 == 0:
        return jnp.concatenate(parts, axis=0)
    return jnp.concatenate([part.astype(F32) for part in parts], axis=0).astype(BF16)


def sum_squares(raw):
    return jnp.sum(raw * raw, axis=1, keepdims=True)


def project_qk(hidden, wq, wk, query_raw, key_raw, squares, wq_v, wk_v, sems):
    chunks, depth = wq_v.shape[0], wq_v.shape[1]
    copies = []
    for c in range(chunks):
        for at, (source, target) in enumerate(((wq, wq_v), (wk, wk_v))):
            copy = pltpu.make_async_copy(
                source.at[pl.ds(c * depth, depth)], target.at[c], sems.at[2 * c + at]
            )
            copy.start()
            copies.append(copy)
    q_sum, k_sum = None, None
    for c in range(chunks):
        part = hidden[:, c * depth : (c + 1) * depth]
        copies[2 * c].wait()
        q = dot(part, wq_v[c])
        copies[2 * c + 1].wait()
        k = dot(part, wk_v[c])
        q_sum = q if c == 0 else q_sum + q
        k_sum = k if c == 0 else k_sum + k
    query_raw[...] = q_sum
    key_raw[...] = k_sum
    lane = iota(squares.shape[1:], 1)
    both = jnp.where(lane == 0, sum_squares(q_sum), sum_squares(k_sum))
    for t in range(squares.shape[0]):
        squares[t] = both


def project_v_and_tree(
    lengths, leaves, hidden, parents, freqs, wv, value, own_tree, targets, cosine, sine, wv_v, anc_v, sems
):
    chunks, depth = wv_v.shape[0], wv_v.shape[1]
    copies = []
    for c in range(chunks):
        copy = pltpu.make_async_copy(wv.at[pl.ds(c * depth, depth)], wv_v.at[c], sems.at[c])
        copy.start()
        copies.append(copy)
    requests, draft = parents.shape
    own = hidden.shape[0]
    first = lax.axis_index("seq") * own
    row, col = iota((draft, draft), 0), iota((draft, draft), 1)
    eye = (row == col).astype(BF16)
    trees = [
        jnp.where((parents[pl.ds(r, 1), :] == row) | (row == col), 1.0, 0.0).astype(BF16)
        for r in range(requests)
    ]
    for _ in range(max(1, (draft - 1).bit_length())):
        trees = [jnp.minimum(dot(tree, tree), 1.0).astype(BF16) for tree in trees]
    for r in range(requests):
        upright = lax.dot_general(
            trees[r], eye, (((0,), (0,)), ((), ())), preferred_element_type=F32
        )
        anc_v[pl.ds(r * draft, draft), :] = upright
        level = jnp.sum(trees[r].astype(F32), axis=0, keepdims=True) - 1.0
        on_path = jnp.sum(jnp.where(row == leaves[r], upright, 0.0), axis=0, keepdims=True)
        place = lengths[r] + level.astype(jnp.int32)
        targets[r] = jnp.where(on_path > 0.5, place, -1)
    mine = anc_v[pl.ds(pl.multiple_of(first, own), own), :]
    own_tree[...] = mine
    level = jnp.sum(mine, axis=1, keepdims=True) - 1.0
    position = lengths[first // draft].astype(F32) + level
    angles = position * freqs[...]
    cosine[...] = jnp.cos(angles)
    half = jnp.sin(angles)
    sine[...] = jnp.where(iota(half.shape, 1) < HEAD_DIM // 2, -half, half)
    total = None
    for c in range(chunks):
        copies[c].wait()
        v = dot(hidden[:, c * depth : (c + 1) * depth], wv_v[c])
        total = v if c == 0 else total + v
    value[...] = total.astype(BF16)


def prepare(
    width_all, query_raw, key_raw, value, q_gain, k_gain, cosine, sine, squares, queries, keys_values
):
    width = query_raw.shape[1]
    total = sum(squares[k] for k in range(squares.shape[0]))
    cos, sin = cosine[...], sine[...]
    for at, (raw, gain, out) in enumerate(
        ((query_raw, q_gain, queries), (key_raw, k_gain, keys_values))
    ):
        scale = lax.rsqrt(total[:, at : at + 1] / width_all + EPS)
        for h in range(width // HEAD_DIM):
            lanes = slice(h * HEAD_DIM, (h + 1) * HEAD_DIM)
            x = raw[:, lanes] * scale * gain[:, lanes]
            turned = x * cos + pltpu.roll(x, HEAD_DIM // 2, 1) * sin
            turned = turned.astype(BF16)
            for s in range(out.shape[0]):
                out[s, :, lanes] = turned
    for s in range(keys_values.shape[0]):
        keys_values[s, :, width:] = value[...]


def attend_cache(group, lengths, key_cache, value_cache, queries, partials):
    requests, block, width = key_cache.shape
    own = queries.shape[1]
    heads = width // HEAD_DIM
    me = lax.axis_index("seq")
    factor = 1.0 / math.sqrt(HEAD_DIM)
    rows = group * own
    place = me * block + iota((rows, block), 1)
    lane = iota((rows, LANES), 1)
    for request in range(requests):
        q = stacked([queries[request * group + j] for j in range(group)])
        visible = place < lengths[request]
        stats = jnp.zeros((rows, LANES), F32)
        for h in range(heads):
            lanes = slice(h * HEAD_DIM, (h + 1) * HEAD_DIM)
            scores = dot_t(q[:, lanes], key_cache[request, :, lanes]) * factor
            scores = jnp.where(visible, scores, NEG)
            peak = jnp.max(scores, axis=1, keepdims=True).astype(BF16).astype(F32)
            weights = jnp.exp(jnp.where(visible, scores - peak, NEG))
            total = jnp.sum(weights, axis=1, keepdims=True)
            high = total.astype(BF16).astype(F32)
            out = dot(weights.astype(BF16), value_cache[request, :, lanes]).astype(BF16)
            for j in range(group):
                partials[request * group + j, :, lanes] = out[j * own : (j + 1) * own]
            stats = jnp.where(lane == h, peak, stats)
            stats = jnp.where(lane == heads + h, high, stats)
            stats = jnp.where(lane == 2 * heads + h, total - high, stats)
        stats = stats.astype(BF16)
        for j in range(group):
            partials[request * group + j, :, width:] = stats[j * own : (j + 1) * own]


def attend_draft(group, own_tree, queries, keys_values, out, stats):
    own, width = queries.shape[1:]
    heads = width // HEAD_DIM
    me = lax.axis_index("seq")
    first = me // group * group
    q = queries[me]
    pair = stacked([keys_values[first + j] for j in range(group)])
    factor = 1.0 / math.sqrt(HEAD_DIM)
    allowed = own_tree[...] > 0.5
    lane = iota((own, LANES), 1)
    kept = jnp.zeros((own, LANES), F32)
    for h in range(heads):
        lanes = slice(h * HEAD_DIM, (h + 1) * HEAD_DIM)
        there = slice(width + h * HEAD_DIM, width + (h + 1) * HEAD_DIM)
        scores = dot_t(q[:, lanes], pair[:, lanes]) * factor
        scores = jnp.where(allowed, scores, NEG)
        peak = jnp.max(scores, axis=1, keepdims=True)
        weights = jnp.exp(jnp.where(allowed, scores - peak, NEG))
        out[:, lanes] = dot(weights.astype(BF16), pair[:, there])
        kept = jnp.where(lane == h, peak, kept)
        kept = jnp.where(lane == heads + h, jnp.sum(weights, axis=1, keepdims=True), kept)
    stats[...] = kept


def merge_and_project(draft_out, draft_stats, wo, partials, projected, wo_v, sems):
    count, width, columns = wo_v.shape
    heads = width // HEAD_DIM
    copies = []
    for k in range(count):
        copy = pltpu.make_async_copy(
            wo.at[:, pl.ds(k * columns, columns)], wo_v.at[k], sems.at[k]
        )
        copy.start()
        copies.append(copy)
    parts = range(partials.shape[0])
    stats = [partials[s, :, width:].astype(F32) for s in parts]
    own_stats = draft_stats[...]
    attention = []
    for h in range(heads):
        lanes = slice(h * HEAD_DIM, (h + 1) * HEAD_DIM)
        peaks = [s[:, h : h + 1] for s in stats] + [own_stats[:, h : h + 1]]
        highest = functools.reduce(jnp.maximum, peaks)
        scales = [jnp.exp(peak - highest) for peak in peaks]
        total = own_stats[:, heads + h : heads + h + 1] * scales[-1]
        summed = draft_out[:, lanes] * scales[-1]
        for at in parts:
            s = stats[at]
            own_total = s[:, heads + h : heads + h + 1] + s[:, 2 * heads + h : 2 * heads + h + 1]
            total = total + own_total * scales[at]
            summed = summed + partials[at, :, lanes].astype(F32) * scales[at]
        attention.append((summed / total).astype(BF16))
    attention = jnp.concatenate(attention, axis=1)
    for k in range(count):
        copies[k].wait()
        projected[k] = dot(attention, wo_v[k]).astype(projected.dtype)


def add_up(parts, summed, power):
    total = sum(parts[k].astype(F32) for k in range(parts.shape[0]))
    summed[...] = total
    own_power = jnp.broadcast_to(sum_squares(total), power.shape[1:])
    for k in range(power.shape[0]):
        power[k] = own_power


def finish(model_width, summed, gain, hidden, powers, out):
    columns = summed.shape[1]
    power = sum(powers[k] for k in range(powers.shape[0]))[:, :1]
    start = pl.multiple_of(lax.axis_index("tp") * columns, columns)
    normed = summed[...] * lax.rsqrt(power / model_width + EPS) * gain[...]
    out[...] = (hidden[:, pl.ds(start, columns)].astype(F32) + normed).astype(BF16)


def compact(group, targets, key_cache, value_cache, keys_values, new_keys, new_values):
    requests, block, width = key_cache.shape
    own = keys_values.shape[1]
    me = lax.axis_index("seq")
    place = me * block + iota((block, group * own), 0)
    for request in range(requests):
        kv = stacked([keys_values[request * group + j] for j in range(group)])
        placing = place == targets[request]
        written = jnp.max(placing.astype(F32), axis=1, keepdims=True) > 0.5
        fresh = dot(placing.astype(BF16), kv)
        new_keys[request] = jnp.where(
            written, fresh[:, :width], key_cache[request].astype(F32)
        ).astype(BF16)
        new_values[request] = jnp.where(
            written, fresh[:, width:], value_cache[request].astype(F32)
        ).astype(BF16)


def shaped(shape, dtype):
    return jax.ShapeDtypeStruct(shape, dtype)


def body_general(
    hidden_in,
    query_weight,
    key_weight,
    value_weight,
    out_weight,
    query_gain,
    key_gain,
    post_gain,
    key_cache,
    value_cache,
    cache_lengths,
    parents,
    accepted_leaf,
):
    requests, block, width = key_cache.shape
    draft = parents.shape[1]
    own, model = hidden_in.shape
    tp = lax.axis_size("tp")
    seq = lax.axis_size("seq")
    group = draft // own
    columns = model // tp
    chunks = 4
    depth = model // chunks

    def exchange(x, axis):
        return lax.all_to_all(x, axis, 0, 0, tiled=True)

    query_raw, key_raw, squares = pl.pallas_call(
        project_qk,
        out_shape=(
            shaped((own, width), F32),
            shaped((own, width), F32),
            shaped((tp, own, LANES), F32),
        ),
        in_specs=[VMEM, ANY, ANY],
        out_specs=(VMEM, VMEM, VMEM),
        scratch_shapes=[
            pltpu.VMEM((chunks, depth, width), BF16),
            pltpu.VMEM((chunks, depth, width), BF16),
            pltpu.SemaphoreType.DMA((2 * chunks,)),
        ],
        compiler_params=params(56),
        cost_estimate=pl.CostEstimate(
            flops=4 * own * model * width, bytes_accessed=4 * model * width, transcendentals=0
        ),
        name="project_qk",
    )(hidden_in, query_weight, key_weight)
    squares = exchange(squares, "tp")

    exponents = -2.0 * (jnp.arange(HEAD_DIM) % (HEAD_DIM // 2)).astype(F32) / HEAD_DIM
    freqs = (THETA**exponents)[None, :]
    value, own_tree, targets, cosine, sine = pl.pallas_call(
        project_v_and_tree,
        out_shape=(
            shaped((own, width), BF16),
            shaped((own, draft), F32),
            shaped((requests, 1, draft), jnp.int32),
            shaped((own, HEAD_DIM), F32),
            shaped((own, HEAD_DIM), F32),
        ),
        in_specs=[SMEM, SMEM, VMEM, VMEM, VMEM, ANY],
        out_specs=(VMEM,) * 5,
        scratch_shapes=[
            pltpu.VMEM((chunks, depth, width), BF16),
            pltpu.VMEM((requests * draft, draft), F32),
            pltpu.SemaphoreType.DMA((chunks,)),
        ],
        compiler_params=params(16),
        cost_estimate=pl.CostEstimate(
            flops=2 * own * model * width, bytes_accessed=2 * model * width, transcendentals=0
        ),
        name="project_v_and_tree",
    )(cache_lengths, accepted_leaf, hidden_in, parents, freqs, value_weight)

    queries, keys_values = pl.pallas_call(
        functools.partial(prepare, tp * width),
        out_shape=(shaped((seq, own, width), BF16), shaped((seq, own, 2 * width), BF16)),
        in_specs=[VMEM] * 8,
        out_specs=(VMEM, VMEM),
        compiler_params=params(16),
        name="prepare",
    )(
        query_raw,
        key_raw,
        value,
        query_gain[None, :],
        key_gain[None, :],
        cosine,
        sine,
        squares,
    )
    queries = exchange(queries, "seq")
    keys_values = exchange(keys_values, "seq")

    partials = pl.pallas_call(
        functools.partial(attend_cache, group),
        out_shape=shaped((seq, own, width + LANES), BF16),
        in_specs=[SMEM, VMEM, VMEM, VMEM],
        out_specs=VMEM,
        compiler_params=params(16),
        name="attend_cache",
    )(cache_lengths, key_cache, value_cache, queries)
    partials = exchange(partials, "seq")

    draft_out, draft_stats = pl.pallas_call(
        functools.partial(attend_draft, group),
        out_shape=(shaped((own, width), F32), shaped((own, LANES), F32)),
        in_specs=[VMEM] * 3,
        out_specs=(VMEM, VMEM),
        compiler_params=params(16),
        name="attend_draft",
    )(own_tree, queries, keys_values)

    projected = pl.pallas_call(
        merge_and_project,
        out_shape=shaped((tp, own, columns), BF16),
        in_specs=[VMEM, VMEM, ANY, VMEM],
        out_specs=VMEM,
        scratch_shapes=[
            pltpu.VMEM((tp, width, columns), BF16),
            pltpu.SemaphoreType.DMA((tp,)),
        ],
        compiler_params=params(16),
        name="merge_and_project",
    )(draft_out, draft_stats, out_weight, partials)
    projected = exchange(projected, "tp")

    summed, power = pl.pallas_call(
        add_up,
        out_shape=(shaped((own, columns), F32), shaped((tp, own, LANES), F32)),
        in_specs=[VMEM],
        out_specs=(VMEM, VMEM),
        compiler_params=params(16),
        name="add_up",
    )(projected)
    power = exchange(power, "tp")

    hidden_out = pl.pallas_call(
        functools.partial(finish, model),
        out_shape=shaped((own, columns), BF16),
        in_specs=[VMEM] * 4,
        out_specs=VMEM,
        compiler_params=params(16),
        name="finish",
    )(summed, post_gain[None, :], hidden_in, power)

    new_key_cache, new_value_cache = pl.pallas_call(
        functools.partial(compact, group),
        out_shape=(shaped(key_cache.shape, BF16), shaped(value_cache.shape, BF16)),
        in_specs=[VMEM] * 4,
        out_specs=(VMEM, VMEM),
        compiler_params=params(24),
        name="compact",
    )(targets, key_cache, value_cache, keys_values)
    return (hidden_out, new_key_cache, new_value_cache)


def across(column):
    rows = column.shape[0]
    eye = iota((rows, rows), 0) == iota((rows, rows), 1)
    return jnp.sum(jnp.where(eye, column, 0.0), axis=0, keepdims=True)


def upright(line):
    rows = line.shape[1]
    eye = iota((rows, rows), 0) == iota((rows, rows), 1)
    return jnp.sum(jnp.where(eye, line, 0.0), axis=1, keepdims=True)


def eye_of(size):
    return (iota((size, size), 0) == iota((size, size), 1)).astype(BF16)


def plane():
    return lax.axis_index("seq") // 2


def twin_project_qk(hidden, wq, wk, query_raw, key_raw, squares):
    rows = hidden[...]
    own = rows.shape[0]
    for at, (weight, raw) in enumerate(((wq, query_raw), (wk, key_raw))):
        product = dot(rows, weight[...])
        raw[...] = product
        line = across(sum_squares(product))
        line = jnp.concatenate([line, jnp.zeros((1, LANES - own), F32)], axis=1)
        squares[:, at * LANES : (at + 1) * LANES] = jnp.broadcast_to(
            line, (squares.shape[0], LANES)
        )


def twin_project_v(hidden, wv, value):
    value[...] = dot(hidden[...], wv[...]).astype(BF16)


def twin_tree(
    turns, lengths, leaves, parents, freqs, own_tree, targets, cosine, sine, limits, held
):
    requests, draft = parents.shape
    own = own_tree.shape[1]
    row, col = iota((draft, draft), 0), iota((draft, draft), 1)
    eye = eye_of(draft)

    def length_of(request):
        picked = iota(lengths.shape, 1) == request
        return jnp.sum(jnp.where(picked, lengths[...], 0), axis=1, keepdims=True)

    for at, turn in enumerate(turns):
        limits[at : at + 1, :] = jnp.broadcast_to(
            length_of(plane() ^ turn), (1, limits.shape[1])
        )
    trees = [
        jnp.where((parents[pl.ds(r, 1), :] == row) | (row == col), 1.0, 0.0).astype(BF16)
        for r in range(requests)
    ]
    for _ in range(max(1, (draft - 1).bit_length())):
        trees = [jnp.minimum(dot(tree, tree), 1.0).astype(BF16) for tree in trees]
    for r in range(requests):
        standing = lax.dot_general(
            trees[r], eye, (((0,), (0,)), ((), ())), preferred_element_type=F32
        )
        held[r] = standing
        level = jnp.sum(trees[r].astype(F32), axis=0, keepdims=True) - 1.0
        on_path = jnp.where(row == leaves[:, r : r + 1], standing, 0.0)
        on_path = jnp.sum(on_path, axis=0, keepdims=True)
        place = lengths[:, r : r + 1] + level.astype(jnp.int32)
        targets[r] = jnp.where(on_path > 0.5, place, -1)
    within = lax.rem(lax.axis_index("seq"), 2)
    for at in range(2):
        first = (within ^ at) * own
        rows = held[plane(), pl.ds(pl.multiple_of(first, own), own), :]
        own_tree[at * own : (at + 1) * own, :] = jnp.where(
            within == 0, rows[:, :own], rows[:, own:]
        )
        mine = rows if at == 0 else mine
    level = jnp.sum(mine, axis=1, keepdims=True) - 1.0
    angles = (length_of(plane()).astype(F32) + level) * freqs[...]
    cosine[...] = jnp.cos(angles)
    half = jnp.sin(angles)
    sine[...] = jnp.where(iota(half.shape, 1) < HEAD_DIM // 2, -half, half)


def turned(raw, scale, gain, cos, sin):
    x = raw * scale * gain
    return (x * cos + pltpu.roll(x, HEAD_DIM // 2, 1) * sin).astype(BF16)


def twin_prepare(width_all, query_raw, key_raw, value, q_gain, k_gain, cosine, sine, *refs):
    squares, (queries, packed) = refs[:-2], refs[-2:]
    own, width = query_raw.shape
    cos, sin = cosine[...], sine[...]
    total = sum(ref[:1, :] for ref in squares)
    for at, (raw, gain) in enumerate(((query_raw, q_gain), (key_raw, k_gain))):
        scale = upright(total[:, at * LANES : at * LANES + own])
        scale = lax.rsqrt(scale / width_all + EPS)
        for h in range(width // HEAD_DIM):
            lanes = slice(h * HEAD_DIM, (h + 1) * HEAD_DIM)
            there = slice(at * width + h * HEAD_DIM, at * width + (h + 1) * HEAD_DIM)
            found = turned(raw[:, lanes], scale, gain[:, lanes], cos, sin)
            packed[:, there] = found
            if at == 0:
                queries[:, lanes] = found
    packed[:, 2 * width :] = value[...]


def weigh(s, visible):
    peak = jnp.max(s, axis=1, keepdims=True).astype(BF16).astype(F32)
    weights = jnp.exp(jnp.where(visible, s - peak, NEG))
    total = jnp.sum(weights, axis=1, keepdims=True)
    high = total.astype(BF16).astype(F32)
    return weights.astype(BF16), (peak, high, total - high)


def kept(stats, h, heads, found):
    lane = iota(stats.shape, 1)
    for at, column in enumerate(found):
        stats = jnp.where(lane == at * heads + h, column, stats)
    return stats


def write_stats(stats, out):
    own, width = stats.shape[0], out.shape[1]
    flat = lax.dot_general(
        stats.astype(BF16), eye_of(own), (((0,), (0,)), ((), ())), preferred_element_type=F32
    )
    flat = jnp.concatenate([flat[:16], jnp.zeros((16, width - own), F32)], axis=1)
    out[own : own + 16, :] = flat.astype(BF16)


def twin_attend_far(turns, limits, key_cache, value_cache, swapped, *refs):
    count = len(turns)
    queries, outs, scores = refs[:count], refs[count : 2 * count], refs[2 * count]
    block, width = key_cache.shape[1:]
    heads = width // HEAD_DIM
    own = queries[0].shape[0]
    me = lax.axis_index("seq")
    factor = 1.0 / math.sqrt(HEAD_DIM)
    place = iota((1, block), 1)
    both = jnp.concatenate([me * block + place, (me ^ 1) * block + place], axis=1)
    visible = [both < limits[at + 1 : at + 2, :] for at in range(count)]
    for at, turn in enumerate(turns):
        for h in range(heads):
            lanes = slice(h * HEAD_DIM, (h + 1) * HEAD_DIM)
            q = queries[at][:, lanes]
            first = dot_t(q, key_cache[plane() ^ turn, :, lanes])
            second = dot_t(q, swapped[at, 0, :, lanes])
            product = jnp.concatenate([first, second], axis=1) * factor
            scores[at, h] = jnp.where(visible[at], product, NEG)
    for at, turn in enumerate(turns):
        stats = jnp.zeros((own, LANES), F32)
        for h in range(heads):
            lanes = slice(h * HEAD_DIM, (h + 1) * HEAD_DIM)
            weights, found = weigh(scores[at, h], visible[at])
            out = dot(weights[:, :block], value_cache[plane() ^ turn, :, lanes])
            out = out + dot(weights[:, block:], swapped[at, 1, :, lanes])
            outs[at][:own, lanes] = out.astype(BF16)
            stats = kept(stats, h, heads, found)
        write_stats(stats, outs[at])


def twin_attend_near(limits, key_cache, value_cache, own_tree, mine, other, *refs):
    queries, (crossing, local, copied, own_scores) = refs[:-4], refs[-4:]
    count = len(queries)
    block, width = key_cache.shape[1:]
    heads = width // HEAD_DIM
    own = other.shape[0]
    factor = 1.0 / math.sqrt(HEAD_DIM)
    place = lax.axis_index("seq") * block + iota((1, block), 1)
    here = jnp.broadcast_to(place < limits[:1, :block], (2 * own, block))
    rest = own_scores.shape[2] - block - own
    near = jnp.concatenate(
        [jnp.where(here, 1.0, 0.0), own_tree[...], jnp.zeros((2 * own, rest), F32)], axis=1
    )
    near = near > 0.5
    pair = stacked([mine[:, :width], other[...]])
    for h in range(heads):
        lanes = slice(h * HEAD_DIM, (h + 1) * HEAD_DIM)
        keys = jnp.concatenate(
            [mine[:, width + h * HEAD_DIM : width + (h + 1) * HEAD_DIM]] * (1 + rest // own), axis=0
        )
        first = dot_t(pair[:, lanes], key_cache[plane(), :, lanes])
        product = jnp.concatenate([first, dot_t(pair[:, lanes], keys)], axis=1) * factor
        own_scores[h] = jnp.where(near, product, NEG)
    stats = jnp.zeros((2 * own, LANES), F32)
    for h in range(heads):
        lanes = slice(h * HEAD_DIM, (h + 1) * HEAD_DIM)
        weights, found = weigh(own_scores[h], near)
        out = dot(weights[:, :block], value_cache[plane(), :, lanes])
        values = mine[:, 2 * width + h * HEAD_DIM : 2 * width + (h + 1) * HEAD_DIM]
        out = out + dot(weights[:, block : block + own], values)
        out = out.astype(BF16)
        local[:own, lanes] = out[:own]
        crossing[:own, lanes] = out[own:]
        stats = kept(stats, h, heads, found)
    write_stats(stats[:own], local)
    write_stats(stats[own:], crossing)
    for at, ref in enumerate((mine, *queries)):
        for part in range(2):
            rows = slice((2 * at + part) * own, (2 * at + part + 1) * own)
            copied[rows, :] = ref[:, (part + 1) * width : (part + 2) * width]
    last = 2 * (count + 1) * own
    copied[last:, :] = jnp.zeros((copied.shape[0] - last, width), BF16)


def twin_rows(mine, theirs, held):
    within = lax.rem(lax.axis_index("seq"), 2)
    held[within] = mine
    held[1 - within] = theirs
    return stacked([held[0], held[1]])


def twin_merge_and_project(*refs):
    partials, (wo, total_out, rounded) = refs[:-3], refs[-3:]
    own, width = total_out.shape[0], partials[0].shape[1]
    heads = width // HEAD_DIM
    stats = [dot_t(eye_of(own), ref[own : own + 16, :own]) for ref in partials]
    attention = []
    for h in range(heads):
        lanes = slice(h * HEAD_DIM, (h + 1) * HEAD_DIM)
        peaks = [s[:, h : h + 1] for s in stats]
        highest = functools.reduce(jnp.maximum, peaks)
        total, summed = 0.0, 0.0
        for ref, s, peak in zip(partials, stats, peaks):
            scale = jnp.exp(peak - highest)
            own_total = s[:, heads + h : heads + h + 1] + s[:, 2 * heads + h : 2 * heads + h + 1]
            total = total + own_total * scale
            summed = summed + ref[:own, lanes].astype(F32) * scale
        attention.append((summed / total).astype(BF16))
    product = dot(jnp.concatenate(attention, axis=1), wo[...])
    total_out[...] = product
    rounded[...] = product.astype(BF16)


def own_half(width):
    half = width // 2
    return pl.ds(pl.multiple_of(lax.rem(lax.axis_index("tp"), 2) * half, half), half)


def other_half(width):
    half = width // 2
    return pl.ds(pl.multiple_of((1 - lax.rem(lax.axis_index("tp"), 2)) * half, half), half)


def twin_add(mine, theirs, total, rounded):
    width = mine.shape[1]
    total[...] = mine[...] + theirs[...].astype(F32)
    lanes = own_half(width)
    rounded[...] = (mine[:, lanes] + theirs[:, lanes].astype(F32)).astype(BF16)


def twin_finish(mine, here, passed, gain, hidden, out, total):
    model_width = mine.shape[1]
    columns = out.shape[1]
    square = 0.0
    for lanes, ref in ((own_half(model_width), here), (other_half(model_width), passed)):
        both = mine[:, lanes] + ref[...].astype(F32)
        total[:, lanes] = both
        square = square + sum_squares(both)
    scale = lax.rsqrt(square / model_width + EPS)
    lanes = pl.ds(pl.multiple_of(lax.axis_index("tp") * columns, columns), columns)
    normed = total[:, lanes] * scale * gain[...]
    out[...] = (hidden[:, lanes].astype(F32) + normed).astype(BF16)


def twin_compact(far, targets, key_cache, value_cache, *refs):
    count = len(far) + 1
    ours, (copied, new_keys, new_values, held) = refs[:count], refs[count:]
    block, width = key_cache.shape[1:]
    own = ours[0].shape[0]
    me = lax.axis_index("seq")
    place = me * block + iota((block, targets.shape[2]), 0)
    for at, turn in enumerate((0, *far)):
        request = plane() ^ turn
        placing = place == targets[request]
        written = jnp.max(placing.astype(F32), axis=1, keepdims=True) > 0.5
        placing = placing.astype(BF16)
        for part, (cache, out) in enumerate(((key_cache, new_keys), (value_cache, new_values))):
            lanes = slice((part + 1) * width, (part + 2) * width)
            rows = slice((2 * at + part) * own, (2 * at + part + 1) * own)
            theirs = copied[rows, :]
            fresh = twin_rows(ours[at][:, lanes], theirs, held.at[at, part])
            moved = dot(placing, fresh)
            out[request] = jnp.where(written, moved, cache[request].astype(F32)).astype(BF16)


def body_twin(
    hidden_in,
    query_weight,
    key_weight,
    value_weight,
    out_weight,
    query_gain,
    key_gain,
    post_gain,
    key_cache,
    value_cache,
    cache_lengths,
    parents,
    accepted_leaf,
):
    requests, block, width = key_cache.shape
    draft = parents.shape[1]
    own, model = hidden_in.shape
    tp = lax.axis_size("tp")
    seq = lax.axis_size("seq")
    columns = model // tp
    heads = width // HEAD_DIM
    far = tuple(range(requests - 1, 0, -1))

    def call(kernel, outs, inputs, scratch=(), mib=16, specs=None, ties=()):
        count = len(inputs)

        def run(*refs):
            kernel(*refs[:count], *refs[count + len(ties) :])

        return pl.pallas_call(
            run,
            out_shape=outs,
            in_specs=([VMEM] * count if specs is None else specs) + [ANY] * len(ties),
            out_specs=jax.tree.map(lambda _: VMEM, outs),
            scratch_shapes=list(scratch),
            compiler_params=params(mib),
            name=getattr(kernel, "func", kernel).__name__,
        )(*inputs, *ties)

    def over_tp(x, k):
        return lax.ppermute(x, "tp", [(i, i ^ k) for i in range(tp)])

    def beside(x):
        return lax.ppermute(x, "seq", [(i, i ^ 1) for i in range(seq)])

    def over_planes(x, turn):
        return lax.ppermute(x, "seq", [(i, (i // 2 ^ turn) * 2 + i % 2) for i in range(seq)])

    me = lax.axis_index("seq") // 2

    def picked(turns):
        parts = [
            [lax.dynamic_index_in_dim(x, me ^ turn, 0, False) for x in (key_cache, value_cache)]
            for turn in turns
        ]
        return jnp.stack([jnp.stack(part) for part in parts])

    swapped = beside(picked(far))
    query_raw, key_raw, squares = call(
        twin_project_qk,
        (shaped((own, width), F32), shaped((own, width), F32), shaped((8, 2 * LANES), F32)),
        (hidden_in, query_weight, key_weight),
    )
    all_squares = [squares] + [over_tp(squares, k) for k in range(tp - 1, 0, -1)]

    exponents = -2.0 * (jnp.arange(HEAD_DIM) % (HEAD_DIM // 2)).astype(F32) / HEAD_DIM
    freqs = (THETA**exponents)[None, :]
    own_tree, targets, cosine, sine, limits = call(
        functools.partial(twin_tree, (0, *far)),
        (
            shaped((draft, own), F32),
            shaped((requests, 1, draft), jnp.int32),
            shaped((own, HEAD_DIM), F32),
            shaped((own, HEAD_DIM), F32),
            shaped((requests, 2 * block), jnp.int32),
        ),
        (cache_lengths[None, :], accepted_leaf[None, :], parents, freqs),
        [pltpu.VMEM((requests, draft, draft), F32)],
    )
    value = call(twin_project_v, shaped((own, width), BF16), (hidden_in, value_weight))
    queries, packed = call(
        functools.partial(twin_prepare, tp * width),
        (shaped((own, width), BF16), shaped((own, 3 * width), BF16)),
        (
            query_raw,
            key_raw,
            value,
            query_gain[None, :],
            key_gain[None, :],
            cosine,
            sine,
            *all_squares,
        ),
    )
    from_far = [over_planes(packed, turn) for turn in far]
    other = beside(queries)

    rows = own + 16
    partials = call(
        functools.partial(twin_attend_far, far),
        (shaped((rows, width), BF16),) * len(far),
        (limits, key_cache, value_cache, swapped, *from_far),
        [pltpu.VMEM((len(far), heads, own, 2 * block), F32)],
    )
    crossing, local, copied = call(
        twin_attend_near,
        (shaped((rows, width), BF16),) * 2 + (shaped((2 * requests * own + own, width), BF16),),
        (limits, key_cache, value_cache, own_tree, packed, other, *from_far),
        [pltpu.VMEM((heads, 2 * own, block + LANES), F32)],
        ties=partials[:1],
    )
    partials = [over_planes(part, turn) for part, turn in zip(partials, far)]
    partials += [beside(crossing)]
    partials = [partials[0], partials[1], partials[3], partials[2], local]
    copied = beside(copied)

    total, rounded = call(
        twin_merge_and_project,
        (shaped((own, model), F32), shaped((own, model), BF16)),
        (*partials, out_weight),
    )
    total, rounded = call(
        twin_add,
        (shaped((own, model), F32), shaped((own, model // 2), BF16)),
        (total, over_tp(rounded, 1)),
    )
    here = over_tp(rounded, 2)
    new_key_cache, new_value_cache = call(
        functools.partial(twin_compact, far),
        (shaped(key_cache.shape, BF16), shaped(value_cache.shape, BF16)),
        (targets, key_cache, value_cache, packed, *from_far, copied),
        [pltpu.VMEM((requests, 2, 2, own, width), BF16)],
    )
    ready, new_key_cache = lax.optimization_barrier((here, new_key_cache))
    passed = over_tp(ready, 1)
    hidden_out = call(
        twin_finish,
        shaped((own, columns), BF16),
        (total, here, passed, post_gain[None, :], hidden_in),
        [pltpu.VMEM((own, model), F32)],
    )
    return (hidden_out, new_key_cache, new_value_cache)


def body(*args):
    hidden_in, key_cache, parents = args[0], args[8], args[11]
    tp = lax.axis_size("tp")
    own, draft = hidden_in.shape[0], parents.shape[1]
    requests, _, width = key_cache.shape
    twin = (
        own % 16 == 0
        and draft == 2 * own
        and requests == 4
        and lax.axis_size("seq") == 2 * requests
        and own <= LANES
        and LANES % own == 0
        and own <= width
        and 3 * (width // HEAD_DIM) <= 16
        and tp == 4
    )
    return (body_twin if twin else body_general)(*args)


def solution(mesh):
    return jax.shard_map(
        body,
        mesh=mesh,
        in_specs=(
            P("seq", None),
            P(None, "tp"),
            P(None, "tp"),
            P(None, "tp"),
            P("tp", None),
            P("tp"),
            P("tp"),
            P("tp"),
            P(None, "seq", "tp"),
            P(None, "seq", "tp"),
            P(),
            P(),
            P(),
        ),
        out_specs=(P("seq", "tp"), P(None, "seq", "tp"), P(None, "seq", "tp")),
        check_vma=False,
    )
```

```python
import functools
import math

import jax
import jax.numpy as jnp
from jax import lax
from jax.experimental import pallas as pl
from jax.experimental.pallas import tpu as pltpu
from jax.sharding import PartitionSpec as P

HEAD_DIM = 128
LANES = 128
EPS = 1e-06
THETA = 500000.0
NEG = -1e30
F32 = jnp.float32
BF16 = jnp.bfloat16
VMEM = pl.BlockSpec(memory_space=pltpu.VMEM)
SMEM = pl.BlockSpec(memory_space=pltpu.SMEM)
ANY = pl.BlockSpec(memory_space=pl.ANY)


def params(mib):
    return pltpu.CompilerParams(vmem_limit_bytes=mib * 1024 * 1024)


def dot(a, b):
    return jnp.dot(a, b, preferred_element_type=F32)


def dot_t(a, b):
    return lax.dot_general(a, b, (((1,), (1,)), ((), ())), preferred_element_type=F32)


def iota(shape, axis):
    return lax.broadcasted_iota(jnp.int32, shape, axis)


def stacked(parts):
    if len(parts) == 1:
        return parts[0]
    if parts[0].shape[0] % 16 == 0:
        return jnp.concatenate(parts, axis=0)
    return jnp.concatenate([part.astype(F32) for part in parts], axis=0).astype(BF16)


def sum_squares(raw):
    return jnp.sum(raw * raw, axis=1, keepdims=True)


def project_qk(hidden, wq, wk, query_raw, key_raw, squares, wq_v, wk_v, sems):
    chunks, depth = wq_v.shape[0], wq_v.shape[1]
    copies = []
    for c in range(chunks):
        for at, (source, target) in enumerate(((wq, wq_v), (wk, wk_v))):
            copy = pltpu.make_async_copy(
                source.at[pl.ds(c * depth, depth)], target.at[c], sems.at[2 * c + at]
            )
            copy.start()
            copies.append(copy)
    q_sum, k_sum = None, None
    for c in range(chunks):
        part = hidden[:, c * depth : (c + 1) * depth]
        copies[2 * c].wait()
        q = dot(part, wq_v[c])
        copies[2 * c + 1].wait()
        k = dot(part, wk_v[c])
        q_sum = q if c == 0 else q_sum + q
        k_sum = k if c == 0 else k_sum + k
    query_raw[...] = q_sum
    key_raw[...] = k_sum
    lane = iota(squares.shape[1:], 1)
    both = jnp.where(lane == 0, sum_squares(q_sum), sum_squares(k_sum))
    for t in range(squares.shape[0]):
        squares[t] = both


def project_v_and_tree(
    lengths, leaves, hidden, parents, freqs, wv, value, own_tree, targets, cosine, sine, wv_v, anc_v, sems
):
    chunks, depth = wv_v.shape[0], wv_v.shape[1]
    copies = []
    for c in range(chunks):
        copy = pltpu.make_async_copy(wv.at[pl.ds(c * depth, depth)], wv_v.at[c], sems.at[c])
        copy.start()
        copies.append(copy)
    requests, draft = parents.shape
    own = hidden.shape[0]
    first = lax.axis_index("seq") * own
    row, col = iota((draft, draft), 0), iota((draft, draft), 1)
    eye = (row == col).astype(BF16)
    trees = [
        jnp.where((parents[pl.ds(r, 1), :] == row) | (row == col), 1.0, 0.0).astype(BF16)
        for r in range(requests)
    ]
    for _ in range(max(1, (draft - 1).bit_length())):
        trees = [jnp.minimum(dot(tree, tree), 1.0).astype(BF16) for tree in trees]
    for r in range(requests):
        upright = lax.dot_general(
            trees[r], eye, (((0,), (0,)), ((), ())), preferred_element_type=F32
        )
        anc_v[pl.ds(r * draft, draft), :] = upright
        level = jnp.sum(trees[r].astype(F32), axis=0, keepdims=True) - 1.0
        on_path = jnp.sum(jnp.where(row == leaves[r], upright, 0.0), axis=0, keepdims=True)
        place = lengths[r] + level.astype(jnp.int32)
        targets[r] = jnp.where(on_path > 0.5, place, -1)
    mine = anc_v[pl.ds(pl.multiple_of(first, own), own), :]
    own_tree[...] = mine
    level = jnp.sum(mine, axis=1, keepdims=True) - 1.0
    position = lengths[first // draft].astype(F32) + level
    angles = position * freqs[...]
    cosine[...] = jnp.cos(angles)
    half = jnp.sin(angles)
    sine[...] = jnp.where(iota(half.shape, 1) < HEAD_DIM // 2, -half, half)
    total = None
    for c in range(chunks):
        copies[c].wait()
        v = dot(hidden[:, c * depth : (c + 1) * depth], wv_v[c])
        total = v if c == 0 else total + v
    value[...] = total.astype(BF16)


def prepare(
    width_all, query_raw, key_raw, value, q_gain, k_gain, cosine, sine, squares, queries, keys_values
):
    width = query_raw.shape[1]
    total = sum(squares[k] for k in range(squares.shape[0]))
    cos, sin = cosine[...], sine[...]
    for at, (raw, gain, out) in enumerate(
        ((query_raw, q_gain, queries), (key_raw, k_gain, keys_values))
    ):
        scale = lax.rsqrt(total[:, at : at + 1] / width_all + EPS)
        for h in range(width // HEAD_DIM):
            lanes = slice(h * HEAD_DIM, (h + 1) * HEAD_DIM)
            x = raw[:, lanes] * scale * gain[:, lanes]
            turned = x * cos + pltpu.roll(x, HEAD_DIM // 2, 1) * sin
            turned = turned.astype(BF16)
            for s in range(out.shape[0]):
                out[s, :, lanes] = turned
    for s in range(keys_values.shape[0]):
        keys_values[s, :, width:] = value[...]


def attend_cache(group, lengths, key_cache, value_cache, queries, partials):
    requests, block, width = key_cache.shape
    own = queries.shape[1]
    heads = width // HEAD_DIM
    me = lax.axis_index("seq")
    factor = 1.0 / math.sqrt(HEAD_DIM)
    rows = group * own
    place = me * block + iota((rows, block), 1)
    lane = iota((rows, LANES), 1)
    for request in range(requests):
        q = stacked([queries[request * group + j] for j in range(group)])
        visible = place < lengths[request]
        stats = jnp.zeros((rows, LANES), F32)
        for h in range(heads):
            lanes = slice(h * HEAD_DIM, (h + 1) * HEAD_DIM)
            scores = dot_t(q[:, lanes], key_cache[request, :, lanes]) * factor
            scores = jnp.where(visible, scores, NEG)
            peak = jnp.max(scores, axis=1, keepdims=True).astype(BF16).astype(F32)
            weights = jnp.exp(jnp.where(visible, scores - peak, NEG))
            total = jnp.sum(weights, axis=1, keepdims=True)
            high = total.astype(BF16).astype(F32)
            out = dot(weights.astype(BF16), value_cache[request, :, lanes]).astype(BF16)
            for j in range(group):
                partials[request * group + j, :, lanes] = out[j * own : (j + 1) * own]
            stats = jnp.where(lane == h, peak, stats)
            stats = jnp.where(lane == heads + h, high, stats)
            stats = jnp.where(lane == 2 * heads + h, total - high, stats)
        stats = stats.astype(BF16)
        for j in range(group):
            partials[request * group + j, :, width:] = stats[j * own : (j + 1) * own]


def attend_draft(group, own_tree, queries, keys_values, out, stats):
    own, width = queries.shape[1:]
    heads = width // HEAD_DIM
    me = lax.axis_index("seq")
    first = me // group * group
    q = queries[me]
    pair = stacked([keys_values[first + j] for j in range(group)])
    factor = 1.0 / math.sqrt(HEAD_DIM)
    allowed = own_tree[...] > 0.5
    lane = iota((own, LANES), 1)
    kept = jnp.zeros((own, LANES), F32)
    for h in range(heads):
        lanes = slice(h * HEAD_DIM, (h + 1) * HEAD_DIM)
        there = slice(width + h * HEAD_DIM, width + (h + 1) * HEAD_DIM)
        scores = dot_t(q[:, lanes], pair[:, lanes]) * factor
        scores = jnp.where(allowed, scores, NEG)
        peak = jnp.max(scores, axis=1, keepdims=True)
        weights = jnp.exp(jnp.where(allowed, scores - peak, NEG))
        out[:, lanes] = dot(weights.astype(BF16), pair[:, there])
        kept = jnp.where(lane == h, peak, kept)
        kept = jnp.where(lane == heads + h, jnp.sum(weights, axis=1, keepdims=True), kept)
    stats[...] = kept


def merge_and_project(draft_out, draft_stats, wo, partials, projected, wo_v, sems):
    count, width, columns = wo_v.shape
    heads = width // HEAD_DIM
    copies = []
    for k in range(count):
        copy = pltpu.make_async_copy(
            wo.at[:, pl.ds(k * columns, columns)], wo_v.at[k], sems.at[k]
        )
        copy.start()
        copies.append(copy)
    parts = range(partials.shape[0])
    stats = [partials[s, :, width:].astype(F32) for s in parts]
    own_stats = draft_stats[...]
    attention = []
    for h in range(heads):
        lanes = slice(h * HEAD_DIM, (h + 1) * HEAD_DIM)
        peaks = [s[:, h : h + 1] for s in stats] + [own_stats[:, h : h + 1]]
        highest = functools.reduce(jnp.maximum, peaks)
        scales = [jnp.exp(peak - highest) for peak in peaks]
        total = own_stats[:, heads + h : heads + h + 1] * scales[-1]
        summed = draft_out[:, lanes] * scales[-1]
        for at in parts:
            s = stats[at]
            own_total = s[:, heads + h : heads + h + 1] + s[:, 2 * heads + h : 2 * heads + h + 1]
            total = total + own_total * scales[at]
            summed = summed + partials[at, :, lanes].astype(F32) * scales[at]
        attention.append((summed / total).astype(BF16))
    attention = jnp.concatenate(attention, axis=1)
    for k in range(count):
        copies[k].wait()
        projected[k] = dot(attention, wo_v[k]).astype(projected.dtype)


def add_up(parts, summed, power):
    total = sum(parts[k].astype(F32) for k in range(parts.shape[0]))
    summed[...] = total
    own_power = jnp.broadcast_to(sum_squares(total), power.shape[1:])
    for k in range(power.shape[0]):
        power[k] = own_power


def finish(model_width, summed, gain, hidden, powers, out):
    columns = summed.shape[1]
    power = sum(powers[k] for k in range(powers.shape[0]))[:, :1]
    start = pl.multiple_of(lax.axis_index("tp") * columns, columns)
    normed = summed[...] * lax.rsqrt(power / model_width + EPS) * gain[...]
    out[...] = (hidden[:, pl.ds(start, columns)].astype(F32) + normed).astype(BF16)


def compact(group, targets, key_cache, value_cache, keys_values, new_keys, new_values):
    requests, block, width = key_cache.shape
    own = keys_values.shape[1]
    me = lax.axis_index("seq")
    place = me * block + iota((block, group * own), 0)
    for request in range(requests):
        kv = stacked([keys_values[request * group + j] for j in range(group)])
        placing = place == targets[request]
        written = jnp.max(placing.astype(F32), axis=1, keepdims=True) > 0.5
        fresh = dot(placing.astype(BF16), kv)
        new_keys[request] = jnp.where(
            written, fresh[:, :width], key_cache[request].astype(F32)
        ).astype(BF16)
        new_values[request] = jnp.where(
            written, fresh[:, width:], value_cache[request].astype(F32)
        ).astype(BF16)


def shaped(shape, dtype):
    return jax.ShapeDtypeStruct(shape, dtype)


def body_general(
    hidden_in,
    query_weight,
    key_weight,
    value_weight,
    out_weight,
    query_gain,
    key_gain,
    post_gain,
    key_cache,
    value_cache,
    cache_lengths,
    parents,
    accepted_leaf,
):
    requests, block, width = key_cache.shape
    draft = parents.shape[1]
    own, model = hidden_in.shape
    tp = lax.axis_size("tp")
    seq = lax.axis_size("seq")
    group = draft // own
    columns = model // tp
    chunks = 4
    depth = model // chunks

    def exchange(x, axis):
        return lax.all_to_all(x, axis, 0, 0, tiled=True)

    query_raw, key_raw, squares = pl.pallas_call(
        project_qk,
        out_shape=(
            shaped((own, width), F32),
            shaped((own, width), F32),
            shaped((tp, own, LANES), F32),
        ),
        in_specs=[VMEM, ANY, ANY],
        out_specs=(VMEM, VMEM, VMEM),
        scratch_shapes=[
            pltpu.VMEM((chunks, depth, width), BF16),
            pltpu.VMEM((chunks, depth, width), BF16),
            pltpu.SemaphoreType.DMA((2 * chunks,)),
        ],
        compiler_params=params(56),
        cost_estimate=pl.CostEstimate(
            flops=4 * own * model * width, bytes_accessed=4 * model * width, transcendentals=0
        ),
        name="project_qk",
    )(hidden_in, query_weight, key_weight)
    squares = exchange(squares, "tp")

    exponents = -2.0 * (jnp.arange(HEAD_DIM) % (HEAD_DIM // 2)).astype(F32) / HEAD_DIM
    freqs = (THETA**exponents)[None, :]
    value, own_tree, targets, cosine, sine = pl.pallas_call(
        project_v_and_tree,
        out_shape=(
            shaped((own, width), BF16),
            shaped((own, draft), F32),
            shaped((requests, 1, draft), jnp.int32),
            shaped((own, HEAD_DIM), F32),
            shaped((own, HEAD_DIM), F32),
        ),
        in_specs=[SMEM, SMEM, VMEM, VMEM, VMEM, ANY],
        out_specs=(VMEM,) * 5,
        scratch_shapes=[
            pltpu.VMEM((chunks, depth, width), BF16),
            pltpu.VMEM((requests * draft, draft), F32),
            pltpu.SemaphoreType.DMA((chunks,)),
        ],
        compiler_params=params(16),
        cost_estimate=pl.CostEstimate(
            flops=2 * own * model * width, bytes_accessed=2 * model * width, transcendentals=0
        ),
        name="project_v_and_tree",
    )(cache_lengths, accepted_leaf, hidden_in, parents, freqs, value_weight)

    queries, keys_values = pl.pallas_call(
        functools.partial(prepare, tp * width),
        out_shape=(shaped((seq, own, width), BF16), shaped((seq, own, 2 * width), BF16)),
        in_specs=[VMEM] * 8,
        out_specs=(VMEM, VMEM),
        compiler_params=params(16),
        name="prepare",
    )(
        query_raw,
        key_raw,
        value,
        query_gain[None, :],
        key_gain[None, :],
        cosine,
        sine,
        squares,
    )
    queries = exchange(queries, "seq")
    keys_values = exchange(keys_values, "seq")

    partials = pl.pallas_call(
        functools.partial(attend_cache, group),
        out_shape=shaped((seq, own, width + LANES), BF16),
        in_specs=[SMEM, VMEM, VMEM, VMEM],
        out_specs=VMEM,
        compiler_params=params(16),
        name="attend_cache",
    )(cache_lengths, key_cache, value_cache, queries)
    partials = exchange(partials, "seq")

    draft_out, draft_stats = pl.pallas_call(
        functools.partial(attend_draft, group),
        out_shape=(shaped((own, width), F32), shaped((own, LANES), F32)),
        in_specs=[VMEM] * 3,
        out_specs=(VMEM, VMEM),
        compiler_params=params(16),
        name="attend_draft",
    )(own_tree, queries, keys_values)

    projected = pl.pallas_call(
        merge_and_project,
        out_shape=shaped((tp, own, columns), BF16),
        in_specs=[VMEM, VMEM, ANY, VMEM],
        out_specs=VMEM,
        scratch_shapes=[
            pltpu.VMEM((tp, width, columns), BF16),
            pltpu.SemaphoreType.DMA((tp,)),
        ],
        compiler_params=params(16),
        name="merge_and_project",
    )(draft_out, draft_stats, out_weight, partials)
    projected = exchange(projected, "tp")

    summed, power = pl.pallas_call(
        add_up,
        out_shape=(shaped((own, columns), F32), shaped((tp, own, LANES), F32)),
        in_specs=[VMEM],
        out_specs=(VMEM, VMEM),
        compiler_params=params(16),
        name="add_up",
    )(projected)
    power = exchange(power, "tp")

    hidden_out = pl.pallas_call(
        functools.partial(finish, model),
        out_shape=shaped((own, columns), BF16),
        in_specs=[VMEM] * 4,
        out_specs=VMEM,
        compiler_params=params(16),
        name="finish",
    )(summed, post_gain[None, :], hidden_in, power)

    new_key_cache, new_value_cache = pl.pallas_call(
        functools.partial(compact, group),
        out_shape=(shaped(key_cache.shape, BF16), shaped(value_cache.shape, BF16)),
        in_specs=[VMEM] * 4,
        out_specs=(VMEM, VMEM),
        compiler_params=params(24),
        name="compact",
    )(targets, key_cache, value_cache, keys_values)
    return (hidden_out, new_key_cache, new_value_cache)


def across(column):
    rows = column.shape[0]
    eye = iota((rows, rows), 0) == iota((rows, rows), 1)
    return jnp.sum(jnp.where(eye, column, 0.0), axis=0, keepdims=True)


def upright(line):
    rows = line.shape[1]
    eye = iota((rows, rows), 0) == iota((rows, rows), 1)
    return jnp.sum(jnp.where(eye, line, 0.0), axis=1, keepdims=True)


def eye_of(size):
    return (iota((size, size), 0) == iota((size, size), 1)).astype(BF16)


def plane():
    return lax.axis_index("seq") // 2


def twin_project_qk(hidden, wq, wk, query_raw, key_raw, squares):
    rows = hidden[...]
    own = rows.shape[0]
    for at, (weight, raw) in enumerate(((wq, query_raw), (wk, key_raw))):
        product = dot(rows, weight[...])
        raw[...] = product
        line = across(sum_squares(product))
        line = jnp.concatenate([line, jnp.zeros((1, LANES - own), F32)], axis=1)
        squares[:, at * LANES : (at + 1) * LANES] = jnp.broadcast_to(
            line, (squares.shape[0], LANES)
        )


def twin_project_v(hidden, wv, value):
    value[...] = dot(hidden[...], wv[...]).astype(BF16)


def twin_tree(
    turns, lengths, leaves, parents, freqs, own_tree, targets, cosine, sine, limits, held
):
    requests, draft = parents.shape
    own = own_tree.shape[1]
    row, col = iota((draft, draft), 0), iota((draft, draft), 1)
    eye = eye_of(draft)

    def length_of(request):
        picked = iota(lengths.shape, 1) == request
        return jnp.sum(jnp.where(picked, lengths[...], 0), axis=1, keepdims=True)

    for at, turn in enumerate(turns):
        limits[at : at + 1, :] = jnp.broadcast_to(
            length_of(plane() ^ turn), (1, limits.shape[1])
        )
    trees = [
        jnp.where((parents[pl.ds(r, 1), :] == row) | (row == col), 1.0, 0.0).astype(BF16)
        for r in range(requests)
    ]
    for _ in range(max(1, (draft - 1).bit_length())):
        trees = [jnp.minimum(dot(tree, tree), 1.0).astype(BF16) for tree in trees]
    for r in range(requests):
        standing = lax.dot_general(
            trees[r], eye, (((0,), (0,)), ((), ())), preferred_element_type=F32
        )
        held[r] = standing
        level = jnp.sum(trees[r].astype(F32), axis=0, keepdims=True) - 1.0
        on_path = jnp.where(row == leaves[:, r : r + 1], standing, 0.0)
        on_path = jnp.sum(on_path, axis=0, keepdims=True)
        place = lengths[:, r : r + 1] + level.astype(jnp.int32)
        targets[r] = jnp.where(on_path > 0.5, place, -1)
    within = lax.rem(lax.axis_index("seq"), 2)
    for at in range(2):
        first = (within ^ at) * own
        rows = held[plane(), pl.ds(pl.multiple_of(first, own), own), :]
        own_tree[at * own : (at + 1) * own, :] = jnp.where(
            within == 0, rows[:, :own], rows[:, own:]
        )
        mine = rows if at == 0 else mine
    level = jnp.sum(mine, axis=1, keepdims=True) - 1.0
    angles = (length_of(plane()).astype(F32) + level) * freqs[...]
    cosine[...] = jnp.cos(angles)
    half = jnp.sin(angles)
    sine[...] = jnp.where(iota(half.shape, 1) < HEAD_DIM // 2, -half, half)


def turned(raw, scale, gain, cos, sin):
    x = raw * scale * gain
    return (x * cos + pltpu.roll(x, HEAD_DIM // 2, 1) * sin).astype(BF16)


def twin_prepare(width_all, query_raw, key_raw, value, q_gain, k_gain, cosine, sine, *refs):
    squares, (queries, packed) = refs[:-2], refs[-2:]
    own, width = query_raw.shape
    cos, sin = cosine[...], sine[...]
    total = sum(ref[:1, :] for ref in squares)
    for at, (raw, gain) in enumerate(((query_raw, q_gain), (key_raw, k_gain))):
        scale = upright(total[:, at * LANES : at * LANES + own])
        scale = lax.rsqrt(scale / width_all + EPS)
        for h in range(width // HEAD_DIM):
            lanes = slice(h * HEAD_DIM, (h + 1) * HEAD_DIM)
            there = slice(at * width + h * HEAD_DIM, at * width + (h + 1) * HEAD_DIM)
            found = turned(raw[:, lanes], scale, gain[:, lanes], cos, sin)
            packed[:, there] = found
            if at == 0:
                queries[:, lanes] = found
    packed[:, 2 * width :] = value[...]


def weigh(s):
    peak = jnp.max(s, axis=1, keepdims=True).astype(BF16).astype(F32)
    weights = jnp.exp(s - jnp.maximum(peak, 0.1 * NEG))
    total = jnp.sum(weights, axis=1, keepdims=True)
    high = total.astype(BF16).astype(F32)
    return weights.astype(BF16), (peak, high, total - high)


def kept(stats, h, heads, found):
    lane = iota(stats.shape, 1)
    for at, column in enumerate(found):
        stats = jnp.where(lane == at * heads + h, column, stats)
    return stats


def write_stats(stats, out):
    own, width = stats.shape[0], out.shape[1]
    flat = lax.dot_general(
        stats.astype(BF16), eye_of(own), (((0,), (0,)), ((), ())), preferred_element_type=F32
    )
    flat = jnp.concatenate([flat[:16], jnp.zeros((16, width - own), F32)], axis=1)
    out[own : own + 16, :] = flat.astype(BF16)


def twin_attend_far(turns, limits, key_cache, value_cache, swapped, *refs):
    count = len(turns)
    queries, outs, scores = refs[:count], refs[count : 2 * count], refs[2 * count]
    block, width = key_cache.shape[1:]
    heads = width // HEAD_DIM
    own = queries[0].shape[0]
    me = lax.axis_index("seq")
    factor = 1.0 / math.sqrt(HEAD_DIM)
    place = iota((1, block), 1)
    both = jnp.concatenate([me * block + place, (me ^ 1) * block + place], axis=1)
    visible = [both < limits[at + 1 : at + 2, :] for at in range(count)]
    for at, turn in enumerate(turns):
        for h in range(heads):
            lanes = slice(h * HEAD_DIM, (h + 1) * HEAD_DIM)
            q = queries[at][:, lanes]
            first = dot_t(q, key_cache[plane() ^ turn, :, lanes])
            second = dot_t(q, swapped[2 * at, :, lanes])
            product = jnp.concatenate([first, second], axis=1) * factor
            scores[at, h] = jnp.where(visible[at], product, NEG)
    for at, turn in enumerate(turns):
        stats = jnp.zeros((own, LANES), F32)
        for h in range(heads):
            lanes = slice(h * HEAD_DIM, (h + 1) * HEAD_DIM)
            weights, found = weigh(scores[at, h])
            out = dot(weights[:, :block], value_cache[plane() ^ turn, :, lanes])
            out = out + dot(weights[:, block:], swapped[2 * at + 1, :, lanes])
            outs[at][:own, lanes] = out.astype(BF16)
            stats = kept(stats, h, heads, found)
        write_stats(stats, outs[at])


def twin_attend_near(limits, key_cache, value_cache, own_tree, mine, other, *refs):
    queries, (crossing, local, copied, own_scores) = refs[:-4], refs[-4:]
    count = len(queries)
    block, width = key_cache.shape[1:]
    heads = width // HEAD_DIM
    own = other.shape[0]
    factor = 1.0 / math.sqrt(HEAD_DIM)
    place = lax.axis_index("seq") * block + iota((1, block), 1)
    here = jnp.broadcast_to(place < limits[:1, :block], (2 * own, block))
    rest = own_scores.shape[2] - block - own
    near = jnp.concatenate(
        [jnp.where(here, 1.0, 0.0), own_tree[...], jnp.zeros((2 * own, rest), F32)], axis=1
    )
    near = near > 0.5
    pair = stacked([mine[:, :width], other[...]])
    for h in range(heads):
        lanes = slice(h * HEAD_DIM, (h + 1) * HEAD_DIM)
        keys = jnp.concatenate(
            [mine[:, width + h * HEAD_DIM : width + (h + 1) * HEAD_DIM]] * (1 + rest // own), axis=0
        )
        first = dot_t(pair[:, lanes], key_cache[plane(), :, lanes])
        product = jnp.concatenate([first, dot_t(pair[:, lanes], keys)], axis=1) * factor
        own_scores[h] = jnp.where(near, product, NEG)
    stats = jnp.zeros((2 * own, LANES), F32)
    for h in range(heads):
        lanes = slice(h * HEAD_DIM, (h + 1) * HEAD_DIM)
        weights, found = weigh(own_scores[h])
        out = dot(weights[:, :block], value_cache[plane(), :, lanes])
        values = mine[:, 2 * width + h * HEAD_DIM : 2 * width + (h + 1) * HEAD_DIM]
        out = out + dot(weights[:, block : block + own], values)
        out = out.astype(BF16)
        local[:own, lanes] = out[:own]
        crossing[:own, lanes] = out[own:]
        stats = kept(stats, h, heads, found)
    write_stats(stats[:own], local)
    write_stats(stats[own:], crossing)
    for at, ref in enumerate((mine, *queries)):
        for part in range(2):
            rows = slice((2 * at + part) * own, (2 * at + part + 1) * own)
            copied[rows, :] = ref[:, (part + 1) * width : (part + 2) * width]
    last = 2 * (count + 1) * own
    copied[last:, :] = jnp.zeros((copied.shape[0] - last, width), BF16)


def twin_rows(mine, theirs, held):
    within = lax.rem(lax.axis_index("seq"), 2)
    held[within] = mine
    held[1 - within] = theirs
    return stacked([held[0], held[1]])


def twin_merge_and_project(*refs):
    partials, (wo, total_out, rounded) = refs[:-3], refs[-3:]
    own, width = total_out.shape[0], partials[0].shape[1]
    heads = width // HEAD_DIM
    stats = [dot_t(eye_of(own), ref[own : own + 16, :own]) for ref in partials]
    attention = []
    for h in range(heads):
        lanes = slice(h * HEAD_DIM, (h + 1) * HEAD_DIM)
        peaks = [s[:, h : h + 1] for s in stats]
        highest = functools.reduce(jnp.maximum, peaks)
        total, summed = 0.0, 0.0
        for ref, s, peak in zip(partials, stats, peaks):
            scale = jnp.exp(peak - highest)
            own_total = s[:, heads + h : heads + h + 1] + s[:, 2 * heads + h : 2 * heads + h + 1]
            total = total + own_total * scale
            summed = summed + ref[:own, lanes].astype(F32) * scale
        attention.append((summed / total).astype(BF16))
    product = dot(jnp.concatenate(attention, axis=1), wo[...])
    total_out[...] = product
    rounded[...] = product.astype(BF16)


def twin_add(mine, theirs, total, rounded):
    both = mine[...] + theirs[...].astype(F32)
    total[...] = both
    rounded[...] = both.astype(BF16)


def twin_finish(mine, theirs, gain, hidden, out):
    model_width = mine.shape[1]
    columns = out.shape[1]
    total = mine[...] + theirs[...].astype(F32)
    scale = lax.rsqrt(sum_squares(total) / model_width + EPS)
    lanes = pl.ds(pl.multiple_of(lax.axis_index("tp") * columns, columns), columns)
    normed = (mine[:, lanes] + theirs[:, lanes].astype(F32)) * scale * gain[...]
    out[...] = (hidden[:, lanes].astype(F32) + normed).astype(BF16)


def twin_compact(far, targets, key_cache, value_cache, *refs):
    count = len(far) + 1
    ours, (copied, new_keys, new_values, held) = refs[:count], refs[count:]
    block, width = key_cache.shape[1:]
    own = ours[0].shape[0]
    me = lax.axis_index("seq")
    place = me * block + iota((block, targets.shape[2]), 0)
    for at, turn in enumerate((0, *far)):
        request = plane() ^ turn
        placing = place == targets[request]
        written = jnp.max(placing.astype(F32), axis=1, keepdims=True) > 0.5
        placing = placing.astype(BF16)
        for part, (cache, out) in enumerate(((key_cache, new_keys), (value_cache, new_values))):
            lanes = slice((part + 1) * width, (part + 2) * width)
            rows = slice((2 * at + part) * own, (2 * at + part + 1) * own)
            theirs = copied[rows, :]
            fresh = twin_rows(ours[at][:, lanes], theirs, held.at[at, part])
            moved = dot(placing, fresh)
            out[request] = jnp.where(written, moved, cache[request].astype(F32)).astype(BF16)


def body_twin(
    hidden_in,
    query_weight,
    key_weight,
    value_weight,
    out_weight,
    query_gain,
    key_gain,
    post_gain,
    key_cache,
    value_cache,
    cache_lengths,
    parents,
    accepted_leaf,
):
    requests, block, width = key_cache.shape
    draft = parents.shape[1]
    own, model = hidden_in.shape
    tp = lax.axis_size("tp")
    seq = lax.axis_size("seq")
    columns = model // tp
    heads = width // HEAD_DIM
    far = tuple(range(requests - 1, 0, -1))

    def call(kernel, outs, inputs, scratch=(), mib=16, specs=None, ties=()):
        count = len(inputs)

        def run(*refs):
            kernel(*refs[:count], *refs[count + len(ties) :])

        return pl.pallas_call(
            run,
            out_shape=outs,
            in_specs=([VMEM] * count if specs is None else specs) + [ANY] * len(ties),
            out_specs=jax.tree.map(lambda _: VMEM, outs),
            scratch_shapes=list(scratch),
            compiler_params=params(mib),
            name=getattr(kernel, "func", kernel).__name__,
        )(*inputs, *ties)

    def over_tp(x, k):
        return lax.ppermute(x, "tp", [(i, i ^ k) for i in range(tp)])

    def beside(x):
        return lax.ppermute(x, "seq", [(i, i ^ 1) for i in range(seq)])

    def over_planes(x, turn):
        return lax.ppermute(x, "seq", [(i, (i // 2 ^ turn) * 2 + i % 2) for i in range(seq)])

    me = lax.axis_index("seq") // 2

    def picked(turns):
        return jnp.stack(
            [
                lax.dynamic_index_in_dim(x, me ^ turn, 0, False)
                for turn in turns
                for x in (key_cache, value_cache)
            ]
        )

    swapped = beside(picked(far))
    query_raw, key_raw, squares = call(
        twin_project_qk,
        (shaped((own, width), F32), shaped((own, width), F32), shaped((8, 2 * LANES), F32)),
        (hidden_in, query_weight, key_weight),
    )
    all_squares = [squares] + [over_tp(squares, k) for k in range(tp - 1, 0, -1)]

    exponents = -2.0 * (jnp.arange(HEAD_DIM) % (HEAD_DIM // 2)).astype(F32) / HEAD_DIM
    freqs = (THETA**exponents)[None, :]
    own_tree, targets, cosine, sine, limits = call(
        functools.partial(twin_tree, (0, *far)),
        (
            shaped((draft, own), F32),
            shaped((requests, 1, draft), jnp.int32),
            shaped((own, HEAD_DIM), F32),
            shaped((own, HEAD_DIM), F32),
            shaped((requests, 2 * block), jnp.int32),
        ),
        (cache_lengths[None, :], accepted_leaf[None, :], parents, freqs),
        [pltpu.VMEM((requests, draft, draft), F32)],
    )
    value = call(twin_project_v, shaped((own, width), BF16), (hidden_in, value_weight))
    queries, packed = call(
        functools.partial(twin_prepare, tp * width),
        (shaped((own, width), BF16), shaped((own, 3 * width), BF16)),
        (
            query_raw,
            key_raw,
            value,
            query_gain[None, :],
            key_gain[None, :],
            cosine,
            sine,
            *all_squares,
        ),
    )
    from_far = [over_planes(packed, turn) for turn in far]
    other = beside(queries)

    rows = own + 16
    partials = call(
        functools.partial(twin_attend_far, far),
        (shaped((rows, width), BF16),) * len(far),
        (limits, key_cache, value_cache, swapped, *from_far),
        [pltpu.VMEM((len(far), heads, own, 2 * block), F32)],
    )
    crossing, local, copied = call(
        twin_attend_near,
        (shaped((rows, width), BF16),) * 2 + (shaped((2 * requests * own + own, width), BF16),),
        (limits, key_cache, value_cache, own_tree, packed, other, *from_far),
        [pltpu.VMEM((heads, 2 * own, block + LANES), F32)],
        ties=partials[:1],
    )
    partials = [over_planes(part, turn) for part, turn in zip(partials, far)]
    partials += [beside(crossing)]
    partials = [partials[0], partials[1], partials[3], partials[2], local]
    copied = beside(copied)

    total, rounded = call(
        twin_merge_and_project,
        (shaped((own, model), F32), shaped((own, model), BF16)),
        (*partials, out_weight),
    )
    bit = 1
    while 2 * bit < tp:
        total, rounded = call(
            twin_add,
            (shaped((own, model), F32), shaped((own, model), BF16)),
            (total, over_tp(rounded, bit)),
        )
        bit *= 2
    arrived = over_tp(rounded, bit)
    new_key_cache, new_value_cache = call(
        functools.partial(twin_compact, far),
        (shaped(key_cache.shape, BF16), shaped(value_cache.shape, BF16)),
        (targets, key_cache, value_cache, packed, *from_far, copied),
        [pltpu.VMEM((requests, 2, 2, own, width), BF16)],
    )
    hidden_out = call(
        twin_finish,
        shaped((own, columns), BF16),
        (total, arrived, post_gain[None, :], hidden_in),
    )
    return (hidden_out, new_key_cache, new_value_cache)


def body(*args):
    hidden_in, key_cache, parents = args[0], args[8], args[11]
    tp = lax.axis_size("tp")
    own, draft = hidden_in.shape[0], parents.shape[1]
    requests, _, width = key_cache.shape
    twin = (
        own % 16 == 0
        and draft == 2 * own
        and requests == 4
        and lax.axis_size("seq") == 2 * requests
        and own <= LANES
        and LANES % own == 0
        and own <= width
        and 3 * (width // HEAD_DIM) <= 16
        and tp > 1
        and tp & (tp - 1) == 0
    )
    return (body_twin if twin else body_general)(*args)


def solution(mesh):
    return jax.shard_map(
        body,
        mesh=mesh,
        in_specs=(
            P("seq", None),
            P(None, "tp"),
            P(None, "tp"),
            P(None, "tp"),
            P("tp", None),
            P("tp"),
            P("tp"),
            P("tp"),
            P(None, "seq", "tp"),
            P(None, "seq", "tp"),
            P(),
            P(),
            P(),
        ),
        out_specs=(P("seq", "tp"), P(None, "seq", "tp"), P(None, "seq", "tp")),
        check_vma=False,
    )
```

```python
import functools
import math

import jax
import jax.numpy as jnp
from jax import lax
from jax.experimental import pallas as pl
from jax.experimental.pallas import tpu as pltpu
from jax.sharding import PartitionSpec as P

HEAD_DIM = 128
LANES = 128
EPS = 1e-06
THETA = 500000.0
NEG = -1e30
F32 = jnp.float32
BF16 = jnp.bfloat16
VMEM = pl.BlockSpec(memory_space=pltpu.VMEM)
SMEM = pl.BlockSpec(memory_space=pltpu.SMEM)
ANY = pl.BlockSpec(memory_space=pl.ANY)


def params(mib):
    return pltpu.CompilerParams(vmem_limit_bytes=mib * 1024 * 1024)


def dot(a, b):
    return jnp.dot(a, b, preferred_element_type=F32)


def dot_t(a, b):
    return lax.dot_general(a, b, (((1,), (1,)), ((), ())), preferred_element_type=F32)


def iota(shape, axis):
    return lax.broadcasted_iota(jnp.int32, shape, axis)


def stacked(parts):
    if len(parts) == 1:
        return parts[0]
    if parts[0].shape[0] % 16 == 0:
        return jnp.concatenate(parts, axis=0)
    return jnp.concatenate([part.astype(F32) for part in parts], axis=0).astype(BF16)


def sum_squares(raw):
    return jnp.sum(raw * raw, axis=1, keepdims=True)


def project_qk(hidden, wq, wk, query_raw, key_raw, squares, wq_v, wk_v, sems):
    chunks, depth = wq_v.shape[0], wq_v.shape[1]
    copies = []
    for c in range(chunks):
        for at, (source, target) in enumerate(((wq, wq_v), (wk, wk_v))):
            copy = pltpu.make_async_copy(
                source.at[pl.ds(c * depth, depth)], target.at[c], sems.at[2 * c + at]
            )
            copy.start()
            copies.append(copy)
    q_sum, k_sum = None, None
    for c in range(chunks):
        part = hidden[:, c * depth : (c + 1) * depth]
        copies[2 * c].wait()
        q = dot(part, wq_v[c])
        copies[2 * c + 1].wait()
        k = dot(part, wk_v[c])
        q_sum = q if c == 0 else q_sum + q
        k_sum = k if c == 0 else k_sum + k
    query_raw[...] = q_sum
    key_raw[...] = k_sum
    lane = iota(squares.shape[1:], 1)
    both = jnp.where(lane == 0, sum_squares(q_sum), sum_squares(k_sum))
    for t in range(squares.shape[0]):
        squares[t] = both


def project_v_and_tree(
    lengths, leaves, hidden, parents, freqs, wv, value, own_tree, targets, cosine, sine, wv_v, anc_v, sems
):
    chunks, depth = wv_v.shape[0], wv_v.shape[1]
    copies = []
    for c in range(chunks):
        copy = pltpu.make_async_copy(wv.at[pl.ds(c * depth, depth)], wv_v.at[c], sems.at[c])
        copy.start()
        copies.append(copy)
    requests, draft = parents.shape
    own = hidden.shape[0]
    first = lax.axis_index("seq") * own
    row, col = iota((draft, draft), 0), iota((draft, draft), 1)
    eye = (row == col).astype(BF16)
    trees = [
        jnp.where((parents[pl.ds(r, 1), :] == row) | (row == col), 1.0, 0.0).astype(BF16)
        for r in range(requests)
    ]
    for _ in range(max(1, (draft - 1).bit_length())):
        trees = [jnp.minimum(dot(tree, tree), 1.0).astype(BF16) for tree in trees]
    for r in range(requests):
        upright = lax.dot_general(
            trees[r], eye, (((0,), (0,)), ((), ())), preferred_element_type=F32
        )
        anc_v[pl.ds(r * draft, draft), :] = upright
        level = jnp.sum(trees[r].astype(F32), axis=0, keepdims=True) - 1.0
        on_path = jnp.sum(jnp.where(row == leaves[r], upright, 0.0), axis=0, keepdims=True)
        place = lengths[r] + level.astype(jnp.int32)
        targets[r] = jnp.where(on_path > 0.5, place, -1)
    mine = anc_v[pl.ds(pl.multiple_of(first, own), own), :]
    own_tree[...] = mine
    level = jnp.sum(mine, axis=1, keepdims=True) - 1.0
    position = lengths[first // draft].astype(F32) + level
    angles = position * freqs[...]
    cosine[...] = jnp.cos(angles)
    half = jnp.sin(angles)
    sine[...] = jnp.where(iota(half.shape, 1) < HEAD_DIM // 2, -half, half)
    total = None
    for c in range(chunks):
        copies[c].wait()
        v = dot(hidden[:, c * depth : (c + 1) * depth], wv_v[c])
        total = v if c == 0 else total + v
    value[...] = total.astype(BF16)


def prepare(
    width_all, query_raw, key_raw, value, q_gain, k_gain, cosine, sine, squares, queries, keys_values
):
    width = query_raw.shape[1]
    total = sum(squares[k] for k in range(squares.shape[0]))
    cos, sin = cosine[...], sine[...]
    for at, (raw, gain, out) in enumerate(
        ((query_raw, q_gain, queries), (key_raw, k_gain, keys_values))
    ):
        scale = lax.rsqrt(total[:, at : at + 1] / width_all + EPS)
        for h in range(width // HEAD_DIM):
            lanes = slice(h * HEAD_DIM, (h + 1) * HEAD_DIM)
            x = raw[:, lanes] * scale * gain[:, lanes]
            turned = x * cos + pltpu.roll(x, HEAD_DIM // 2, 1) * sin
            turned = turned.astype(BF16)
            for s in range(out.shape[0]):
                out[s, :, lanes] = turned
    for s in range(keys_values.shape[0]):
        keys_values[s, :, width:] = value[...]


def attend_cache(group, lengths, key_cache, value_cache, queries, partials):
    requests, block, width = key_cache.shape
    own = queries.shape[1]
    heads = width // HEAD_DIM
    me = lax.axis_index("seq")
    factor = 1.0 / math.sqrt(HEAD_DIM)
    rows = group * own
    place = me * block + iota((rows, block), 1)
    lane = iota((rows, LANES), 1)
    for request in range(requests):
        q = stacked([queries[request * group + j] for j in range(group)])
        visible = place < lengths[request]
        stats = jnp.zeros((rows, LANES), F32)
        for h in range(heads):
            lanes = slice(h * HEAD_DIM, (h + 1) * HEAD_DIM)
            scores = dot_t(q[:, lanes], key_cache[request, :, lanes]) * factor
            scores = jnp.where(visible, scores, NEG)
            peak = jnp.max(scores, axis=1, keepdims=True).astype(BF16).astype(F32)
            weights = jnp.exp(jnp.where(visible, scores - peak, NEG))
            total = jnp.sum(weights, axis=1, keepdims=True)
            high = total.astype(BF16).astype(F32)
            out = dot(weights.astype(BF16), value_cache[request, :, lanes]).astype(BF16)
            for j in range(group):
                partials[request * group + j, :, lanes] = out[j * own : (j + 1) * own]
            stats = jnp.where(lane == h, peak, stats)
            stats = jnp.where(lane == heads + h, high, stats)
            stats = jnp.where(lane == 2 * heads + h, total - high, stats)
        stats = stats.astype(BF16)
        for j in range(group):
            partials[request * group + j, :, width:] = stats[j * own : (j + 1) * own]


def attend_draft(group, own_tree, queries, keys_values, out, stats):
    own, width = queries.shape[1:]
    heads = width // HEAD_DIM
    me = lax.axis_index("seq")
    first = me // group * group
    q = queries[me]
    pair = stacked([keys_values[first + j] for j in range(group)])
    factor = 1.0 / math.sqrt(HEAD_DIM)
    allowed = own_tree[...] > 0.5
    lane = iota((own, LANES), 1)
    kept = jnp.zeros((own, LANES), F32)
    for h in range(heads):
        lanes = slice(h * HEAD_DIM, (h + 1) * HEAD_DIM)
        there = slice(width + h * HEAD_DIM, width + (h + 1) * HEAD_DIM)
        scores = dot_t(q[:, lanes], pair[:, lanes]) * factor
        scores = jnp.where(allowed, scores, NEG)
        peak = jnp.max(scores, axis=1, keepdims=True)
        weights = jnp.exp(jnp.where(allowed, scores - peak, NEG))
        out[:, lanes] = dot(weights.astype(BF16), pair[:, there])
        kept = jnp.where(lane == h, peak, kept)
        kept = jnp.where(lane == heads + h, jnp.sum(weights, axis=1, keepdims=True), kept)
    stats[...] = kept


def merge_and_project(draft_out, draft_stats, wo, partials, projected, wo_v, sems):
    count, width, columns = wo_v.shape
    heads = width // HEAD_DIM
    copies = []
    for k in range(count):
        copy = pltpu.make_async_copy(
            wo.at[:, pl.ds(k * columns, columns)], wo_v.at[k], sems.at[k]
        )
        copy.start()
        copies.append(copy)
    parts = range(partials.shape[0])
    stats = [partials[s, :, width:].astype(F32) for s in parts]
    own_stats = draft_stats[...]
    attention = []
    for h in range(heads):
        lanes = slice(h * HEAD_DIM, (h + 1) * HEAD_DIM)
        peaks = [s[:, h : h + 1] for s in stats] + [own_stats[:, h : h + 1]]
        highest = functools.reduce(jnp.maximum, peaks)
        scales = [jnp.exp(peak - highest) for peak in peaks]
        total = own_stats[:, heads + h : heads + h + 1] * scales[-1]
        summed = draft_out[:, lanes] * scales[-1]
        for at in parts:
            s = stats[at]
            own_total = s[:, heads + h : heads + h + 1] + s[:, 2 * heads + h : 2 * heads + h + 1]
            total = total + own_total * scales[at]
            summed = summed + partials[at, :, lanes].astype(F32) * scales[at]
        attention.append((summed / total).astype(BF16))
    attention = jnp.concatenate(attention, axis=1)
    for k in range(count):
        copies[k].wait()
        projected[k] = dot(attention, wo_v[k]).astype(projected.dtype)


def add_up(parts, summed, power):
    total = sum(parts[k].astype(F32) for k in range(parts.shape[0]))
    summed[...] = total
    own_power = jnp.broadcast_to(sum_squares(total), power.shape[1:])
    for k in range(power.shape[0]):
        power[k] = own_power


def finish(model_width, summed, gain, hidden, powers, out):
    columns = summed.shape[1]
    power = sum(powers[k] for k in range(powers.shape[0]))[:, :1]
    start = pl.multiple_of(lax.axis_index("tp") * columns, columns)
    normed = summed[...] * lax.rsqrt(power / model_width + EPS) * gain[...]
    out[...] = (hidden[:, pl.ds(start, columns)].astype(F32) + normed).astype(BF16)


def compact(group, targets, key_cache, value_cache, keys_values, new_keys, new_values):
    requests, block, width = key_cache.shape
    own = keys_values.shape[1]
    me = lax.axis_index("seq")
    place = me * block + iota((block, group * own), 0)
    for request in range(requests):
        kv = stacked([keys_values[request * group + j] for j in range(group)])
        placing = place == targets[request]
        written = jnp.max(placing.astype(F32), axis=1, keepdims=True) > 0.5
        fresh = dot(placing.astype(BF16), kv)
        new_keys[request] = jnp.where(
            written, fresh[:, :width], key_cache[request].astype(F32)
        ).astype(BF16)
        new_values[request] = jnp.where(
            written, fresh[:, width:], value_cache[request].astype(F32)
        ).astype(BF16)


def shaped(shape, dtype):
    return jax.ShapeDtypeStruct(shape, dtype)


def body_general(
    hidden_in,
    query_weight,
    key_weight,
    value_weight,
    out_weight,
    query_gain,
    key_gain,
    post_gain,
    key_cache,
    value_cache,
    cache_lengths,
    parents,
    accepted_leaf,
):
    requests, block, width = key_cache.shape
    draft = parents.shape[1]
    own, model = hidden_in.shape
    tp = lax.axis_size("tp")
    seq = lax.axis_size("seq")
    group = draft // own
    columns = model // tp
    chunks = 4
    depth = model // chunks

    def exchange(x, axis):
        return lax.all_to_all(x, axis, 0, 0, tiled=True)

    query_raw, key_raw, squares = pl.pallas_call(
        project_qk,
        out_shape=(
            shaped((own, width), F32),
            shaped((own, width), F32),
            shaped((tp, own, LANES), F32),
        ),
        in_specs=[VMEM, ANY, ANY],
        out_specs=(VMEM, VMEM, VMEM),
        scratch_shapes=[
            pltpu.VMEM((chunks, depth, width), BF16),
            pltpu.VMEM((chunks, depth, width), BF16),
            pltpu.SemaphoreType.DMA((2 * chunks,)),
        ],
        compiler_params=params(56),
        cost_estimate=pl.CostEstimate(
            flops=4 * own * model * width, bytes_accessed=4 * model * width, transcendentals=0
        ),
        name="project_qk",
    )(hidden_in, query_weight, key_weight)
    squares = exchange(squares, "tp")

    exponents = -2.0 * (jnp.arange(HEAD_DIM) % (HEAD_DIM // 2)).astype(F32) / HEAD_DIM
    freqs = (THETA**exponents)[None, :]
    value, own_tree, targets, cosine, sine = pl.pallas_call(
        project_v_and_tree,
        out_shape=(
            shaped((own, width), BF16),
            shaped((own, draft), F32),
            shaped((requests, 1, draft), jnp.int32),
            shaped((own, HEAD_DIM), F32),
            shaped((own, HEAD_DIM), F32),
        ),
        in_specs=[SMEM, SMEM, VMEM, VMEM, VMEM, ANY],
        out_specs=(VMEM,) * 5,
        scratch_shapes=[
            pltpu.VMEM((chunks, depth, width), BF16),
            pltpu.VMEM((requests * draft, draft), F32),
            pltpu.SemaphoreType.DMA((chunks,)),
        ],
        compiler_params=params(16),
        cost_estimate=pl.CostEstimate(
            flops=2 * own * model * width, bytes_accessed=2 * model * width, transcendentals=0
        ),
        name="project_v_and_tree",
    )(cache_lengths, accepted_leaf, hidden_in, parents, freqs, value_weight)

    queries, keys_values = pl.pallas_call(
        functools.partial(prepare, tp * width),
        out_shape=(shaped((seq, own, width), BF16), shaped((seq, own, 2 * width), BF16)),
        in_specs=[VMEM] * 8,
        out_specs=(VMEM, VMEM),
        compiler_params=params(16),
        name="prepare",
    )(
        query_raw,
        key_raw,
        value,
        query_gain[None, :],
        key_gain[None, :],
        cosine,
        sine,
        squares,
    )
    queries = exchange(queries, "seq")
    keys_values = exchange(keys_values, "seq")

    partials = pl.pallas_call(
        functools.partial(attend_cache, group),
        out_shape=shaped((seq, own, width + LANES), BF16),
        in_specs=[SMEM, VMEM, VMEM, VMEM],
        out_specs=VMEM,
        compiler_params=params(16),
        name="attend_cache",
    )(cache_lengths, key_cache, value_cache, queries)
    partials = exchange(partials, "seq")

    draft_out, draft_stats = pl.pallas_call(
        functools.partial(attend_draft, group),
        out_shape=(shaped((own, width), F32), shaped((own, LANES), F32)),
        in_specs=[VMEM] * 3,
        out_specs=(VMEM, VMEM),
        compiler_params=params(16),
        name="attend_draft",
    )(own_tree, queries, keys_values)

    projected = pl.pallas_call(
        merge_and_project,
        out_shape=shaped((tp, own, columns), BF16),
        in_specs=[VMEM, VMEM, ANY, VMEM],
        out_specs=VMEM,
        scratch_shapes=[
            pltpu.VMEM((tp, width, columns), BF16),
            pltpu.SemaphoreType.DMA((tp,)),
        ],
        compiler_params=params(16),
        name="merge_and_project",
    )(draft_out, draft_stats, out_weight, partials)
    projected = exchange(projected, "tp")

    summed, power = pl.pallas_call(
        add_up,
        out_shape=(shaped((own, columns), F32), shaped((tp, own, LANES), F32)),
        in_specs=[VMEM],
        out_specs=(VMEM, VMEM),
        compiler_params=params(16),
        name="add_up",
    )(projected)
    power = exchange(power, "tp")

    hidden_out = pl.pallas_call(
        functools.partial(finish, model),
        out_shape=shaped((own, columns), BF16),
        in_specs=[VMEM] * 4,
        out_specs=VMEM,
        compiler_params=params(16),
        name="finish",
    )(summed, post_gain[None, :], hidden_in, power)

    new_key_cache, new_value_cache = pl.pallas_call(
        functools.partial(compact, group),
        out_shape=(shaped(key_cache.shape, BF16), shaped(value_cache.shape, BF16)),
        in_specs=[VMEM] * 4,
        out_specs=(VMEM, VMEM),
        compiler_params=params(24),
        name="compact",
    )(targets, key_cache, value_cache, keys_values)
    return (hidden_out, new_key_cache, new_value_cache)


def across(column):
    rows = column.shape[0]
    eye = iota((rows, rows), 0) == iota((rows, rows), 1)
    return jnp.sum(jnp.where(eye, column, 0.0), axis=0, keepdims=True)


def upright(line):
    rows = line.shape[1]
    eye = iota((rows, rows), 0) == iota((rows, rows), 1)
    return jnp.sum(jnp.where(eye, line, 0.0), axis=1, keepdims=True)


def eye_of(size):
    return (iota((size, size), 0) == iota((size, size), 1)).astype(BF16)


def plane():
    return lax.axis_index("seq") // 2


def twin_project_qk(hidden, wq, wk, query_raw, key_raw, squares):
    rows = hidden[...]
    own = rows.shape[0]
    for at, (weight, raw) in enumerate(((wq, query_raw), (wk, key_raw))):
        product = dot(rows, weight[...])
        raw[...] = product
        line = across(sum_squares(product))
        line = jnp.concatenate([line, jnp.zeros((1, LANES - own), F32)], axis=1)
        squares[:, at * LANES : (at + 1) * LANES] = jnp.broadcast_to(
            line, (squares.shape[0], LANES)
        )


def twin_project_v(hidden, wv, value):
    value[...] = dot(hidden[...], wv[...]).astype(BF16)


def twin_tree(
    turns, lengths, leaves, parents, freqs, own_tree, targets, cosine, sine, limits, held
):
    requests, draft = parents.shape
    own = own_tree.shape[1]
    row, col = iota((draft, draft), 0), iota((draft, draft), 1)
    eye = eye_of(draft)

    def length_of(request):
        picked = iota(lengths.shape, 1) == request
        return jnp.sum(jnp.where(picked, lengths[...], 0), axis=1, keepdims=True)

    for at, turn in enumerate(turns):
        limits[at : at + 1, :] = jnp.broadcast_to(
            length_of(plane() ^ turn), (1, limits.shape[1])
        )
    trees = [
        jnp.where((parents[pl.ds(r, 1), :] == row) | (row == col), 1.0, 0.0).astype(BF16)
        for r in range(requests)
    ]
    for _ in range(max(1, (draft - 1).bit_length())):
        trees = [jnp.minimum(dot(tree, tree), 1.0).astype(BF16) for tree in trees]
    for r in range(requests):
        standing = lax.dot_general(
            trees[r], eye, (((0,), (0,)), ((), ())), preferred_element_type=F32
        )
        held[r] = standing
        level = jnp.sum(trees[r].astype(F32), axis=0, keepdims=True) - 1.0
        on_path = jnp.where(row == leaves[:, r : r + 1], standing, 0.0)
        on_path = jnp.sum(on_path, axis=0, keepdims=True)
        place = lengths[:, r : r + 1] + level.astype(jnp.int32)
        targets[r] = jnp.where(on_path > 0.5, place, -1)
    within = lax.rem(lax.axis_index("seq"), 2)
    for at in range(2):
        first = (within ^ at) * own
        rows = held[plane(), pl.ds(pl.multiple_of(first, own), own), :]
        own_tree[at * own : (at + 1) * own, :] = jnp.where(
            within == 0, rows[:, :own], rows[:, own:]
        )
        mine = rows if at == 0 else mine
    level = jnp.sum(mine, axis=1, keepdims=True) - 1.0
    angles = (length_of(plane()).astype(F32) + level) * freqs[...]
    cosine[...] = jnp.cos(angles)
    half = jnp.sin(angles)
    sine[...] = jnp.where(iota(half.shape, 1) < HEAD_DIM // 2, -half, half)


def turned(raw, scale, gain, cos, sin):
    x = raw * scale * gain
    return (x * cos + pltpu.roll(x, HEAD_DIM // 2, 1) * sin).astype(BF16)


def twin_prepare(width_all, query_raw, key_raw, value, q_gain, k_gain, cosine, sine, *refs):
    squares, (queries, packed) = refs[:-2], refs[-2:]
    own, width = query_raw.shape
    cos, sin = cosine[...], sine[...]
    total = sum(ref[:1, :] for ref in squares)
    for at, (raw, gain) in enumerate(((query_raw, q_gain), (key_raw, k_gain))):
        scale = upright(total[:, at * LANES : at * LANES + own])
        scale = lax.rsqrt(scale / width_all + EPS)
        for h in range(width // HEAD_DIM):
            lanes = slice(h * HEAD_DIM, (h + 1) * HEAD_DIM)
            there = slice(at * width + h * HEAD_DIM, at * width + (h + 1) * HEAD_DIM)
            found = turned(raw[:, lanes], scale, gain[:, lanes], cos, sin)
            packed[:, there] = found
            if at == 0:
                queries[:, lanes] = found
    packed[:, 2 * width :] = value[...]


def weigh(s):
    peak = jnp.max(s, axis=1, keepdims=True).astype(BF16).astype(F32)
    weights = jnp.exp(s - jnp.maximum(peak, 0.1 * NEG))
    total = jnp.sum(weights, axis=1, keepdims=True)
    high = total.astype(BF16).astype(F32)
    return weights.astype(BF16), (peak, high, total - high)


def kept(stats, h, heads, found):
    lane = iota(stats.shape, 1)
    for at, column in enumerate(found):
        stats = jnp.where(lane == at * heads + h, column, stats)
    return stats


def write_stats(stats, out):
    own, width = stats.shape[0], out.shape[1]
    flat = lax.dot_general(
        stats.astype(BF16), eye_of(own), (((0,), (0,)), ((), ())), preferred_element_type=F32
    )
    flat = jnp.concatenate([flat[:16], jnp.zeros((16, width - own), F32)], axis=1)
    out[own : own + 16, :] = flat.astype(BF16)


def twin_attend_far(turns, limits, key_cache, value_cache, swapped, *refs):
    count = len(turns)
    queries, outs, scores = refs[:count], refs[count : 2 * count], refs[2 * count]
    block, width = key_cache.shape[1:]
    heads = width // HEAD_DIM
    own = queries[0].shape[0]
    me = lax.axis_index("seq")
    factor = 1.0 / math.sqrt(HEAD_DIM)
    place = iota((1, block), 1)
    both = jnp.concatenate([me * block + place, (me ^ 1) * block + place], axis=1)
    visible = [both < limits[at + 1 : at + 2, :] for at in range(count)]
    for at, turn in enumerate(turns):
        for h in range(heads):
            lanes = slice(h * HEAD_DIM, (h + 1) * HEAD_DIM)
            q = queries[at][:, lanes]
            first = dot_t(q, key_cache[plane() ^ turn, :, lanes])
            second = dot_t(q, swapped[at, 0, :, lanes])
            product = jnp.concatenate([first, second], axis=1) * factor
            scores[at, h] = jnp.where(visible[at], product, NEG)
    for at, turn in enumerate(turns):
        stats = jnp.zeros((own, LANES), F32)
        for h in range(heads):
            lanes = slice(h * HEAD_DIM, (h + 1) * HEAD_DIM)
            weights, found = weigh(scores[at, h])
            out = dot(weights[:, :block], value_cache[plane() ^ turn, :, lanes])
            out = out + dot(weights[:, block:], swapped[at, 1, :, lanes])
            outs[at][:own, lanes] = out.astype(BF16)
            stats = kept(stats, h, heads, found)
        write_stats(stats, outs[at])


def twin_attend_near(limits, key_cache, value_cache, own_tree, mine, other, *refs):
    queries, (crossing, local, copied, own_scores) = refs[:-4], refs[-4:]
    count = len(queries)
    block, width = key_cache.shape[1:]
    heads = width // HEAD_DIM
    own = other.shape[0]
    factor = 1.0 / math.sqrt(HEAD_DIM)
    place = lax.axis_index("seq") * block + iota((1, block), 1)
    here = jnp.broadcast_to(place < limits[:1, :block], (2 * own, block))
    rest = own_scores.shape[2] - block - own
    near = jnp.concatenate(
        [jnp.where(here, 1.0, 0.0), own_tree[...], jnp.zeros((2 * own, rest), F32)], axis=1
    )
    near = near > 0.5
    pair = stacked([mine[:, :width], other[...]])
    for h in range(heads):
        lanes = slice(h * HEAD_DIM, (h + 1) * HEAD_DIM)
        keys = jnp.concatenate(
            [mine[:, width + h * HEAD_DIM : width + (h + 1) * HEAD_DIM]] * (1 + rest // own), axis=0
        )
        first = dot_t(pair[:, lanes], key_cache[plane(), :, lanes])
        product = jnp.concatenate([first, dot_t(pair[:, lanes], keys)], axis=1) * factor
        own_scores[h] = jnp.where(near, product, NEG)
    stats = jnp.zeros((2 * own, LANES), F32)
    for h in range(heads):
        lanes = slice(h * HEAD_DIM, (h + 1) * HEAD_DIM)
        weights, found = weigh(own_scores[h])
        out = dot(weights[:, :block], value_cache[plane(), :, lanes])
        values = mine[:, 2 * width + h * HEAD_DIM : 2 * width + (h + 1) * HEAD_DIM]
        out = out + dot(weights[:, block : block + own], values)
        out = out.astype(BF16)
        local[:own, lanes] = out[:own]
        crossing[:own, lanes] = out[own:]
        stats = kept(stats, h, heads, found)
    write_stats(stats[:own], local)
    write_stats(stats[own:], crossing)
    for at, ref in enumerate((mine, *queries)):
        for part in range(2):
            rows = slice((2 * at + part) * own, (2 * at + part + 1) * own)
            copied[rows, :] = ref[:, (part + 1) * width : (part + 2) * width]
    last = 2 * (count + 1) * own
    copied[last:, :] = jnp.zeros((copied.shape[0] - last, width), BF16)


def twin_rows(mine, theirs, held):
    within = lax.rem(lax.axis_index("seq"), 2)
    held[within] = mine
    held[1 - within] = theirs
    return stacked([held[0], held[1]])


def twin_merge_and_project(*refs):
    partials, (wo, total_out, rounded) = refs[:-3], refs[-3:]
    own, width = total_out.shape[0], partials[0].shape[1]
    heads = width // HEAD_DIM
    stats = [dot_t(eye_of(own), ref[own : own + 16, :own]) for ref in partials]
    attention = []
    for h in range(heads):
        lanes = slice(h * HEAD_DIM, (h + 1) * HEAD_DIM)
        peaks = [s[:, h : h + 1] for s in stats]
        highest = functools.reduce(jnp.maximum, peaks)
        total, summed = 0.0, 0.0
        for ref, s, peak in zip(partials, stats, peaks):
            scale = jnp.exp(peak - highest)
            own_total = s[:, heads + h : heads + h + 1] + s[:, 2 * heads + h : 2 * heads + h + 1]
            total = total + own_total * scale
            summed = summed + ref[:own, lanes].astype(F32) * scale
        attention.append((summed / total).astype(BF16))
    product = dot(jnp.concatenate(attention, axis=1), wo[...])
    total_out[...] = product
    rounded[...] = product.astype(BF16)


def twin_add(mine, theirs, total, rounded):
    both = mine[...] + theirs[...].astype(F32)
    total[...] = both
    rounded[...] = both.astype(BF16)


def twin_finish(mine, theirs, gain, hidden, out):
    model_width = mine.shape[1]
    columns = out.shape[1]
    total = mine[...] + theirs[...].astype(F32)
    scale = lax.rsqrt(sum_squares(total) / model_width + EPS)
    lanes = pl.ds(pl.multiple_of(lax.axis_index("tp") * columns, columns), columns)
    normed = (mine[:, lanes] + theirs[:, lanes].astype(F32)) * scale * gain[...]
    out[...] = (hidden[:, lanes].astype(F32) + normed).astype(BF16)


def twin_compact(far, targets, key_cache, value_cache, *refs):
    count = len(far) + 1
    ours, (copied, new_keys, new_values, held) = refs[:count], refs[count:]
    block, width = key_cache.shape[1:]
    own = ours[0].shape[0]
    me = lax.axis_index("seq")
    place = me * block + iota((block, targets.shape[2]), 0)
    for at, turn in enumerate((0, *far)):
        request = plane() ^ turn
        placing = place == targets[request]
        written = jnp.max(placing.astype(F32), axis=1, keepdims=True) > 0.5
        placing = placing.astype(BF16)
        for part, (cache, out) in enumerate(((key_cache, new_keys), (value_cache, new_values))):
            lanes = slice((part + 1) * width, (part + 2) * width)
            rows = slice((2 * at + part) * own, (2 * at + part + 1) * own)
            theirs = copied[rows, :]
            fresh = twin_rows(ours[at][:, lanes], theirs, held.at[at, part])
            moved = dot(placing, fresh)
            out[request] = jnp.where(written, moved, cache[request].astype(F32)).astype(BF16)


def body_twin(
    hidden_in,
    query_weight,
    key_weight,
    value_weight,
    out_weight,
    query_gain,
    key_gain,
    post_gain,
    key_cache,
    value_cache,
    cache_lengths,
    parents,
    accepted_leaf,
):
    requests, block, width = key_cache.shape
    draft = parents.shape[1]
    own, model = hidden_in.shape
    tp = lax.axis_size("tp")
    seq = lax.axis_size("seq")
    columns = model // tp
    heads = width // HEAD_DIM
    far = tuple(range(requests - 1, 0, -1))

    def call(kernel, outs, inputs, scratch=(), mib=16, specs=None, ties=()):
        count = len(inputs)

        def run(*refs):
            kernel(*refs[:count], *refs[count + len(ties) :])

        return pl.pallas_call(
            run,
            out_shape=outs,
            in_specs=([VMEM] * count if specs is None else specs) + [ANY] * len(ties),
            out_specs=jax.tree.map(lambda _: VMEM, outs),
            scratch_shapes=list(scratch),
            compiler_params=params(mib),
            name=getattr(kernel, "func", kernel).__name__,
        )(*inputs, *ties)

    def over_tp(x, k):
        return lax.ppermute(x, "tp", [(i, i ^ k) for i in range(tp)])

    def beside(x):
        return lax.ppermute(x, "seq", [(i, i ^ 1) for i in range(seq)])

    def over_planes(x, turn):
        return lax.ppermute(x, "seq", [(i, (i // 2 ^ turn) * 2 + i % 2) for i in range(seq)])

    me = lax.axis_index("seq") // 2

    def picked(turns):
        parts = [
            [lax.dynamic_index_in_dim(x, me ^ turn, 0, False) for x in (key_cache, value_cache)]
            for turn in turns
        ]
        return jnp.stack([jnp.stack(part) for part in parts])

    swapped = beside(picked(far))
    query_raw, key_raw, squares = call(
        twin_project_qk,
        (shaped((own, width), F32), shaped((own, width), F32), shaped((8, 2 * LANES), F32)),
        (hidden_in, query_weight, key_weight),
    )
    all_squares = [squares] + [over_tp(squares, k) for k in range(tp - 1, 0, -1)]

    exponents = -2.0 * (jnp.arange(HEAD_DIM) % (HEAD_DIM // 2)).astype(F32) / HEAD_DIM
    freqs = (THETA**exponents)[None, :]
    own_tree, targets, cosine, sine, limits = call(
        functools.partial(twin_tree, (0, *far)),
        (
            shaped((draft, own), F32),
            shaped((requests, 1, draft), jnp.int32),
            shaped((own, HEAD_DIM), F32),
            shaped((own, HEAD_DIM), F32),
            shaped((requests, 2 * block), jnp.int32),
        ),
        (cache_lengths[None, :], accepted_leaf[None, :], parents, freqs),
        [pltpu.VMEM((requests, draft, draft), F32)],
    )
    value = call(twin_project_v, shaped((own, width), BF16), (hidden_in, value_weight))
    queries, packed = call(
        functools.partial(twin_prepare, tp * width),
        (shaped((own, width), BF16), shaped((own, 3 * width), BF16)),
        (
            query_raw,
            key_raw,
            value,
            query_gain[None, :],
            key_gain[None, :],
            cosine,
            sine,
            *all_squares,
        ),
    )
    from_far = [over_planes(packed, turn) for turn in far]
    other = beside(queries)

    rows = own + 16
    partials = call(
        functools.partial(twin_attend_far, far),
        (shaped((rows, width), BF16),) * len(far),
        (limits, key_cache, value_cache, swapped, *from_far),
        [pltpu.VMEM((len(far), heads, own, 2 * block), F32)],
    )
    crossing, local, copied = call(
        twin_attend_near,
        (shaped((rows, width), BF16),) * 2 + (shaped((2 * requests * own + own, width), BF16),),
        (limits, key_cache, value_cache, own_tree, packed, other, *from_far),
        [pltpu.VMEM((heads, 2 * own, block + LANES), F32)],
        ties=partials[:1],
    )
    partials = [over_planes(part, turn) for part, turn in zip(partials, far)]
    partials += [beside(crossing)]
    partials = [partials[0], partials[1], partials[3], partials[2], local]
    copied = beside(copied)

    total, rounded = call(
        twin_merge_and_project,
        (shaped((own, model), F32), shaped((own, model), BF16)),
        (*partials, out_weight),
    )
    bit = 1
    while 2 * bit < tp:
        total, rounded = call(
            twin_add,
            (shaped((own, model), F32), shaped((own, model), BF16)),
            (total, over_tp(rounded, bit)),
        )
        bit *= 2
    arrived = over_tp(rounded, bit)
    new_key_cache, new_value_cache = call(
        functools.partial(twin_compact, far),
        (shaped(key_cache.shape, BF16), shaped(value_cache.shape, BF16)),
        (targets, key_cache, value_cache, packed, *from_far, copied),
        [pltpu.VMEM((requests, 2, 2, own, width), BF16)],
    )
    hidden_out = call(
        twin_finish,
        shaped((own, columns), BF16),
        (total, arrived, post_gain[None, :], hidden_in),
    )
    return (hidden_out, new_key_cache, new_value_cache)


def body(*args):
    hidden_in, key_cache, parents = args[0], args[8], args[11]
    tp = lax.axis_size("tp")
    own, draft = hidden_in.shape[0], parents.shape[1]
    requests, _, width = key_cache.shape
    twin = (
        own % 16 == 0
        and draft == 2 * own
        and requests == 4
        and lax.axis_size("seq") == 2 * requests
        and own <= LANES
        and LANES % own == 0
        and own <= width
        and 3 * (width // HEAD_DIM) <= 16
        and tp > 1
        and tp & (tp - 1) == 0
    )
    return (body_twin if twin else body_general)(*args)


def solution(mesh):
    return jax.shard_map(
        body,
        mesh=mesh,
        in_specs=(
            P("seq", None),
            P(None, "tp"),
            P(None, "tp"),
            P(None, "tp"),
            P("tp", None),
            P("tp"),
            P("tp"),
            P("tp"),
            P(None, "seq", "tp"),
            P(None, "seq", "tp"),
            P(),
            P(),
            P(),
        ),
        out_specs=(P("seq", "tp"), P(None, "seq", "tp"), P(None, "seq", "tp")),
        check_vma=False,
    )
```
